32 devices in a mesh: dp: 16 (over z, y, x), stream: 2 (over core).
Axes of the slice: x: 2, y: 2, z: 4, core: 2. Of those that a mesh axis runs over, the one named last changes fastest.
Arguments:
- tokens: bfloat16 [32768, 1024], P('dp'), may hold values from -6 to 6
- norm_gain: float32 [1024], replicated, may hold values from 0.1 to 1.9
- w_qkv: bfloat16 [1024, 3072], replicated, may hold values from -0.1875 to 0.1875
- w_proj: bfloat16 [1024, 1024], replicated, may hold values from -4 to 4
- w_in: bfloat16 [1024, 4096], replicated, may hold values from -0.1875 to 0.1875
- w_out: bfloat16 [4096, 1024], replicated, may hold values from -0.09375 to 0.09375
- feature_weight: float32 [1024], replicated, may hold values from 0.25 to 4
- lengths: int32 [16], P('dp'), may hold values from 128 to 2048, as said below
- cotangent: bfloat16 [32768, 1024], P('dp'), may hold values from -6 to 6
Outputs:
- output: bfloat16 [32768, 1024], P('dp')
- input_grad: bfloat16 [32768, 1024], P('dp')
- gain_grad: float32 [1024], P(('dp', 'stream'))
- qkv_grad: float32 [1024, 3072], P(('dp', 'stream'))
- proj_grad: float32 [1024, 1024], P(('dp', 'stream'))
- in_grad: float32 [1024, 4096], P(('dp', 'stream'))
- out_grad: float32 [4096, 1024], P(('dp', 'stream'))
- feature_grad: float32 [1024], P(('dp', 'stream'))
The draws below stay inside these ranges and needn't reach their ends.
Inputs may be any that keep to these rules, and one draw needn't show every extreme that they name: `lengths`: lengths have many short values; some slot holds 2048 and some holds 128.
All inputs are finite; a program needn't handle non-finite values.
Results may differ from the reference program's by a relative error of at most 0.015.
Values sent between devices are 32-bit elements; how exact they have to be, the bound alone decides.
A program may use at most 320 MiB of HBM per device.

```python
import math
import jax
import jax.numpy as jnp
from jax import lax

D = 1024
HEADS = 16
HEAD = 64
FF = 4096
ROT = 16
SPAN = 64
SLOT = 2048
MIN_LEN = 128
SLOTS = 16
TOKENS = 32768


def draw_lengths(key, part):
    key = jax.random.fold_in(key, 7)
    random_key, order_key = jax.random.split(key)
    raw_values = jax.random.randint(random_key, (SLOTS,), 0, 1024)
    curved = (raw_values + raw_values * raw_values // 1024) // 2
    lengths = MIN_LEN + (SLOT - MIN_LEN) * curved // 1023
    order_perm = jax.random.permutation(order_key, SLOTS)
    lengths = lengths.at[order_perm[0]].set(SLOT).at[order_perm[1]].set(MIN_LEN)
    return lengths.astype(jnp.int32)


def levels(own_key, extent, cuts, low, top_value):
    loudness = 1.0
    for dim, parts in cuts:
        heights = jax.random.uniform(jax.random.fold_in(jax.random.fold_in(own_key, 6), dim), (parts,), jnp.float32, low / len(cuts), top_value / len(cuts))
        loudness = loudness * jnp.repeat(jnp.exp(heights), extent[dim] // parts).reshape((-1,) + (1,) * (len(extent) - 1 - dim))
    return loudness


def normal_values(stream_key, extent, scale, most, cuts=(), kind=jnp.bfloat16):
    factor_of = levels(stream_key, extent, cuts, -0.22, 0.18) if cuts else 1.0
    array = jax.random.normal(stream_key, extent, jnp.float32) * scale * factor_of
    return jnp.minimum(jnp.maximum(array, -most), most).astype(kind)


def setup_inputs(seed: int = 0) -> dict:
    splits = jax.random.split(jax.random.key(seed), 10)
    tokens = normal_values(splits[0], (TOKENS, D), 1.0, 6.0, ((0, 16),))
    norm_gain = jnp.clip(1.0 + 0.18 * jax.random.normal(splits[1], (D,), jnp.float32), 0.1, 1.9)
    w_qkv = normal_values(splits[2], (D, 3 * D), D ** -0.5, 0.1875)
    w_proj = normal_values(splits[3], (D, D), (max(D * 4 // SLOT, 1)) ** -0.5, 4.0)
    w_in = normal_values(splits[4], (D, FF), D ** -0.5, 0.1875)
    w_out = normal_values(splits[5], (FF, D), FF ** -0.5, 0.09375)
    feature_weight = jnp.clip(jnp.exp(jax.random.uniform(splits[6], (D,), jnp.float32, math.log(0.25), math.log(4.0))), 0.25, 4.0)
    lengths = draw_lengths(jax.random.fold_in(splits[9], 71), 0)
    cotangent = normal_values(splits[8], (TOKENS, D), 1.0, 6.0, ((0, 16),))
    return {"tokens": tokens, "norm_gain": norm_gain, "w_qkv": w_qkv, "w_proj": w_proj, "w_in": w_in, "w_out": w_out, "feature_weight": feature_weight, "lengths": lengths, "cotangent": cotangent}


@jax.custom_vjp
def low(v):
    return lax.optimization_barrier(v.astype(jnp.bfloat16)).astype(jnp.float32)

@jax.custom_vjp
def low_back(v):
    return v

def low_keep(v):
    return (low(v), None)

def low_pass(kept, grad):
    return (grad,)

def back_keep(v):
    return (v, None)

def back_low(kept, grad):
    return (low(grad),)
low.defvjp(low_keep, low_pass)
low_back.defvjp(back_keep, back_low)
EPSILON = 1e-05
HIGHEST = lax.Precision.HIGHEST

def feature_table():
    indices = jnp.arange(HEAD).astype(jnp.float32)
    cos_table = jnp.cos(jnp.pi * (2.0 * indices[:, None] + 1.0) * indices[None, :] / (2.0 * HEAD))
    weights = jnp.where(indices == 0, jnp.sqrt(1.0 / HEAD), jnp.sqrt(2.0 / HEAD))
    quantiles = jnp.sqrt(2.0) * lax.erf_inv(2.0 * (indices + 0.5) / HEAD - 1.0)
    return cos_table * (weights * 0.5 * quantiles)[None, :]

def rotary_tables():
    half_rot = ROT // 2
    positions = jnp.arange(SLOT).astype(jnp.float32)
    inverse = 10000.0 ** (-2.0 * jnp.arange(half_rot).astype(jnp.float32) / ROT)
    angles = positions[:, None] * inverse[None, :]
    return (jnp.cos(angles)[None, :, None, :], jnp.sin(angles)[None, :, None, :])

def rotate(heads_in, cosine, sine_table):
    half_rot = ROT // 2
    upper_half = heads_in[..., :half_rot]
    lower_half = heads_in[..., half_rot:ROT]
    return jnp.concatenate([upper_half * cosine - lower_half * sine_table, lower_half * cosine + upper_half * sine_table, heads_in[..., ROT:]], axis=-1)

def exclusive(blocks_in):
    running = jnp.cumsum(blocks_in, axis=2)
    return jnp.concatenate([jnp.zeros_like(running[:, :, :1]), running[:, :, :-1]], axis=2)

def to_blocks(blocks_in):
    slot_count = blocks_in.shape[0]
    return blocks_in.reshape(slot_count, SLOT // SPAN, SPAN, HEADS, HEAD).transpose(0, 3, 1, 2, 4)

def layer_forward(inputs, gain, w_qkv, w_proj, w_in, w_out, feature_weight, valid_rows):
    slot_count = inputs.shape[0]
    average = lax.optimization_barrier(jnp.mean(inputs, axis=-1, keepdims=True))
    centered = inputs - average
    variance = lax.optimization_barrier(jnp.mean(centered * centered, axis=-1, keepdims=True))
    normed = low(centered * lax.rsqrt(variance + EPSILON) * gain)
    projected = low_back(jnp.einsum('bsd,de->bse', normed, w_qkv, precision=HIGHEST))
    heads_view = projected.reshape(slot_count, SLOT, 3, HEADS, HEAD)
    cosine, sine_table = rotary_tables()
    feature_map = feature_table()
    scales = feature_weight.reshape(HEADS, HEAD)
    queries = rotate(heads_view[:, :, 0], cosine, sine_table)
    keys_rot = rotate(heads_view[:, :, 1], cosine, sine_table)
    values = low(heads_view[:, :, 2])
    q_feature = low(scales * jnp.exp(jnp.einsum('bshi,im->bshm', queries, feature_map, precision=HIGHEST)))
    k_feature = low(scales * jnp.exp(jnp.einsum('bshi,im->bshm', keys_rot, feature_map, precision=HIGHEST)) * valid_rows[:, :, None, None])
    q_blocks = to_blocks(q_feature)
    k_blocks = to_blocks(k_feature)
    v_blocks = to_blocks(values)
    causal = (jnp.arange(SPAN)[:, None] >= jnp.arange(SPAN)[None, :]).astype(jnp.float32)
    scores = low(low_back(jnp.einsum('bhnqm,bhnkm->bhnqk', q_blocks, k_blocks, precision=HIGHEST) * causal))
    kv_block = low_back(jnp.einsum('bhnkm,bhnkd->bhnmd', k_blocks, v_blocks, precision=HIGHEST))
    prefix_state = low(low_back(exclusive(kv_block)))
    key_state = low(low_back(exclusive(lax.optimization_barrier(jnp.sum(k_blocks, axis=3)))))
    numerator = low_back(jnp.einsum('bhnqk,bhnkd->bhnqd', scores, v_blocks, precision=HIGHEST) + jnp.einsum('bhnqm,bhnmd->bhnqd', q_blocks, prefix_state, precision=HIGHEST))
    denominator = low_back(lax.optimization_barrier(jnp.sum(scores, axis=-1)) + jnp.einsum('bhnqm,bhnm->bhnq', q_blocks, key_state, precision=HIGHEST))
    mixed_heads = low((numerator / denominator[..., None]).transpose(0, 2, 3, 1, 4).reshape(slot_count, SLOT, HEADS * HEAD))
    attention = jnp.einsum('bsd,de->bse', mixed_heads, w_proj, precision=HIGHEST)
    hidden = low_back(jnp.einsum('bsd,df->bsf', normed, w_in, precision=HIGHEST))
    active = low(jax.nn.gelu(hidden, approximate=False))
    feed = jnp.einsum('bsf,fd->bsd', active, w_out, precision=HIGHEST)
    return inputs + valid_rows[:, :, None] * (attention + feed)

def reference(tokens, norm_gain, w_qkv, w_proj, w_in, w_out, feature_weight, lengths, cotangent):
    group_count = SLOTS // 2
    positions = jnp.arange(SLOT).astype(jnp.int32)
    valid_all = (positions[None, :] < lengths.astype(jnp.int32)[:, None]).astype(jnp.float32).reshape(group_count, 2, SLOT)
    inputs_all = tokens.astype(jnp.float32).reshape(group_count, 2, SLOT, D)
    cot_all = cotangent.astype(jnp.float32).reshape(group_count, 2, SLOT, D)
    weights = (norm_gain.astype(jnp.float32), w_qkv.astype(jnp.float32), w_proj.astype(jnp.float32), w_in.astype(jnp.float32), w_out.astype(jnp.float32), feature_weight.astype(jnp.float32))

    def slot_step(totals, packed):
        inputs, cot_pair, valid_pair = packed

        def wrapped(inputs_in, gain, qkv_weight, proj_weight, in_weight, out_weight, feat_weight):
            return layer_forward(inputs_in, gain, qkv_weight, proj_weight, in_weight, out_weight, feat_weight, valid_pair)
        result, pullback = jax.vjp(wrapped, inputs, *weights)
        gradients = pullback(cot_pair)
        totals = tuple((summed + addend for summed, addend in zip(totals, gradients[1:])))
        return (totals, (result.astype(jnp.bfloat16), gradients[0].astype(jnp.bfloat16)))
    initial = tuple((jnp.zeros_like(member) for member in weights))
    totals, (results, input_grads) = lax.scan(slot_step, initial, (inputs_all, cot_all, valid_all))
    output = results.reshape(TOKENS, D)
    input_grad = input_grads.reshape(TOKENS, D)
    return (output, input_grad, totals[0], totals[1], totals[2], totals[3], totals[4], totals[5])
```

```python
import math
from functools import partial

import jax
import jax.numpy as jnp
import numpy as np
from jax import lax
from jax.experimental import pallas as pl
from jax.experimental.pallas import tpu as pltpu
from jax.sharding import PartitionSpec as P

D = 1024
HEADS = 16
HEAD = 64
FF = 4096
ROT = 16
SLOT = 2048
EPSILON = 1e-05

f32 = jnp.float32
bf16 = jnp.bfloat16
VMEM_LIMIT = 56 * 1024 * 1024
BLK = 256
PAIR = 2 * HEAD


def dot(a, b):
    return lax.dot_general(a, b, (((1,), (0,)), ((), ())), preferred_element_type=f32)


def dot_nt(a, b):
    return lax.dot_general(a, b, (((1,), (1,)), ((), ())), preferred_element_type=f32)


def dot_tn(a, b):
    return lax.dot_general(a, b, (((0,), (0,)), ((), ())), preferred_element_type=f32)


def erf_inverse(y):
    x = 0.0
    for _ in range(200):
        step = (math.erf(x) - y) / (2.0 / math.sqrt(math.pi) * math.exp(-x * x))
        x -= max(-0.5, min(0.5, step))
    return x


def feature_table():
    i = np.arange(HEAD, dtype=np.float64)
    cos_table = np.cos(np.pi * (2.0 * i[:, None] + 1.0) * i[None, :] / (2.0 * HEAD))
    weights = np.where(i == 0, math.sqrt(1.0 / HEAD), math.sqrt(2.0 / HEAD))
    quantiles = math.sqrt(2.0) * np.array([erf_inverse(2.0 * (m + 0.5) / HEAD - 1.0) for m in range(HEAD)])
    return cos_table * (weights * 0.5 * quantiles)[None, :]


def split_table(table):
    high = table.astype(np.float32).astype(bf16)
    low = (table - high.astype(np.float64)).astype(np.float32).astype(bf16)
    return high, low


def attention_tables():
    half = ROT // 2
    pos = np.arange(SLOT, dtype=np.float32)
    inverse = (np.float32(10000.0) ** (-2.0 * np.arange(half, dtype=np.float32) / np.float32(ROT))).astype(np.float32)
    angles = (pos[:, None] * inverse[None, :]).astype(np.float32).astype(np.float64)
    cos_one = np.ones((SLOT, HEAD))
    sin_one = np.zeros((SLOT, HEAD))
    cos_one[:, :half] = np.cos(angles)
    cos_one[:, half:ROT] = np.cos(angles)
    sin_one[:, :half] = np.sin(angles)
    sin_one[:, half:ROT] = -np.sin(angles)
    cosine = np.concatenate([cos_one, cos_one], 1).astype(np.float32)
    sine = np.concatenate([sin_one, sin_one], 1).astype(np.float32)
    one = feature_table()
    pair = np.zeros((PAIR, PAIR))
    pair[:HEAD, :HEAD] = one
    pair[HEAD:, HEAD:] = one
    swapped = pair.copy()
    for base in (0, HEAD):
        swapped[base : base + half] = pair[base + half : base + ROT]
        swapped[base + half : base + ROT] = pair[base : base + half]
    both = np.concatenate([pair, swapped], 0)
    high, low = split_table(both)
    forward = np.concatenate([high, low], 1)
    back_high, back_low = split_table(np.concatenate([pair.T, swapped.T], 1))
    back_high2 = np.concatenate([back_high, back_high], 0)
    return cosine, sine, forward, back_high2, back_low


def params(**extra):
    return pltpu.CompilerParams(vmem_limit_bytes=VMEM_LIMIT, **extra)


def prep_kernel(len_ref, tok_ref, cot_ref, gain_ref, normed_ref, normed_t_ref, g_ref):
    tile = tok_ref.shape[0]
    x = tok_ref[...].astype(f32)
    centered = x - jnp.mean(x, axis=-1, keepdims=True)
    var = jnp.mean(centered * centered, axis=-1, keepdims=True)
    normed = centered * lax.rsqrt(var + EPSILON) * gain_ref[...]
    low = normed.astype(bf16)
    normed_ref[...] = low
    normed_t_ref[...] = low.T
    rows = pl.program_id(0) * tile + lax.broadcasted_iota(jnp.int32, (tile, 1), 0)
    valid = jnp.where(rows < len_ref[0], 1.0, 0.0)
    g_ref[...] = (cot_ref[...].astype(f32) * valid).astype(bf16)


def prep(lengths, tokens, cotangent, gain):
    rows = tokens.shape[0]
    tile = 256
    return pl.pallas_call(
        prep_kernel,
        grid_spec=pltpu.PrefetchScalarGridSpec(
            num_scalar_prefetch=1,
            grid=(rows // tile,),
            in_specs=[
                pl.BlockSpec((tile, D), lambda i, n: (i, 0)),
                pl.BlockSpec((tile, D), lambda i, n: (i, 0)),
                pl.BlockSpec((1, D), lambda i, n: (0, 0)),
            ],
            out_specs=[
                pl.BlockSpec((tile, D), lambda i, n: (i, 0)),
                pl.BlockSpec((D, tile), lambda i, n: (0, i)),
                pl.BlockSpec((tile, D), lambda i, n: (i, 0)),
            ],
        ),
        out_shape=[
            jax.ShapeDtypeStruct((rows, D), bf16),
            jax.ShapeDtypeStruct((D, rows), bf16),
            jax.ShapeDtypeStruct((rows, D), bf16),
        ],
        compiler_params=params(),
        name="prep",
    )(lengths, tokens, cotangent, gain)


def gather_kernel(core_ref, a_ref, b_ref, a_out, b_out):
    a_out[...] = a_ref[...]
    b_out[...] = b_ref[...]


def gather_units(core, w_in, w_out, parts, streams):
    unit = FF // (parts * streams)
    if unit % 128:
        a = lax.dynamic_index_in_dim(w_in.reshape(D, parts, streams, unit), core[0], 2, False)
        b = lax.dynamic_index_in_dim(w_out.reshape(parts, streams, unit, D), core[0], 1, False)
        return a.reshape(D, parts * unit), b.reshape(parts * unit, D)
    return pl.pallas_call(
        gather_kernel,
        grid_spec=pltpu.PrefetchScalarGridSpec(
            num_scalar_prefetch=1,
            grid=(parts,),
            in_specs=[
                pl.BlockSpec((D, unit), lambda i, c: (0, streams * i + c[0])),
                pl.BlockSpec((unit, D), lambda i, c: (streams * i + c[0], 0)),
            ],
            out_specs=[
                pl.BlockSpec((D, unit), lambda i, c: (0, i)),
                pl.BlockSpec((unit, D), lambda i, c: (i, 0)),
            ],
        ),
        out_shape=[
            jax.ShapeDtypeStruct((D, parts * unit), bf16),
            jax.ShapeDtypeStruct((parts * unit, D), bf16),
        ],
        compiler_params=params(),
        name="gather_units",
    )(core, w_in, w_out)


def store_pieces(table_ref, acc, send_ref, keep_ref, columns=None):
    half, rows, _ = keep_ref.shape
    for p in range(2 * half):
        start = pl.multiple_of(table_ref[p] * rows, rows)
        value = acc[pl.ds(start, rows), :]
        if p < half:
            keep_ref[p] = value
        else:
            send_ref[p - half] = value


def piece_specs(parts, rows, columns):
    half = parts // 2
    spec = pl.BlockSpec((half, rows, columns), lambda *_: (0, 0, 0))
    shape = jax.ShapeDtypeStruct((half, rows, columns), f32)
    return [spec, spec], [shape, shape]


def gelu_parts(x):
    density = jnp.exp(x * x * -0.5)
    t = 1.0 / (1.0 + (0.3275911 / math.sqrt(2.0)) * jnp.abs(x))
    poly = 1.061405429 * t - 1.453152027
    poly = poly * t + 1.421413741
    poly = poly * t - 0.284496736
    poly = (poly * t + 0.254829592) * t
    tail = 0.5 * poly * density
    cdf = jnp.where(x >= 0, 1.0 - tail, tail)
    return x * cdf, cdf + x * density * (1.0 / math.sqrt(2.0 * math.pi))


def ff_kernel(row_steps, table_ref, normed_ref, g_ref, nt_ref, win_ref, wout_ref, *rest):
    act_ref, dh_ref, send_ref, keep_ref, dh_all, acc = rest[-6:]
    step = pl.program_id(0)
    tile = normed_ref.shape[0]

    @pl.when(step < row_steps)
    def _():
        hidden = dot(normed_ref[...], win_ref[...])
        d_active = dot_nt(g_ref[...], wout_ref[...])
        value, slope = gelu_parts(hidden)
        act_ref[...] = value.astype(bf16)
        d_hidden = (d_active * slope).astype(bf16)
        dh_ref[...] = d_hidden
        dh_all[pl.ds(pl.multiple_of(step * tile, tile), tile), :] = d_hidden

    @pl.when(step >= row_steps)
    def _():
        rows = nt_ref.shape[0]
        start = pl.multiple_of((step - row_steps) * rows, rows)
        acc[pl.ds(start, rows), :] = dot(nt_ref[...], dh_all[...])

    @pl.when(step == pl.num_programs(0) - 1)
    def _():
        store_pieces(table_ref, acc, send_ref, keep_ref)


def ff_chunk(table, normed, g, normed_t, w_in, w_out, start, units, earlier, parts):
    rows = normed.shape[0]
    total = w_in.shape[1]
    tile, mtile = 512, 256
    row_steps, m_steps = rows // tile, D // mtile
    block = start // units
    last = row_steps - 1
    piece, piece_shape = piece_specs(parts, D // parts, units)
    earlier_specs = [pl.BlockSpec(memory_space=pl.ANY)] * len(earlier)
    return pl.pallas_call(
        partial(ff_kernel, row_steps),
        grid_spec=pltpu.PrefetchScalarGridSpec(
            num_scalar_prefetch=1,
            grid=(row_steps + m_steps,),
            in_specs=[
                pl.BlockSpec((tile, D), lambda i, t: (jnp.minimum(i, last), 0)),
                pl.BlockSpec((tile, D), lambda i, t: (jnp.minimum(i, last), 0)),
                pl.BlockSpec((mtile, rows), lambda i, t: (jnp.maximum(i - row_steps, 0), 0)),
                pl.BlockSpec((D, units), lambda i, t: (0, block)),
                pl.BlockSpec((units, D), lambda i, t: (block, 0)),
            ]
            + earlier_specs,
            out_specs=[
                pl.BlockSpec((tile, units), lambda i, t: (jnp.minimum(i, last), block)),
                pl.BlockSpec((tile, units), lambda i, t: (jnp.minimum(i, last), block)),
            ]
            + piece,
            scratch_shapes=[pltpu.VMEM((rows, units), bf16), pltpu.VMEM((D, units), f32)],
        ),
        out_shape=[
            jax.ShapeDtypeStruct((rows, total), bf16),
            jax.ShapeDtypeStruct((rows, total), bf16),
        ]
        + piece_shape,
        input_output_aliases={6: 0, 7: 1} if earlier else {},
        compiler_params=params(),
        cost_estimate=pl.CostEstimate(
            flops=6 * rows * D * units,
            bytes_accessed=2 * (3 * rows * D + 2 * units * D + 2 * rows * units) + 4 * D * units,
            transcendentals=rows * units,
        ),
        name=f"ff_chunk_{start}",
    )(table, normed, g, normed_t, w_in, w_out, *earlier)


def left_grad_kernel(table_ref, left_ref, right_ref, send_ref, keep_ref, acc):
    step = pl.program_id(0)
    width = left_ref.shape[1]
    start = pl.multiple_of(step * width, width)
    acc[pl.ds(start, width), :] = dot_tn(left_ref[...], right_ref[...])

    @pl.when(step == pl.num_programs(0) - 1)
    def _():
        store_pieces(table_ref, acc, send_ref, keep_ref)


def left_grad(table, left, right, column_block, columns, parts, name):
    rows, total = left.shape
    width = 256
    piece, piece_shape = piece_specs(parts, total // parts, columns)
    return pl.pallas_call(
        left_grad_kernel,
        grid_spec=pltpu.PrefetchScalarGridSpec(
            num_scalar_prefetch=1,
            grid=(total // width,),
            in_specs=[
                pl.BlockSpec((rows, width), lambda i, t: (0, i)),
                pl.BlockSpec((rows, columns), lambda i, t: (0, column_block(t))),
            ],
            out_specs=piece,
            scratch_shapes=[pltpu.VMEM((total, columns), f32)],
        ),
        out_shape=piece_shape,
        compiler_params=params(),
        cost_estimate=pl.CostEstimate(
            flops=2 * rows * total * columns,
            bytes_accessed=2 * rows * (total + columns) + 4 * total * columns,
            transcendentals=0,
        ),
        name=name,
    )(table, left, right)


def proj_grad_kernel(half, table_ref, core_ref, mine_ref, other_ref, right_ref, send_ref, keep_ref, acc):
    step = pl.program_id(0)
    width = mine_ref.shape[1]
    core = core_ref[0]

    @pl.when(step < half)
    def _():
        start = pl.multiple_of((core * half + step) * width, width)
        acc[pl.ds(start, width), :] = dot_tn(mine_ref[...], right_ref[...])

    @pl.when(step >= half)
    def _():
        start = pl.multiple_of(((1 - core) * half + step - half) * width, width)
        acc[pl.ds(start, width), :] = dot_tn(other_ref[...].astype(bf16), right_ref[...])

    @pl.when(step == pl.num_programs(0) - 1)
    def _():
        store_pieces(table_ref, acc, send_ref, keep_ref)


def proj_grad_pieces(table, core, mine, other, right, parts, streams):
    rows, part = mine.shape
    width = 256
    half = part // width
    columns = D // streams
    piece, piece_shape = piece_specs(parts, D // parts, columns)
    return pl.pallas_call(
        partial(proj_grad_kernel, half),
        grid_spec=pltpu.PrefetchScalarGridSpec(
            num_scalar_prefetch=2,
            grid=(2 * half,),
            in_specs=[
                pl.BlockSpec((rows, width), lambda i, t, c: (0, jnp.minimum(i, half - 1))),
                pl.BlockSpec((rows, width), lambda i, t, c: (0, jnp.maximum(i - half, 0))),
                pl.BlockSpec((rows, columns), lambda i, t, c: (0, c[0])),
            ],
            out_specs=piece,
            scratch_shapes=[pltpu.VMEM((D, columns), f32)],
        ),
        out_shape=piece_shape,
        compiler_params=params(),
        cost_estimate=pl.CostEstimate(
            flops=2 * rows * D * columns,
            bytes_accessed=rows * (6 * part + 2 * columns) + 4 * D * columns,
            transcendentals=0,
        ),
        name="proj_grad",
    )(table, core, mine, other, right)


def causal_mask(transposed):
    row = lax.broadcasted_iota(jnp.int32, (BLK, BLK), 0)
    col = lax.broadcasted_iota(jnp.int32, (BLK, BLK), 1)
    return col >= row if transposed else row >= col


def head_masks():
    lane = lax.broadcasted_iota(jnp.int32, (1, PAIR), 1)
    first = lane < HEAD
    m0 = jnp.where(first, 1.0, 0.0)
    return m0.astype(bf16), (1.0 - m0).astype(bf16)


def state_mask():
    row = lax.broadcasted_iota(jnp.int32, (PAIR, 2 * PAIR), 0)
    col = lax.broadcasted_iota(jnp.int32, (PAIR, 2 * PAIR), 1)
    return (row < HEAD) == (col < PAIR)


def attention_forward_kernel(
    len_ref, core_ref, normed_ref, wq_ref, wk_ref, wv_ref, cos_ref, sin_ref, fw_ref, map_ref,
    q_ref, k_ref, v_ref, mix_ref, den_ref, state_ref, send_ref, weights, state,
):
    block = pl.program_id(1)

    @pl.when(block == 0)
    def _():
        weights[:, :PAIR] = wq_ref[...]
        weights[:, PAIR : 2 * PAIR] = wk_ref[...]
        weights[:, 2 * PAIR :] = wv_ref[...]
        state[...] = jnp.zeros_like(state)

    projected = dot(normed_ref[...], weights[...])
    cosine, sine = cos_ref[...], sin_ref[...]
    queries, keys = projected[:, :PAIR], projected[:, PAIR : 2 * PAIR]
    turned = jnp.concatenate(
        [
            jnp.concatenate([queries * cosine, queries * sine], 1),
            jnp.concatenate([keys * cosine, keys * sine], 1),
        ],
        0,
    )
    high = turned.astype(bf16)
    low = (turned - high.astype(f32)).astype(bf16)
    main = dot(high, map_ref[...])
    exponent = main[:, :PAIR] + main[:, PAIR:] + dot(low, map_ref[:, :PAIR])
    phi = jnp.exp(exponent) * fw_ref[...]
    rows = block * BLK + lax.broadcasted_iota(jnp.int32, (BLK, 1), 0)
    valid = jnp.where(rows < len_ref[0], 1.0, 0.0)
    q = phi[:BLK].astype(bf16)
    k = (phi[BLK:] * valid).astype(bf16)
    v = projected[:, 2 * PAIR :].astype(bf16)
    q_ref[...] = q
    k_ref[...] = k
    v_ref[...] = v

    m0, m1 = head_masks()
    v0, v1 = v * m0 + m1, v * m1 + m0
    causal = causal_mask(False)
    s0 = jnp.where(causal, dot_nt(q * m0, k), 0.0).astype(bf16)
    s1 = jnp.where(causal, dot_nt(q * m1, k), 0.0).astype(bf16)
    before = jnp.where(state_mask(), state[...], 0.0).astype(bf16)
    state_ref[0, 0] = before
    far = dot(q, before)
    o0 = dot(s0, v0) + far[:, :PAIR]
    o1 = dot(s1, v1) + far[:, PAIR:]
    first = lax.broadcasted_iota(jnp.int32, (BLK, PAIR), 1) < HEAD
    numerator = jnp.where(first, o0, o1)
    denominator = pltpu.roll(jnp.where(first, o1, o0), HEAD, 1)
    mixed = (numerator / denominator).astype(bf16)
    mix_ref[...] = mixed
    send_ref[...] = mixed.astype(f32)
    den_ref[...] = denominator
    state[...] += dot_tn(k, jnp.concatenate([v0, v1], 1))


def attention_forward(lengths, core, normed, w_qkv, cosine, sine, feature_weight, table, streams):
    rows = normed.shape[0]
    groups = HEADS // streams // 2
    width = groups * PAIR
    blocks = rows // BLK
    per = D // PAIR
    row_spec = pl.BlockSpec((BLK, PAIR), lambda g, b, n, c: (b, g))
    low_shape = jax.ShapeDtypeStruct((rows, width), bf16)

    def weight_spec(which):
        return pl.BlockSpec((D, PAIR), lambda g, b, n, c: (0, which * per + c[0] * groups + g))

    return pl.pallas_call(
        attention_forward_kernel,
        grid_spec=pltpu.PrefetchScalarGridSpec(
            num_scalar_prefetch=2,
            grid=(groups, blocks),
            in_specs=[
                pl.BlockSpec((BLK, D), lambda g, b, n, c: (b, 0)),
                weight_spec(0),
                weight_spec(1),
                weight_spec(2),
                pl.BlockSpec((BLK, PAIR), lambda g, b, n, c: (b, 0)),
                pl.BlockSpec((BLK, PAIR), lambda g, b, n, c: (b, 0)),
                pl.BlockSpec((1, PAIR), lambda g, b, n, c: (0, c[0] * groups + g)),
                pl.BlockSpec((2 * PAIR, 2 * PAIR), lambda g, b, n, c: (0, 0)),
            ],
            out_specs=[
                row_spec,
                row_spec,
                row_spec,
                row_spec,
                row_spec,
                pl.BlockSpec((1, 1, PAIR, 2 * PAIR), lambda g, b, n, c: (g, b, 0, 0)),
                row_spec,
            ],
            scratch_shapes=[pltpu.VMEM((D, 3 * PAIR), bf16), pltpu.VMEM((PAIR, 2 * PAIR), f32)],
        ),
        out_shape=[
            low_shape,
            low_shape,
            low_shape,
            low_shape,
            jax.ShapeDtypeStruct((rows, width), f32),
            jax.ShapeDtypeStruct((groups, blocks, PAIR, 2 * PAIR), bf16),
            jax.ShapeDtypeStruct((rows, width), f32),
        ],
        compiler_params=params(),
        cost_estimate=pl.CostEstimate(
            flops=groups * blocks * 2 * 65536 * 4600,
            bytes_accessed=groups * rows * D * 2 + 3 * D * width * 2 + rows * width * 12,
            transcendentals=2 * rows * width,
        ),
        name="attention_forward",
    )(lengths, core, normed, w_qkv, w_qkv, w_qkv, cosine, sine, feature_weight, table)


def attention_backward_kernel(
    blocks, core_ref, table_ref, g_ref, wp_ref, q_ref, k_ref, v_ref, mix_ref, den_ref, state_ref,
    cos_ref, sin_ref, back_ref, back_low_ref, sums_ref, nt_ref, *rest,
):
    dq_ref, dk_ref, dv_ref, fg_ref, send_ref, keep_ref, later, d_all, acc = rest[-9:]
    step = pl.program_id(0)

    @pl.when(step == 0)
    def _():
        later[...] = jnp.zeros_like(later)
        fg_ref[...] = jnp.zeros_like(fg_ref)

    @pl.when(step < blocks)
    def _():
        m0, m1 = head_masks()
        first = lax.broadcasted_iota(jnp.int32, (BLK, PAIR), 1) < HEAD
        d_mixed = dot_nt(g_ref[...], wp_ref[...])
        numer = d_mixed / den_ref[...]
        product = numer * mix_ref[...].astype(f32)
        p_high = product.astype(bf16)
        p_low = (product - p_high.astype(f32)).astype(bf16)
        sums = dot(jnp.concatenate([p_high, p_low], 1), sums_ref[...])
        d_o0 = jnp.where(first, numer, -sums).astype(bf16)
        d_o1 = jnp.where(first, -sums, numer).astype(bf16)
        low = numer.astype(bf16)
        dn0, dn1 = low * m0, low * m1
        q, k, v = q_ref[...], k_ref[...], v_ref[...]
        q0, q1 = q * m0, q * m1
        v0, v1 = v * m0 + m1, v * m1 + m0
        causal, flipped = causal_mask(False), causal_mask(True)
        ds0 = jnp.where(causal, dot_nt(d_o0, v0), 0.0).astype(bf16)
        ds1 = jnp.where(causal, dot_nt(d_o1, v1), 0.0).astype(bf16)
        st0 = jnp.where(flipped, dot_nt(k, q0), 0.0).astype(bf16)
        st1 = jnp.where(flipped, dot_nt(k, q1), 0.0).astype(bf16)
        dst0 = jnp.where(flipped, dot_nt(v0, d_o0), 0.0).astype(bf16)
        dst1 = jnp.where(flipped, dot_nt(v1, d_o1), 0.0).astype(bf16)
        d_o = jnp.concatenate([d_o0, d_o1], 1)
        after = jnp.where(state_mask(), later[...], 0.0).astype(bf16)
        own = (lax.broadcasted_iota(jnp.int32, (PAIR, PAIR), 0) < HEAD) == (
            lax.broadcasted_iota(jnp.int32, (PAIR, PAIR), 1) < HEAD
        )
        left = lax.broadcasted_iota(jnp.int32, (PAIR, PAIR), 1) < HEAD
        after_v = jnp.where(own, jnp.where(left, later[:, :PAIR], later[:, PAIR:]), 0.0).astype(bf16)
        k0, k1 = k * m0, k * m1
        d_q = dot_nt(d_o, state_ref[0, 0]) + dot(ds0, k0) + dot(ds1, k1)
        d_k = dot_nt(jnp.concatenate([v0, v1], 1), after) + dot(dst0, q0) + dot(dst1, q1)
        d_v = dot(k, after_v) + dot(st0, dn0) + dot(st1, dn1)
        later[...] += dot_tn(q, d_o)
        e_q = d_q * q.astype(f32)
        e_k = d_k * k.astype(f32)
        both = jnp.concatenate([e_q, e_k], 0)
        fg_ref[...] += jnp.sum((e_q + e_k).reshape(BLK // 8, 8, PAIR), axis=0)
        high = both.astype(bf16)
        lower = (both - high.astype(f32)).astype(bf16)
        turned = dot(jnp.concatenate([high, lower], 1), back_ref[...]) + dot(high, back_low_ref[...])
        cosine, sine = cos_ref[...], sin_ref[...]
        dq = (turned[:BLK, :PAIR] * cosine + turned[:BLK, PAIR:] * sine).astype(bf16)
        dk = (turned[BLK:, :PAIR] * cosine + turned[BLK:, PAIR:] * sine).astype(bf16)
        dv = d_v.astype(bf16)
        dq_ref[...] = dq
        dk_ref[...] = dk
        dv_ref[...] = dv
        here = pl.ds(pl.multiple_of((blocks - 1 - step) * BLK, BLK), BLK)
        d_all[here, :PAIR] = dq
        d_all[here, PAIR : 2 * PAIR] = dk
        d_all[here, 2 * PAIR :] = dv

    @pl.when(step >= blocks)
    def _():
        rows = nt_ref.shape[0]
        start = pl.multiple_of((step - blocks) * rows, rows)
        acc[pl.ds(start, rows), :] = dot(nt_ref[...], d_all[...])

    @pl.when(step == pl.num_programs(0) - 1)
    def _():
        store_pieces(table_ref, acc, send_ref, keep_ref)


def attention_backward(core, table, g, w_proj, kept, cosine, sine, backs, sums, normed_t, group, earlier, parts, streams):
    q, k, v, mixed, den, states = kept[:6]
    rows = g.shape[0]
    groups = HEADS // streams // 2
    blocks = rows // BLK
    mtile = 256
    m_steps = D // mtile

    def at(i):
        return jnp.maximum(blocks - 1 - i, 0)

    row_spec = pl.BlockSpec((BLK, PAIR), lambda i, c, t: (at(i), group))
    table_spec = pl.BlockSpec((BLK, PAIR), lambda i, c, t: (at(i), 0))
    piece, piece_shape = piece_specs(parts, D // parts, 3 * PAIR)
    low_shape = jax.ShapeDtypeStruct((rows, groups * PAIR), bf16)
    return pl.pallas_call(
        partial(attention_backward_kernel, blocks),
        grid_spec=pltpu.PrefetchScalarGridSpec(
            num_scalar_prefetch=2,
            grid=(blocks + m_steps,),
            in_specs=[
                pl.BlockSpec((BLK, D), lambda i, c, t: (at(i), 0)),
                pl.BlockSpec((PAIR, D), lambda i, c, t: (c[0] * groups + group, 0)),
                row_spec,
                row_spec,
                row_spec,
                row_spec,
                row_spec,
                pl.BlockSpec((1, 1, PAIR, 2 * PAIR), lambda i, c, t: (group, at(i), 0, 0)),
                table_spec,
                table_spec,
                pl.BlockSpec((2 * PAIR, 2 * PAIR), lambda i, c, t: (0, 0)),
                pl.BlockSpec((PAIR, 2 * PAIR), lambda i, c, t: (0, 0)),
                pl.BlockSpec((2 * PAIR, PAIR), lambda i, c, t: (0, 0)),
                pl.BlockSpec((mtile, rows), lambda i, c, t: (jnp.maximum(i - blocks, 0), 0)),
            ]
            + [pl.BlockSpec(memory_space=pl.ANY)] * len(earlier),
            out_specs=[row_spec, row_spec, row_spec, pl.BlockSpec((8, PAIR), lambda i, c, t: (0, 0))] + piece,
            scratch_shapes=[
                pltpu.VMEM((PAIR, 2 * PAIR), f32),
                pltpu.VMEM((rows, 3 * PAIR), bf16),
                pltpu.VMEM((D, 3 * PAIR), f32),
            ],
        ),
        out_shape=[low_shape, low_shape, low_shape, jax.ShapeDtypeStruct((8, PAIR), f32)] + piece_shape,
        input_output_aliases={16: 0, 17: 1, 18: 2} if earlier else {},
        compiler_params=params(),
        cost_estimate=pl.CostEstimate(
            flops=2 * 65536 * (blocks * 6500 + 16384),
            bytes_accessed=2 * (2 * rows * D + PAIR * D + rows * PAIR * 12) + 4 * D * 3 * PAIR,
            transcendentals=0,
        ),
        name=f"attention_backward_{group}",
    )(core, table, g, w_proj, q, k, v, mixed, den, states, cosine, sine, *backs, sums, normed_t, *earlier)


def branch_kernel(core_ref, act_ref, wout_ref, mix_ref, wproj_ref, out_ref):
    out_ref[...] = dot(act_ref[...], wout_ref[...]) + dot(mix_ref[...], wproj_ref[...])


def branch_sum(core, active, w_out, mixed, w_proj):
    rows, units = active.shape
    width = mixed.shape[1]
    tile = 256
    return pl.pallas_call(
        branch_kernel,
        grid_spec=pltpu.PrefetchScalarGridSpec(
            num_scalar_prefetch=1,
            grid=(rows // tile,),
            in_specs=[
                pl.BlockSpec((tile, units), lambda i, c: (i, 0)),
                pl.BlockSpec((units, D), lambda i, c: (0, 0)),
                pl.BlockSpec((tile, width), lambda i, c: (i, 0)),
                pl.BlockSpec((width, D), lambda i, c: (c[0], 0)),
            ],
            out_specs=pl.BlockSpec((tile, D), lambda i, c: (i, 0)),
        ),
        out_shape=jax.ShapeDtypeStruct((rows, D), f32),
        compiler_params=params(),
        cost_estimate=pl.CostEstimate(
            flops=2 * rows * D * (units + width),
            bytes_accessed=2 * (rows + D) * (units + width) + 4 * rows * D,
            transcendentals=0,
        ),
        name="branch_sum",
    )(core, active, w_out, mixed, w_proj)


def d_normed_kernel(core_ref, dh_ref, win_ref, dq_ref, dk_ref, dv_ref, wq_ref, wk_ref, wv_ref, out_ref):
    total = dot_nt(dh_ref[...], win_ref[...])
    total += dot_nt(dq_ref[...], wq_ref[...])
    total += dot_nt(dk_ref[...], wk_ref[...])
    total += dot_nt(dv_ref[...], wv_ref[...])
    out_ref[...] = total


def d_normed_sum(core, d_hidden, w_in, d_qkv, w_qkv, chunk, chunks, streams):
    rows, units = d_hidden.shape
    width = d_qkv[0].shape[1]
    tile = 256
    steps = rows // tile // chunks

    def row(i, c):
        return (chunk * steps + i, 0)

    def weight(which):
        return pl.BlockSpec((D, width), lambda i, c: (0, which * streams + c[0]))

    return pl.pallas_call(
        d_normed_kernel,
        grid_spec=pltpu.PrefetchScalarGridSpec(
            num_scalar_prefetch=1,
            grid=(steps,),
            in_specs=[
                pl.BlockSpec((tile, units), row),
                pl.BlockSpec((D, units), lambda i, c: (0, 0)),
                pl.BlockSpec((tile, width), row),
                pl.BlockSpec((tile, width), row),
                pl.BlockSpec((tile, width), row),
                weight(0),
                weight(1),
                weight(2),
            ],
            out_specs=pl.BlockSpec((tile, D), lambda i, c: (i, 0)),
        ),
        out_shape=jax.ShapeDtypeStruct((rows // chunks, D), f32),
        compiler_params=params(),
        cost_estimate=pl.CostEstimate(
            flops=2 * rows // chunks * D * (units + 3 * width),
            bytes_accessed=2 * (rows // chunks + D) * (units + 3 * width) + 4 * rows * D // chunks,
            transcendentals=0,
        ),
        name=f"d_normed_sum_{chunk}",
    )(core, d_hidden, w_in, *d_qkv, w_qkv, w_qkv, w_qkv)


def finish_kernel(first, len_ref, tok_ref, cot_ref, gain_ref, b0_ref, b1_ref, n0_ref, n1_ref, *rest):
    out_ref, grad_ref = rest[-2:]
    tile = tok_ref.shape[0]
    x = tok_ref[...].astype(f32)
    centered = x - jnp.mean(x, axis=-1, keepdims=True)
    var = jnp.mean(centered * centered, axis=-1, keepdims=True)
    inv_std = lax.rsqrt(var + EPSILON)
    unit = centered * inv_std
    rows = (first + pl.program_id(0)) * tile + lax.broadcasted_iota(jnp.int32, (tile, 1), 0)
    valid = jnp.where(rows < len_ref[0], 1.0, 0.0)
    out_ref[...] = (x + (b0_ref[...] + b1_ref[...]) * valid).astype(bf16)
    scaled = (n0_ref[...] + n1_ref[...]) * gain_ref[...]
    mean = jnp.mean(scaled, axis=-1, keepdims=True)
    cross = jnp.mean(scaled * unit, axis=-1, keepdims=True)
    grad_ref[...] = (cot_ref[...].astype(f32) + inv_std * (scaled - mean - unit * cross)).astype(bf16)


def finish(lengths, tokens, cotangent, gain, mine, other, n_mine, n_other, chunk, chunks, earlier):
    rows = tokens.shape[0]
    tile = 256
    steps = rows // tile // chunks
    first = chunk * steps
    whole = pl.BlockSpec((tile, D), lambda i, n: (first + i, 0))
    part = pl.BlockSpec((tile, D), lambda i, n: (i, 0))
    shape = jax.ShapeDtypeStruct((rows, D), bf16)
    return pl.pallas_call(
        partial(finish_kernel, first),
        grid_spec=pltpu.PrefetchScalarGridSpec(
            num_scalar_prefetch=1,
            grid=(steps,),
            in_specs=[whole, whole, pl.BlockSpec((1, D), lambda i, n: (0, 0)), whole, whole, part, part]
            + [pl.BlockSpec(memory_space=pl.ANY)] * len(earlier),
            out_specs=[whole, whole],
        ),
        out_shape=[shape, shape],
        input_output_aliases={8: 0, 9: 1} if earlier else {},
        compiler_params=params(),
        name=f"finish_{chunk}",
    )(lengths, tokens, cotangent, gain, mine, other, n_mine, n_other, *earlier)


def add_kernel(keep_lo, keep_hi, recv_lo, recv_hi, send_ref, keep_ref):
    keep_ref[...] = keep_lo[...] + recv_lo[...]
    send_ref[...] = keep_hi[...] + recv_hi[...]


def add_split(keep, recv):
    count, rows, columns = keep.shape
    half = count // 2
    low = pl.BlockSpec((1, rows, columns), lambda i: (i, 0, 0))
    high = pl.BlockSpec((1, rows, columns), lambda i: (half + i, 0, 0))
    shape = jax.ShapeDtypeStruct((half, rows, columns), f32)
    return pl.pallas_call(
        add_kernel,
        grid=(half,),
        in_specs=[low, high, low, high],
        out_specs=[low, low],
        out_shape=[shape, shape],
        compiler_params=params(),
        cost_estimate=pl.CostEstimate(
            flops=count * rows * columns, bytes_accessed=12 * count * rows * columns, transcendentals=0
        ),
        name="add_split",
    )(keep, keep, recv, recv)


def send_order(parts, streams):
    bits = [1 << b for b in range(parts.bit_length() - 1)]
    orders = []
    for s in range(streams):
        order = list(bits)
        if len(bits) >= 3:
            order[:3] = [bits[0], bits[2], bits[1]] if s % 2 == 0 else [bits[1], bits[2], bits[0]]
        orders.append(order)
    return orders


def relative_table(orders, parts):
    table = np.zeros((len(orders), parts), np.int32)
    for s, order in enumerate(orders):
        for p in range(parts):
            for b, mask in enumerate(order):
                if p >> (len(order) - 1 - b) & 1:
                    table[s, p] ^= mask
    return table


def solution(mesh):
    parts, streams = mesh.shape["dp"], mesh.shape["stream"]
    orders = send_order(parts, streams)
    relative = relative_table(orders, parts)
    cosine_np, sine_np, map_np, back_high_np, back_low_np = attention_tables()
    sums_np = np.zeros((2 * PAIR, PAIR), np.float32)
    for base in (0, PAIR):
        sums_np[base : base + HEAD, HEAD] = 1.0
        sums_np[base + HEAD : base + PAIR, 0] = 1.0

    def exchange(value, step):
        pairs = []
        for d in range(parts):
            for s in range(streams):
                pairs.append((d * streams + s, (d ^ orders[s][step]) * streams + s))
        return lax.ppermute(value, ("dp", "stream"), pairs)

    def partner(value):
        pairs = []
        for d in range(parts):
            for s in range(streams):
                pairs.append((d * streams + s, d * streams + (s ^ 1)))
        return lax.ppermute(value, ("dp", "stream"), pairs)

    def scatter(send, keep):
        steps = len(orders[0])
        for step in range(steps):
            recv = exchange(send, step)
            if step == steps - 1:
                return (keep + recv)[0]
            send, keep = add_split(keep, recv)

    def body(tokens, norm_gain, w_qkv, w_proj, w_in, w_out, feature_weight, lengths, cotangent):
        rows = tokens.shape[0]
        chip = lax.axis_index("dp")
        stream = lax.axis_index("stream")
        core = stream.astype(jnp.int32).reshape(1)
        table = jnp.where(stream == 0, relative[0], relative[-1]) ^ chip
        table = table.astype(jnp.int32)
        gain = norm_gain.reshape(1, D)
        fw = feature_weight.reshape(1, D)
        cosine, sine = jnp.asarray(cosine_np), jnp.asarray(sine_np)

        normed, normed_t, g = prep(lengths, tokens, cotangent, gain)
        win, wout = gather_units(core, w_in, w_out, parts, streams)
        units = win.shape[1]

        in_pieces, earlier = [], []
        size = 512
        for start in range(0, units, size):
            act, d_hidden, send, keep = ff_chunk(
                table, normed, g, normed_t, win, wout, start, size, earlier, parts
            )
            earlier = [act, d_hidden]
            in_pieces.append(scatter(send, keep))
        out_pieces = []
        size = 512
        for start in range(0, D, size):
            send, keep = left_grad(table, act, g, lambda t, b=start // size: b, size, parts, f"out_grad_{start}")
            out_pieces.append(scatter(send, keep))

        kept = attention_forward(lengths, core, normed, w_qkv, cosine, sine, fw, jnp.asarray(map_np), streams)
        mixed = kept[3]
        mixed_other = partner(kept[6])

        qkv_pieces, earlier, features = [], [], []
        backs = (jnp.asarray(back_high_np), jnp.asarray(back_low_np))
        for group in range(HEADS // streams // 2):
            dq, dk, dv, feature, send, keep = attention_backward(
                core, table, g, w_proj, kept, cosine, sine, backs, jnp.asarray(sums_np, bf16), normed_t, group,
                earlier, parts, streams,
            )
            earlier = [dq, dk, dv]
            features.append(jnp.sum(feature, axis=0))
            qkv_pieces.append(scatter(send, keep))
        send, keep = proj_grad_pieces(table, core, mixed, mixed_other, g, parts, streams)
        proj_piece = scatter(send, keep)

        branch = branch_sum(core, act, wout, mixed, w_proj)
        branch_other = partner(branch)
        chunks = 4
        done = []
        for chunk in range(chunks):
            part = d_normed_sum(core, d_hidden, win, earlier, w_qkv, chunk, chunks, streams)
            done = finish(
                lengths, tokens, cotangent, gain, branch, branch_other, part, partner(part), chunk, chunks, done
            )
        output, input_grad = done

        own = jnp.concatenate(features) / lax.dynamic_slice_in_dim(
            feature_weight, stream * (D // streams), D // streams
        )
        place = jnp.concatenate([jnp.where(stream == s, own, 0.0) for s in range(streams)])
        shares = place.reshape(parts, 1, D // parts)
        hot = (table[:, None] == jnp.arange(parts)[None, :]).astype(f32)
        shares = jnp.sum(hot[:, :, None, None] * shares[None], axis=1)
        shares = jnp.pad(shares, ((0, 0), (0, 7), (0, 128 - D // parts)))
        value = shares
        for step in range(len(orders[0])):
            half = value.shape[0] // 2
            value = value[:half] + exchange(value[half:], step)
        value = value[0] + partner(value[0])
        share = D // (parts * streams)
        feature_grad = lax.dynamic_slice(value, (0, stream * share), (1, share)).reshape(share)

        share_rows = D // parts
        half = share_rows // streams

        def keep_rows(piece):
            return lax.dynamic_slice_in_dim(piece, stream * half, half)

        def send_rows(piece):
            return lax.dynamic_slice_in_dim(piece, (1 - stream) * half, half)

        pieces = in_pieces + qkv_pieces + [proj_piece]
        mine = jnp.concatenate([keep_rows(p) for p in pieces], 1)
        other = partner(jnp.concatenate([send_rows(p) for p in pieces], 1))
        a = jnp.where(stream == 0, mine, other)
        b = jnp.where(stream == 0, other, mine)
        unit = units // parts
        in_grad = jnp.concatenate(
            [src[:, unit * i : unit * (i + 1)] for i in range(parts) for src in (a, b)], 1
        )
        qa, qb = a[:, units : units + 3 * D // streams], b[:, units : units + 3 * D // streams]
        groups = HEADS // streams // 2

        def third(src, which):
            return [src[:, (3 * g_ + which) * PAIR : (3 * g_ + which + 1) * PAIR] for g_ in range(groups)]

        qkv_grad = jnp.concatenate(sum([third(qa, w) + third(qb, w) for w in range(3)], []), 1)
        proj_grad = jnp.concatenate([a[:, units + 3 * D // streams :], b[:, units + 3 * D // streams :]], 1)
        out_grad = jnp.concatenate(out_pieces, 1)
        first_row = (chip * streams + stream) * half
        w_in_rows = lax.dynamic_slice_in_dim(w_in, first_row, half).astype(f32)
        w_qkv_rows = lax.dynamic_slice_in_dim(w_qkv, first_row, half).astype(f32)
        gain_rows = lax.dynamic_slice_in_dim(norm_gain, first_row, half)
        gain_grad = (jnp.sum(w_in_rows * in_grad, 1) + jnp.sum(w_qkv_rows * qkv_grad, 1)) / gain_rows
        return output, input_grad, gain_grad, qkv_grad, proj_grad, in_grad, out_grad, feature_grad

    both = P(("dp", "stream"), None)
    return jax.shard_map(
        body,
        mesh=mesh,
        in_specs=(P("dp", None), P(), P(), P(), P(), P(), P(), P("dp"), P("dp", None)),
        out_specs=(
            P("dp", None), P("dp", None), P(("dp", "stream")), both, both, both, both, P(("dp", "stream")),
        ),
        check_vma=False,
    )
```

```python
import math
from functools import partial

import jax
import jax.numpy as jnp
import numpy as np
from jax import lax
from jax.experimental import pallas as pl
from jax.experimental.pallas import tpu as pltpu
from jax.sharding import PartitionSpec as P

D = 1024
HEADS = 16
HEAD = 64
FF = 4096
ROT = 16
SLOT = 2048
EPSILON = 1e-05

f32 = jnp.float32
bf16 = jnp.bfloat16
VMEM_LIMIT = 56 * 1024 * 1024
BLK = 256
PAIR = 2 * HEAD


def dot(a, b):
    return lax.dot_general(a, b, (((1,), (0,)), ((), ())), preferred_element_type=f32)


def dot_nt(a, b):
    return lax.dot_general(a, b, (((1,), (1,)), ((), ())), preferred_element_type=f32)


def dot_tn(a, b):
    return lax.dot_general(a, b, (((0,), (0,)), ((), ())), preferred_element_type=f32)


def erf_inverse(y):
    x = 0.0
    for _ in range(200):
        step = (math.erf(x) - y) / (2.0 / math.sqrt(math.pi) * math.exp(-x * x))
        x -= max(-0.5, min(0.5, step))
    return x


def feature_table():
    i = np.arange(HEAD, dtype=np.float64)
    cos_table = np.cos(np.pi * (2.0 * i[:, None] + 1.0) * i[None, :] / (2.0 * HEAD))
    weights = np.where(i == 0, math.sqrt(1.0 / HEAD), math.sqrt(2.0 / HEAD))
    quantiles = math.sqrt(2.0) * np.array([erf_inverse(2.0 * (m + 0.5) / HEAD - 1.0) for m in range(HEAD)])
    return cos_table * (weights * 0.5 * quantiles)[None, :]


def split_table(table):
    high = table.astype(np.float32).astype(bf16)
    low = (table - high.astype(np.float64)).astype(np.float32).astype(bf16)
    return high, low


def attention_tables():
    half = ROT // 2
    pos = np.arange(SLOT, dtype=np.float32)
    inverse = (np.float32(10000.0) ** (-2.0 * np.arange(half, dtype=np.float32) / np.float32(ROT))).astype(np.float32)
    angles = (pos[:, None] * inverse[None, :]).astype(np.float32).astype(np.float64)
    cos_one = np.ones((SLOT, HEAD))
    sin_one = np.zeros((SLOT, HEAD))
    cos_one[:, :half] = np.cos(angles)
    cos_one[:, half:ROT] = np.cos(angles)
    sin_one[:, :half] = np.sin(angles)
    sin_one[:, half:ROT] = -np.sin(angles)
    cosine = np.concatenate([cos_one, cos_one], 1).astype(np.float32)
    sine = np.concatenate([sin_one, sin_one], 1).astype(np.float32)
    one = feature_table()
    pair = np.zeros((PAIR, PAIR))
    pair[:HEAD, :HEAD] = one
    pair[HEAD:, HEAD:] = one
    swapped = pair.copy()
    for base in (0, HEAD):
        swapped[base : base + half] = pair[base + half : base + ROT]
        swapped[base + half : base + ROT] = pair[base : base + half]
    both = np.concatenate([pair, swapped], 0)
    high, low = split_table(both)
    forward = np.concatenate([high, low], 1)
    back_high, back_low = split_table(np.concatenate([pair.T, swapped.T], 1))
    back_high2 = np.concatenate([back_high, back_high], 0)
    return cosine, sine, forward, back_high2, back_low


def params(**extra):
    return pltpu.CompilerParams(vmem_limit_bytes=VMEM_LIMIT, **extra)


def job_plan(job, steps):
    count, rows, _ = job[0][0].shape
    columns = sum(keep.shape[2] for keep, _ in job)
    half = max(count // 2, 1)
    blocks = math.gcd(half, steps) if steps < half else half
    return count, rows, columns, half, blocks


def with_jobs(kernel, scalars, steps, in_specs, out_specs, out_shape, jobs, **call):
    base_in, base_out = len(in_specs), len(out_specs)
    job_in, job_out, job_shape, arrays = [], [], [], []
    plans = [job_plan(job, steps) for job in jobs]
    for job, (count, rows, columns, half, blocks) in zip(jobs, plans):
        per = half // blocks
        for keep, recv in job:
            wide = keep.shape[2]
            low = pl.BlockSpec((per, rows, wide), lambda i, *_, b=blocks: (jnp.minimum(i, b - 1), 0, 0))
            high = pl.BlockSpec((per, rows, wide), lambda i, *_, b=blocks: (b + jnp.minimum(i, b - 1), 0, 0))
            if count == 1:
                job_in += [low, low]
                arrays += [keep, recv]
            else:
                job_in += [low, low, high, high]
                arrays += [keep, recv, keep, recv]
        spec = pl.BlockSpec((per, rows, columns), lambda i, *_, b=blocks: (jnp.minimum(i, b - 1), 0, 0))
        shape = jax.ShapeDtypeStruct((half, rows, columns), f32)
        outs = 1 if count == 1 else 2
        job_out += [spec] * outs
        job_shape += [shape] * outs

    def run(*refs):
        refs = list(refs)
        own = refs[: scalars + base_in]
        refs = refs[scalars + base_in :]
        ins, refs = refs[: len(job_in)], refs[len(job_in) :]
        own += refs[:base_out]
        refs = refs[base_out:]
        outs, rest = refs[: len(job_out)], refs[len(job_out) :]
        kernel(*own, *rest)
        step = pl.program_id(0)
        for job, (count, _, _, _, blocks) in zip(jobs, plans):
            parts_in = ins[: len(job) * (2 if count == 1 else 4)]
            ins = ins[len(parts_in) :]
            parts_out = outs[: 1 if count == 1 else 2]
            outs = outs[len(parts_out) :]

            @pl.when(step < blocks)
            def _(job=job, parts_in=parts_in, parts_out=parts_out):
                at = 0
                group = len(parts_in) // len(job)
                for n, (keep, _) in enumerate(job):
                    wide = keep.shape[2]
                    refs_in = parts_in[n * group : (n + 1) * group]
                    parts_out[0][:, :, at : at + wide] = refs_in[0][...] + refs_in[1][...]
                    if group == 4:
                        parts_out[1][:, :, at : at + wide] = refs_in[2][...] + refs_in[3][...]
                    at += wide

    grid_spec = pltpu.PrefetchScalarGridSpec(
        num_scalar_prefetch=scalars,
        grid=(steps,),
        in_specs=in_specs + job_in,
        out_specs=out_specs + job_out,
        scratch_shapes=call.pop("scratch_shapes", []),
    )
    operands = call.pop("operands")
    results = pl.pallas_call(
        run, grid_spec=grid_spec, out_shape=out_shape + job_shape, compiler_params=params(), **call
    )(*operands, *arrays)
    results = list(results)
    own, rest = results[:base_out], results[base_out:]
    sums = []
    for count, *_ in plans:
        outs = 1 if count == 1 else 2
        sums.append((None, rest[0]) if outs == 1 else (rest[1], rest[0]))
        rest = rest[outs:]
    return own, sums


def add_only(jobs, name):
    steps = max(1, max(job[0][0].shape[0] // 2 for job in jobs))
    return with_jobs(lambda *refs: None, 0, steps, [], [], [], jobs, operands=[], name=name)[1]


def prep_kernel(len_ref, tok_ref, cot_ref, gain_ref, normed_ref, g_ref):
    tile = tok_ref.shape[0]
    x = tok_ref[...].astype(f32)
    centered = x - jnp.mean(x, axis=-1, keepdims=True)
    var = jnp.mean(centered * centered, axis=-1, keepdims=True)
    normed_ref[...] = (centered * lax.rsqrt(var + EPSILON) * gain_ref[...]).astype(bf16)
    rows = pl.program_id(0) * tile + lax.broadcasted_iota(jnp.int32, (tile, 1), 0)
    valid = jnp.where(rows < len_ref[0], 1.0, 0.0)
    g_ref[...] = (cot_ref[...].astype(f32) * valid).astype(bf16)


def prep(lengths, tokens, cotangent, gain):
    rows = tokens.shape[0]
    tile = 256
    spec = pl.BlockSpec((tile, D), lambda i, n: (i, 0))
    shape = jax.ShapeDtypeStruct((rows, D), bf16)
    return pl.pallas_call(
        prep_kernel,
        grid_spec=pltpu.PrefetchScalarGridSpec(
            num_scalar_prefetch=1,
            grid=(rows // tile,),
            in_specs=[spec, spec, pl.BlockSpec((1, D), lambda i, n: (0, 0))],
            out_specs=[spec, spec],
        ),
        out_shape=[shape, shape],
        compiler_params=params(),
        name="prep",
    )(lengths, tokens, cotangent, gain)


ANY = pl.BlockSpec(memory_space=pl.ANY)


def copies(sources, targets, sems):
    return [pltpu.make_async_copy(a, b, sems.at[i]) for i, (a, b) in enumerate(zip(sources, targets))]


def piece_copy(table_ref, acc, share, rows, send_ref, keep_ref, sem, wait):
    half = keep_ref.shape[0]
    place = table_ref[share]
    source = acc.at[pl.ds(share * rows, rows), :]

    @pl.when(place >= half)
    def _():
        copy = pltpu.make_async_copy(source, send_ref.at[place - half], sem)
        copy.wait() if wait else copy.start()

    @pl.when(place < half)
    def _():
        copy = pltpu.make_async_copy(source, keep_ref.at[place], sem)
        copy.wait() if wait else copy.start()


def pieces_out(table_ref, acc, start, count, rows, send_ref, keep_ref, sems, wait=False):
    for share in range(start // rows, (start + count) // rows):
        piece_copy(table_ref, acc, share, rows, send_ref, keep_ref, sems.at[share], wait)


def piece_shapes(parts, rows, columns):
    shape = jax.ShapeDtypeStruct((parts // 2, rows, columns), f32)
    return [shape, shape]


def unit_sources(w_in_ref, w_out_ref, core, start, units, parts, streams, gathered):
    if gathered:
        return [(w_in_ref.at[:, pl.ds(start, units)], w_out_ref.at[pl.ds(start, units), :], 0, units)]
    unit = FF // (parts * streams)
    strips = []
    for at in range(start, start + units, unit):
        first = pl.multiple_of((at // unit * streams + core) * unit, unit)
        strips.append((w_in_ref.at[:, pl.ds(first, unit)], w_out_ref.at[pl.ds(first, unit), :], at - start, unit))
    return strips


def gather_units(core, w_in, w_out, parts, streams):
    unit = FF // (parts * streams)
    if unit % 128 == 0:
        return w_in, w_out, False
    a = lax.dynamic_index_in_dim(w_in.reshape(D, parts, streams, unit), core[0], 2, False)
    b = lax.dynamic_index_in_dim(w_out.reshape(parts, streams, unit, D), core[0], 1, False)
    return a.reshape(D, parts * unit), b.reshape(parts * unit, D), True


def gelu_parts(x):
    density = jnp.exp(x * x * -0.5)
    t = 1.0 / (1.0 + (0.3275911 / math.sqrt(2.0)) * jnp.abs(x))
    poly = 1.061405429 * t - 1.453152027
    poly = poly * t + 1.421413741
    poly = poly * t - 0.284496736
    poly = (poly * t + 0.254829592) * t
    tail = 0.5 * poly * density
    cdf = jnp.where(x >= 0, 1.0 - tail, tail)
    return x * cdf, cdf + x * density * (1.0 / math.sqrt(2.0 * math.pi))


TILE = 256


def ff_kernel(
    strips_of, start, steps, share_rows, core_ref, table_ref, normed_hbm, g_hbm, win_hbm, wout_hbm, *rest
):
    act_hbm, dh_hbm, send_hbm, keep_hbm = rest[-21:-17]
    normed, g, win, wout, h_a, h_b, d_a, d_b, act, d_hidden, acc = rest[-17:-6]
    row_sem, g_sem, in_sem, out_sem, piece_sem, store_sem = rest[-6:]
    step = pl.program_id(0)
    units = win.shape[1]
    rows = normed.shape[0]
    tile = 2 * TILE
    strips = strips_of(win_hbm, wout_hbm, core_ref[0])
    in_copies = copies([a for a, _, _, _ in strips], [win.at[:, pl.ds(at, n)] for _, _, at, n in strips], in_sem)
    out_copies = copies([b for _, b, _, _ in strips], [wout.at[pl.ds(at, n), :] for _, _, at, n in strips], out_sem)

    def row_copy(i, hbm, vmem, sem):
        here = pl.ds(pl.multiple_of(i * tile, tile), tile)
        return pltpu.make_async_copy(hbm.at[here, :], vmem.at[here, :], sem.at[i])

    @pl.when(step == 0)
    def _():
        row_copy(0, normed_hbm, normed, row_sem).start()
        for copy in in_copies:
            copy.start()
        row_copy(0, g_hbm, g, g_sem).start()
        for copy in out_copies:
            copy.start()
        for i in range(1, steps):
            row_copy(i, normed_hbm, normed, row_sem).start()
            row_copy(i, g_hbm, g, g_sem).start()
        for copy in in_copies + out_copies:
            copy.wait()

    def finish_tile(h, d, place):
        value, slope = gelu_parts(h[...])
        here = pl.ds(pl.multiple_of(place, TILE), TILE)
        act[here, :] = value.astype(bf16)
        d_hidden[here, :] = (d[...] * slope).astype(bf16)

    @pl.when(step < steps)
    def _():
        row_copy(step, normed_hbm, normed, row_sem).wait()
        row_copy(step, g_hbm, g, g_sem).wait()
        first = pl.multiple_of(step * tile, tile)
        here_a, here_b = pl.ds(first, TILE), pl.ds(first + TILE, TILE)
        finish_tile(h_b, d_b, step * tile)
        h_a[...] = dot(normed[here_a, :], win[...])
        d_a[...] = dot_nt(g[here_a, :], wout[...])
        finish_tile(h_a, d_a, step * tile + TILE)
        h_b[...] = dot(normed[here_b, :], win[...])
        d_b[...] = dot_nt(g[here_b, :], wout[...])

    columns = pl.ds(start, units)
    stores = [
        pltpu.make_async_copy(act.at[pl.ds(TILE, rows), :], act_hbm.at[:, columns], store_sem.at[0]),
        pltpu.make_async_copy(d_hidden.at[pl.ds(TILE, rows), :], dh_hbm.at[:, columns], store_sem.at[1]),
    ]

    @pl.when(step == steps)
    def _():
        finish_tile(h_b, d_b, step * tile)
        for copy in stores:
            copy.start()

    wide = 512
    for m in range(D // wide):

        @pl.when(step == steps + m)
        def _(m=m):
            acc[m * wide : (m + 1) * wide, :] = dot_tn(
                normed[:, m * wide : (m + 1) * wide], d_hidden[TILE : TILE + rows, :]
            )
            pieces_out(table_ref, acc, m * wide, wide, share_rows, send_hbm, keep_hbm, piece_sem)

    @pl.when(step == pl.num_programs(0) - 1)
    def _():
        pieces_out(table_ref, acc, 0, D, share_rows, send_hbm, keep_hbm, piece_sem, True)
        for copy in stores:
            copy.wait()


def ff_chunk(core, table, normed, g, weights, start, units, earlier, parts, streams, jobs=()):
    w_in, w_out, gathered = weights
    rows = normed.shape[0]
    total = FF // streams
    steps = rows // (2 * TILE)
    strips = 1 if gathered else units // (FF // (parts * streams))

    def strips_of(w_in_ref, w_out_ref, c):
        return unit_sources(w_in_ref, w_out_ref, c, start, units, parts, streams, gathered)

    low = jax.ShapeDtypeStruct((rows, total), bf16)
    return with_jobs(
        partial(ff_kernel, strips_of, start, steps, D // parts),
        2,
        steps + D // 512,
        [ANY] * (4 + len(earlier)),
        [ANY] * 4,
        [low, low] + piece_shapes(parts, D // parts, units),
        jobs,
        operands=[core, table, normed, g, w_in, w_out, *earlier],
        scratch_shapes=[
            pltpu.VMEM((rows, D), bf16),
            pltpu.VMEM((rows, D), bf16),
            pltpu.VMEM((D, units), bf16),
            pltpu.VMEM((units, D), bf16),
            pltpu.VMEM((TILE, units), f32),
            pltpu.VMEM((TILE, units), f32),
            pltpu.VMEM((TILE, units), f32),
            pltpu.VMEM((TILE, units), f32),
            pltpu.VMEM((rows + TILE, units), bf16),
            pltpu.VMEM((rows + TILE, units), bf16),
            pltpu.VMEM((D, units), f32),
            pltpu.SemaphoreType.DMA((steps,)),
            pltpu.SemaphoreType.DMA((steps,)),
            pltpu.SemaphoreType.DMA((strips,)),
            pltpu.SemaphoreType.DMA((strips,)),
            pltpu.SemaphoreType.DMA((parts,)),
            pltpu.SemaphoreType.DMA((2,)),
        ],
        input_output_aliases={6: 0, 7: 1} if earlier else {},
        cost_estimate=pl.CostEstimate(
            flops=6 * rows * D * units,
            bytes_accessed=2 * (2 * rows * D + 2 * units * D + 2 * rows * units) + 4 * D * units,
            transcendentals=rows * units,
        ),
        name=f"ff_chunk_{start}",
    )


def out_grad_kernel(share_rows, table_ref, left_ref, right_ref, after_ref, send_hbm, keep_hbm, acc, piece_sem):
    width = left_ref.shape[1]
    for m in range(acc.shape[0] // width):

        @pl.when(pl.program_id(0) == m)
        def _(m=m):
            acc[m * width : (m + 1) * width, :] = dot_tn(left_ref[...], right_ref[...])
            pieces_out(table_ref, acc, m * width, width, share_rows, send_hbm, keep_hbm, piece_sem)

    @pl.when(pl.program_id(0) == pl.num_programs(0) - 1)
    def _():
        pieces_out(table_ref, acc, 0, acc.shape[0], share_rows, send_hbm, keep_hbm, piece_sem, True)


def out_grad_pieces(table, left, right, block, columns, after, parts, jobs=()):
    rows, total = left.shape
    width = 512
    return with_jobs(
        partial(out_grad_kernel, total // parts),
        1,
        total // width,
        [
            pl.BlockSpec((rows, width), lambda i, t: (0, i)),
            pl.BlockSpec((rows, columns), lambda i, t: (0, block)),
            ANY,
        ],
        [ANY, ANY],
        piece_shapes(parts, total // parts, columns),
        jobs,
        operands=[table, left, right, after],
        scratch_shapes=[pltpu.VMEM((total, columns), f32), pltpu.SemaphoreType.DMA((parts,))],
        cost_estimate=pl.CostEstimate(
            flops=2 * rows * total * columns,
            bytes_accessed=2 * rows * (total + columns) + 4 * total * columns,
            transcendentals=0,
        ),
        name=f"out_grad_{block}",
    )


def proj_grad_kernel(
    share_rows, core_ref, table_ref, mine_ref, other_ref, right_ref, after_ref, send_hbm, keep_hbm, acc, piece_sem
):
    width = mine_ref.shape[1]
    core = core_ref[0]
    step = pl.program_id(0)

    @pl.when(step == 0)
    def _():
        acc[pl.ds(pl.multiple_of(core * width, width), width), :] = dot_tn(mine_ref[...], right_ref[...])

    @pl.when(step == 1)
    def _():
        acc[pl.ds(pl.multiple_of((1 - core) * width, width), width), :] = dot_tn(
            other_ref[...].astype(bf16), right_ref[...]
        )
        pieces_out(table_ref, acc, 0, acc.shape[0], share_rows, send_hbm, keep_hbm, piece_sem)
        pieces_out(table_ref, acc, 0, acc.shape[0], share_rows, send_hbm, keep_hbm, piece_sem, True)


def proj_grad_pieces(core, table, mine, other, right, after, parts, streams, jobs=()):
    rows, part = mine.shape
    columns = D // streams
    return with_jobs(
        partial(proj_grad_kernel, D // parts),
        2,
        2,
        [
            pl.BlockSpec((rows, part), lambda i, c, t: (0, 0)),
            pl.BlockSpec((rows, part), lambda i, c, t: (0, 0)),
            pl.BlockSpec((rows, columns), lambda i, c, t: (0, c[0])),
            ANY,
        ],
        [ANY, ANY],
        piece_shapes(parts, D // parts, columns),
        jobs,
        operands=[core, table, mine, other, right, after],
        scratch_shapes=[pltpu.VMEM((D, columns), f32), pltpu.SemaphoreType.DMA((parts,))],
        cost_estimate=pl.CostEstimate(
            flops=2 * rows * D * columns,
            bytes_accessed=rows * (6 * part + 2 * columns) + 4 * D * columns,
            transcendentals=0,
        ),
        name="proj_grad",
    )


def causal_mask(transposed):
    row = lax.broadcasted_iota(jnp.int32, (BLK, BLK), 0)
    col = lax.broadcasted_iota(jnp.int32, (BLK, BLK), 1)
    return col >= row if transposed else row >= col


def head_masks():
    lane = lax.broadcasted_iota(jnp.int32, (1, PAIR), 1)
    first = lane < HEAD
    m0 = jnp.where(first, 1.0, 0.0)
    return m0.astype(bf16), (1.0 - m0).astype(bf16)


def state_mask():
    row = lax.broadcasted_iota(jnp.int32, (PAIR, 2 * PAIR), 0)
    col = lax.broadcasted_iota(jnp.int32, (PAIR, 2 * PAIR), 1)
    return (row < HEAD) == (col < PAIR)


def attention_forward_kernel(
    groups, len_ref, core_ref, normed_ref, wq_ref, wk_ref, wv_ref, cos_ref, sin_ref, fw_ref, map_ref, after_ref,
    q_ref, k_ref, v_ref, mix_ref, den_ref, state_ref, send_ref, state,
):
    block = pl.program_id(0)

    @pl.when(block == 0)
    def _():
        state[...] = jnp.zeros_like(state)

    rows = normed_ref[...]
    queries_all, keys_all, values_all = dot(rows, wq_ref[...]), dot(rows, wk_ref[...]), dot(rows, wv_ref[...])
    cosine, sine = cos_ref[...], sin_ref[...]
    place = block * BLK + lax.broadcasted_iota(jnp.int32, (BLK, 1), 0)
    valid = jnp.where(place < len_ref[0], 1.0, 0.0)
    m0, m1 = head_masks()
    causal = causal_mask(False)
    keep_state = state_mask()
    first = lax.broadcasted_iota(jnp.int32, (BLK, PAIR), 1) < HEAD
    for group in range(groups):
        here = slice(group * PAIR, (group + 1) * PAIR)
        queries, keys = queries_all[:, here], keys_all[:, here]
        turned = jnp.concatenate(
            [
                jnp.concatenate([queries * cosine, queries * sine], 1),
                jnp.concatenate([keys * cosine, keys * sine], 1),
            ],
            0,
        )
        high = turned.astype(bf16)
        low = (turned - high.astype(f32)).astype(bf16)
        main = dot(high, map_ref[...])
        exponent = main[:, :PAIR] + main[:, PAIR:] + dot(low, map_ref[:, :PAIR])
        phi = jnp.exp(exponent) * fw_ref[:, here]
        q = phi[:BLK].astype(bf16)
        k = (phi[BLK:] * valid).astype(bf16)
        v = values_all[:, here].astype(bf16)
        q_ref[:, here] = q
        k_ref[:, here] = k
        v_ref[:, here] = v
        v0, v1 = v * m0 + m1, v * m1 + m0
        s0 = jnp.where(causal, dot_nt(q * m0, k), 0.0).astype(bf16)
        s1 = jnp.where(causal, dot_nt(q * m1, k), 0.0).astype(bf16)
        before = jnp.where(keep_state, state[group], 0.0).astype(bf16)
        state_ref[group, 0] = before
        far = dot(q, before)
        o0 = dot(s0, v0) + far[:, :PAIR]
        o1 = dot(s1, v1) + far[:, PAIR:]
        numerator = jnp.where(first, o0, o1)
        denominator = pltpu.roll(jnp.where(first, o1, o0), HEAD, 1)
        mixed = (numerator / denominator).astype(bf16)
        mix_ref[:, here] = mixed
        send_ref[:, here] = mixed.astype(f32)
        den_ref[:, here] = denominator
        state[group] += dot_tn(k, jnp.concatenate([v0, v1], 1))


def attention_forward(
    lengths, core, normed, w_qkv, cosine, sine, feature_weight, table, after, streams, jobs=()
):
    rows = normed.shape[0]
    groups = HEADS // streams // 2
    width = groups * PAIR
    blocks = rows // BLK
    row_spec = pl.BlockSpec((BLK, width), lambda b, n, c: (b, 0))
    table_spec = pl.BlockSpec((BLK, PAIR), lambda b, n, c: (b, 0))
    low_shape = jax.ShapeDtypeStruct((rows, width), bf16)
    wide_shape = jax.ShapeDtypeStruct((rows, width), f32)

    def weight_spec(which):
        return pl.BlockSpec((D, width), lambda b, n, c: (0, which * streams + c[0]))

    return with_jobs(
        partial(attention_forward_kernel, groups),
        2,
        blocks,
        [
            pl.BlockSpec((BLK, D), lambda b, n, c: (b, 0)),
            weight_spec(0),
            weight_spec(1),
            weight_spec(2),
            table_spec,
            table_spec,
            pl.BlockSpec((1, width), lambda b, n, c: (0, c[0])),
            pl.BlockSpec((2 * PAIR, 2 * PAIR), lambda b, n, c: (0, 0)),
            ANY,
        ],
        [
            row_spec,
            row_spec,
            row_spec,
            row_spec,
            row_spec,
            pl.BlockSpec((groups, 1, PAIR, 2 * PAIR), lambda b, n, c: (0, b, 0, 0)),
            row_spec,
        ],
        [
            low_shape,
            low_shape,
            low_shape,
            low_shape,
            wide_shape,
            jax.ShapeDtypeStruct((groups, blocks, PAIR, 2 * PAIR), bf16),
            wide_shape,
        ],
        jobs,
        operands=[lengths, core, normed, w_qkv, w_qkv, w_qkv, cosine, sine, feature_weight, table, after],
        scratch_shapes=[pltpu.VMEM((groups, PAIR, 2 * PAIR), f32)],
        cost_estimate=pl.CostEstimate(
            flops=groups * blocks * 2 * 65536 * 4600,
            bytes_accessed=rows * D * 2 + 3 * D * width * 2 + rows * width * 16,
            transcendentals=2 * rows * width,
        ),
        name="attention_forward",
    )


def attention_backward_kernel(
    blocks, groups, share_rows, core_ref, table_ref, g_ref, wp_ref, q_ref, k_ref, v_ref, mix_ref, den_ref, state_ref,
    cos_ref, sin_ref, back_ref, back_low_ref, sums_ref, normed_hbm, *rest,
):
    dq_ref, dk_ref, dv_ref, fg_ref, send_hbm, keep_hbm, later, d_all, acc, normed, load_sem, piece_sem = rest[-12:]
    step = pl.program_id(0)
    width = groups * PAIR
    load = pltpu.make_async_copy(normed_hbm, normed, load_sem)

    @pl.when(step == 0)
    def _():
        load.start()
        later[...] = jnp.zeros_like(later)
        fg_ref[...] = jnp.zeros_like(fg_ref)

    @pl.when(step < blocks)
    def _():
        m0, m1 = head_masks()
        first = lax.broadcasted_iota(jnp.int32, (BLK, PAIR), 1) < HEAD
        left = lax.broadcasted_iota(jnp.int32, (PAIR, PAIR), 1) < HEAD
        own = (lax.broadcasted_iota(jnp.int32, (PAIR, PAIR), 0) < HEAD) == left
        causal, flipped = causal_mask(False), causal_mask(True)
        keep_state = state_mask()
        cosine, sine = cos_ref[...], sin_ref[...]
        d_mixed_all = dot_nt(g_ref[...], wp_ref[...])
        place = pl.ds(pl.multiple_of((blocks - 1 - step) * BLK, BLK), BLK)
        for group in range(groups):
            here = slice(group * PAIR, (group + 1) * PAIR)
            numer = d_mixed_all[:, here] / den_ref[:, here]
            product = numer * mix_ref[:, here].astype(f32)
            p_high = product.astype(bf16)
            p_low = (product - p_high.astype(f32)).astype(bf16)
            sums = dot(jnp.concatenate([p_high, p_low], 1), sums_ref[...])
            d_o0 = jnp.where(first, numer, -sums).astype(bf16)
            d_o1 = jnp.where(first, -sums, numer).astype(bf16)
            low = numer.astype(bf16)
            dn0, dn1 = low * m0, low * m1
            q, k, v = q_ref[:, here], k_ref[:, here], v_ref[:, here]
            q0, q1 = q * m0, q * m1
            v0, v1 = v * m0 + m1, v * m1 + m0
            ds0 = jnp.where(causal, dot_nt(d_o0, v0), 0.0).astype(bf16)
            ds1 = jnp.where(causal, dot_nt(d_o1, v1), 0.0).astype(bf16)
            st0 = jnp.where(flipped, dot_nt(k, q0), 0.0).astype(bf16)
            st1 = jnp.where(flipped, dot_nt(k, q1), 0.0).astype(bf16)
            dst0 = jnp.where(flipped, dot_nt(v0, d_o0), 0.0).astype(bf16)
            dst1 = jnp.where(flipped, dot_nt(v1, d_o1), 0.0).astype(bf16)
            d_o = jnp.concatenate([d_o0, d_o1], 1)
            behind = later[group]
            after = jnp.where(keep_state, behind, 0.0).astype(bf16)
            after_v = jnp.where(own, jnp.where(left, behind[:, :PAIR], behind[:, PAIR:]), 0.0).astype(bf16)
            k0, k1 = k * m0, k * m1
            d_q = dot_nt(d_o, state_ref[group, 0]) + dot(ds0, k0) + dot(ds1, k1)
            d_k = dot_nt(jnp.concatenate([v0, v1], 1), after) + dot(dst0, q0) + dot(dst1, q1)
            d_v = dot(k, after_v) + dot(st0, dn0) + dot(st1, dn1)
            later[group] += dot_tn(q, d_o)
            e_q = d_q * q.astype(f32)
            e_k = d_k * k.astype(f32)
            both = jnp.concatenate([e_q, e_k], 0)
            fg_ref[:, here] += jnp.sum((e_q + e_k).reshape(BLK // 8, 8, PAIR), axis=0)
            high = both.astype(bf16)
            lower = (both - high.astype(f32)).astype(bf16)
            turned = dot(jnp.concatenate([high, lower], 1), back_ref[...]) + dot(high, back_low_ref[...])
            dq = (turned[:BLK, :PAIR] * cosine + turned[:BLK, PAIR:] * sine).astype(bf16)
            dk = (turned[BLK:, :PAIR] * cosine + turned[BLK:, PAIR:] * sine).astype(bf16)
            dv = d_v.astype(bf16)
            dq_ref[:, here] = dq
            dk_ref[:, here] = dk
            dv_ref[:, here] = dv
            d_all[place, group * PAIR : (group + 1) * PAIR] = dq
            d_all[place, width + group * PAIR : width + (group + 1) * PAIR] = dk
            d_all[place, 2 * width + group * PAIR : 2 * width + (group + 1) * PAIR] = dv

    @pl.when(step == blocks)
    def _():
        load.wait()

    wide = 512
    for m in range(D // wide):

        @pl.when(step == blocks + m)
        def _(m=m):
            acc[m * wide : (m + 1) * wide, :] = dot_tn(normed[:, m * wide : (m + 1) * wide], d_all[...])
            pieces_out(table_ref, acc, m * wide, wide, share_rows, send_hbm, keep_hbm, piece_sem)

    @pl.when(step == pl.num_programs(0) - 1)
    def _():
        pieces_out(table_ref, acc, 0, D, share_rows, send_hbm, keep_hbm, piece_sem, True)


def attention_backward(
    core, table, g, w_proj, kept, cosine, sine, backs, sums, normed, call, groups, earlier, after, parts, streams, jobs=()
):
    q, k, v, mixed, den, states = kept[:6]
    rows = g.shape[0]
    calls = HEADS // streams // 2 // groups
    blocks = rows // BLK
    width = groups * PAIR

    def at(i):
        return jnp.maximum(blocks - 1 - i, 0)

    row_spec = pl.BlockSpec((BLK, width), lambda i, c, t: (at(i), call))
    table_spec = pl.BlockSpec((BLK, PAIR), lambda i, c, t: (at(i), 0))
    low_shape = jax.ShapeDtypeStruct((rows, calls * width), bf16)
    return with_jobs(
        partial(attention_backward_kernel, blocks, groups, D // parts),
        2,
        blocks + D // 512,
        [
            pl.BlockSpec((BLK, D), lambda i, c, t: (at(i), 0)),
            pl.BlockSpec((width, D), lambda i, c, t: (c[0] * calls + call, 0)),
            row_spec,
            row_spec,
            row_spec,
            row_spec,
            row_spec,
            pl.BlockSpec((groups, 1, PAIR, 2 * PAIR), lambda i, c, t: (call, at(i), 0, 0)),
            table_spec,
            table_spec,
            pl.BlockSpec((2 * PAIR, 2 * PAIR), lambda i, c, t: (0, 0)),
            pl.BlockSpec((PAIR, 2 * PAIR), lambda i, c, t: (0, 0)),
            pl.BlockSpec((2 * PAIR, PAIR), lambda i, c, t: (0, 0)),
            ANY,
            ANY,
        ]
        + [ANY] * len(earlier),
        [row_spec, row_spec, row_spec, pl.BlockSpec((8, width), lambda i, c, t: (0, 0)), ANY, ANY],
        [low_shape, low_shape, low_shape, jax.ShapeDtypeStruct((8, width), f32)]
        + piece_shapes(parts, D // parts, 3 * width),
        jobs,
        operands=[
            core, table, g, w_proj, q, k, v, mixed, den, states, cosine, sine, *backs, sums, normed, after, *earlier
        ],
        scratch_shapes=[
            pltpu.VMEM((groups, PAIR, 2 * PAIR), f32),
            pltpu.VMEM((rows, 3 * width), bf16),
            pltpu.VMEM((D, 3 * width), f32),
            pltpu.VMEM((rows, D), bf16),
            pltpu.SemaphoreType.DMA,
            pltpu.SemaphoreType.DMA((parts,)),
        ],
        input_output_aliases={17: 0, 18: 1, 19: 2} if earlier else {},
        cost_estimate=pl.CostEstimate(
            flops=2 * 65536 * groups * (blocks * 6500 + 16384),
            bytes_accessed=2 * (2 * rows * D + width * D + rows * width * 12) + 4 * D * 3 * width,
            transcendentals=0,
        ),
        name=f"attention_backward_{call}",
    )


def tail_kernel(
    strips_of, tiles, act_ref, dh_ref, mix_ref, dq_ref, dk_ref, dv_ref, tok_ref, cot_ref, valid_ref, gain_ref,
    wproj_ref, wq_ref, wk_ref, wv_ref, win_hbm, wout_hbm, out_ref, grad_ref,
    win, wout, mine, arrived, in_sem, out_sem, send_sem, recv_sem,
):
    step = pl.program_id(0)
    chip, core = lax.axis_index("dp"), lax.axis_index("stream")
    partner = (chip, 1 - core)
    strips = strips_of(win_hbm, wout_hbm, core)
    loads = copies([a for a, _, _, _ in strips], [win.at[:, pl.ds(at, n)] for _, _, at, n in strips], in_sem)
    loads += copies([b for _, b, _, _ in strips], [wout.at[pl.ds(at, n), :] for _, _, at, n in strips], out_sem)

    def send(i):
        return pltpu.make_async_remote_copy(
            src_ref=mine.at[lax.rem(i, 2)],
            dst_ref=arrived.at[i],
            send_sem=send_sem.at[i],
            recv_sem=recv_sem.at[i],
            device_id=partner,
            device_id_type=pl.DeviceIdType.MESH,
        )

    @pl.when(step == 0)
    def _():
        for load in loads:
            load.start()
        barrier = pltpu.get_barrier_semaphore()
        pl.semaphore_signal(barrier, inc=1, device_id=partner, device_id_type=pl.DeviceIdType.MESH)
        pl.semaphore_wait(barrier, 1)
        for load in loads:
            load.wait()

    @pl.when((step >= 2) & (step < tiles))
    def _():
        send(step - 2).wait_send()

    @pl.when(step < tiles)
    def _():
        slot = lax.rem(step, 2)
        mine[slot, 0] = dot(act_ref[...], wout[...]) + dot(mix_ref[...], wproj_ref[...])
        d_normed = dot_nt(dh_ref[...], win[...]) + dot_nt(dq_ref[...], wq_ref[...])
        d_normed += dot_nt(dk_ref[...], wk_ref[...]) + dot_nt(dv_ref[...], wv_ref[...])
        mine[slot, 1] = d_normed
        send(step).start()

    @pl.when(step >= 1)
    def _():
        send(step - 1).wait_recv()
        slot = lax.rem(step + 1, 2)
        x = tok_ref[...].astype(f32)
        centered = x - jnp.mean(x, axis=-1, keepdims=True)
        var = jnp.mean(centered * centered, axis=-1, keepdims=True)
        inv_std = lax.rsqrt(var + EPSILON)
        unit = centered * inv_std
        out_ref[...] = (x + (mine[slot, 0] + arrived[step - 1, 0]) * valid_ref[...]).astype(bf16)
        scaled = (mine[slot, 1] + arrived[step - 1, 1]) * gain_ref[...]
        mean = jnp.mean(scaled, axis=-1, keepdims=True)
        cross = jnp.mean(scaled * unit, axis=-1, keepdims=True)
        grad_ref[...] = (cot_ref[...].astype(f32) + inv_std * (scaled - mean - unit * cross)).astype(bf16)

    @pl.when(step == tiles)
    def _():
        send(tiles - 2).wait_send()
        send(tiles - 1).wait_send()


def tail(active, d_hidden, mixed, d_qkv, tokens, cotangent, valid, gain, weights, w_proj, w_qkv, parts, streams):
    w_in, w_out, gathered = weights
    rows, units = active.shape
    width = mixed.shape[1]
    tiles = rows // TILE
    strips = 1 if gathered else parts

    def strips_of(w_in_ref, w_out_ref, core):
        return unit_sources(w_in_ref, w_out_ref, core, 0, units, parts, streams, gathered)

    def now(i):
        return (jnp.minimum(i, tiles - 1), 0)

    def before(i):
        return (jnp.maximum(i - 1, 0), 0)

    def weight(which):
        return pl.BlockSpec((D, width), lambda i: (0, which * streams + lax.axis_index("stream")))

    shape = jax.ShapeDtypeStruct((rows, D), bf16)
    return pl.pallas_call(
        partial(tail_kernel, strips_of, tiles),
        grid=(tiles + 1,),
        in_specs=[
            pl.BlockSpec((TILE, units), now),
            pl.BlockSpec((TILE, units), now),
            pl.BlockSpec((TILE, width), now),
            pl.BlockSpec((TILE, width), now),
            pl.BlockSpec((TILE, width), now),
            pl.BlockSpec((TILE, width), now),
            pl.BlockSpec((TILE, D), before),
            pl.BlockSpec((TILE, D), before),
            pl.BlockSpec((TILE, 1), before),
            pl.BlockSpec((1, D), lambda i: (0, 0)),
            pl.BlockSpec((width, D), lambda i: (lax.axis_index("stream"), 0)),
            weight(0),
            weight(1),
            weight(2),
            ANY,
            ANY,
        ],
        out_specs=[pl.BlockSpec((TILE, D), before), pl.BlockSpec((TILE, D), before)],
        out_shape=[shape, shape],
        scratch_shapes=[
            pltpu.VMEM((D, units), bf16),
            pltpu.VMEM((units, D), bf16),
            pltpu.VMEM((2, 2, TILE, D), f32),
            pltpu.VMEM((tiles, 2, TILE, D), f32),
            pltpu.SemaphoreType.DMA((strips,)),
            pltpu.SemaphoreType.DMA((strips,)),
            pltpu.SemaphoreType.DMA((tiles,)),
            pltpu.SemaphoreType.DMA((tiles,)),
        ],
        compiler_params=params(collective_id=0, has_side_effects=True),
        cost_estimate=pl.CostEstimate(
            flops=2 * rows * D * (2 * units + 4 * width),
            bytes_accessed=2 * (rows + D) * (2 * units + 4 * width) + 8 * rows * D,
            transcendentals=0,
        ),
        name="tail",
    )(
        active, d_hidden, mixed, *d_qkv, tokens, cotangent, valid, gain, w_proj, w_qkv, w_qkv, w_qkv, w_in, w_out
    )


def send_orders(parts, streams, kind):
    bits = [1 << b for b in range(parts.bit_length() - 1)]
    first = {"xy": ("xzy", "yzx"), "zz": ("zxy", "zyx"), "xx": ("xyz", "yxz")}[kind]
    orders = []
    for s in range(streams):
        order = list(bits)
        if len(bits) >= 3:
            order[:3] = [bits["xyz".index(axis)] for axis in first[s % 2]]
        orders.append(order)
    return orders


def relative_table(orders, parts):
    table = np.zeros((len(orders), parts), np.int32)
    for s, order in enumerate(orders):
        for p in range(parts):
            for b, mask in enumerate(order):
                if p >> (len(order) - 1 - b) & 1:
                    table[s, p] ^= mask
    return table


KINDS = ("xy", "zz", "xx")
FF_PLAN = ((512, "xy", ()), (512, "xy", ()), (1024, "xy", ("in0",)))
OUT_PLAN = (("xy", ("in1",)), ("xy", ("in0",)))
FORWARD_PLAN = ("in2", "in1")
PROJ_AT = 1
BACKWARD_PLAN = (("xy", ("out0",)), ("xy", ("out1",)))
PROJ_PLAN = ("xy", ("in2",))
AFTER_PLAN = ()


def solution(mesh):
    parts, streams = mesh.shape["dp"], mesh.shape["stream"]
    steps = parts.bit_length() - 1
    orders = {kind: send_orders(parts, streams, kind) for kind in KINDS}
    relative = {kind: relative_table(orders[kind], parts) for kind in KINDS}
    inverse = {kind: np.argsort(relative[kind], axis=1) for kind in KINDS}
    chips = np.arange(parts)
    place_np = np.stack([inverse[kind][:, chips[:, None] ^ chips[None, :]] for kind in KINDS]).astype(np.int32)
    cosine_np, sine_np, map_np, back_high_np, back_low_np = attention_tables()
    sums_np = np.zeros((2 * PAIR, PAIR), np.float32)
    for base in (0, PAIR):
        sums_np[base : base + HEAD, HEAD] = 1.0
        sums_np[base + HEAD : base + PAIR, 0] = 1.0

    def exchange(value, kind, step):
        pairs = []
        for d in range(parts):
            for s in range(streams):
                pairs.append((d * streams + s, (d ^ orders[kind][s][step]) * streams + s))
        return lax.ppermute(value, ("dp", "stream"), pairs)

    def partner(value):
        pairs = []
        for d in range(parts):
            for s in range(streams):
                pairs.append((d * streams + s, d * streams + (s ^ 1)))
        return lax.ppermute(value, ("dp", "stream"), pairs)

    def body(tokens, norm_gain, w_qkv, w_proj, w_in, w_out, feature_weight, lengths, cotangent):
        rows = tokens.shape[0]
        chip = lax.axis_index("dp")
        stream = lax.axis_index("stream")
        core = stream.astype(jnp.int32).reshape(1)
        places = lax.dynamic_slice(
            jnp.asarray(place_np), (0, stream, chip, 0), (len(KINDS), 1, 1, parts)
        ).reshape(len(KINDS), parts)
        places = {kind: places[n] for n, kind in enumerate(KINDS)}
        gain = norm_gain.reshape(1, D)
        fw = feature_weight.reshape(1, D)
        cosine, sine = jnp.asarray(cosine_np), jnp.asarray(sine_np)
        valid = (jnp.arange(rows) < lengths[0]).astype(f32).reshape(rows, 1)
        weights = gather_units(core, w_in, w_out, parts, streams)
        units = FF // streams

        flight, final = {}, {}

        widths = {}

        def launch(name, kind, send, keep, step=0):
            widths.setdefault(name, keep.shape[2])
            flight[name] = (kind, step, keep, exchange(send, kind, step))

        def jobs_of(names):
            groups = [name if isinstance(name, tuple) else (name,) for name in names]
            return [[flight[name][2:] for name in group] for group in groups], groups

        def landed(groups, sums):
            for group, (send, keep) in zip(groups, sums):
                kind, step = flight[group[0]][:2]
                for name in group:
                    del flight[name]
                name = group[0] if len(group) == 1 else "+".join(group)
                if step == steps - 1:
                    final[name] = keep[0]
                else:
                    launch(name, kind, send, keep, step + 1)

        def step_with(function, *args, names=(), **kwargs):
            jobs, groups = jobs_of(names)
            own, sums = function(*args, jobs=jobs, **kwargs)
            landed(groups, sums)
            return own

        normed, g = prep(lengths, tokens, cotangent, gain)

        earlier, start = [], 0
        for n, (size, kind, names) in enumerate(FF_PLAN):
            act, d_hidden, send, keep = step_with(
                ff_chunk, core, places[kind], normed, g, weights, start, size, earlier, parts, streams, names=names
            )
            earlier, start = [act, d_hidden], start + size
            launch(f"in{n}", kind, send, keep)
        width = D // len(OUT_PLAN)
        for n, (kind, names) in enumerate(OUT_PLAN):
            send, keep = step_with(
                out_grad_pieces, places[kind], act, g, n, width, keep, parts, names=names
            )
            launch(f"out{n}", kind, send, keep)

        kept = step_with(
            attention_forward, lengths, core, normed, w_qkv, cosine, sine, fw, jnp.asarray(map_np), keep, streams,
            names=FORWARD_PLAN,
        )
        mixed = kept[3]
        mixed_other = partner(kept[6])

        earlier, features = [], []
        after = mixed
        backs = (jnp.asarray(back_high_np), jnp.asarray(back_low_np))
        groups = 2
        for call, (kind, names) in enumerate(BACKWARD_PLAN):
            if call == PROJ_AT:
                send, keep = step_with(
                    proj_grad_pieces, core, places[PROJ_PLAN[0]], mixed, mixed_other, g, after, parts, streams,
                    names=PROJ_PLAN[1],
                )
                launch("proj", PROJ_PLAN[0], send, keep)
                after = keep
            dq, dk, dv, feature, send, keep = step_with(
                attention_backward, core, places[kind], g, w_proj, kept, cosine, sine, backs,
                jnp.asarray(sums_np, bf16), normed, call, groups, earlier, after, parts, streams, names=names,
            )
            earlier = [dq, dk, dv]
            after = keep
            features.append(jnp.sum(feature, axis=0))
            launch(f"qkv{call}", kind, send, keep)

        def feature_shares(feature_list):
            own = jnp.concatenate(feature_list) / lax.dynamic_slice_in_dim(
                feature_weight, stream * (D // streams), D // streams
            )
            spread = jnp.concatenate([jnp.where(stream == s, own, 0.0) for s in range(streams)])
            table = jnp.zeros((parts,), jnp.int32).at[places["xy"]].set(jnp.arange(parts, dtype=jnp.int32))
            shares = spread.reshape(parts, 1, D // parts)
            hot = (table[:, None] == jnp.arange(parts)[None, :]).astype(f32)
            shares = jnp.sum(hot[:, :, None, None] * shares[None], axis=1)
            return jnp.pad(shares, ((0, 0), (0, 7), (0, 128 - D // parts)))

        shares = feature_shares(features)
        launch("feature", "xy", shares[parts // 2 :], shares[: parts // 2])
        for n, names in enumerate(AFTER_PLAN):
            jobs, lists = jobs_of(names)
            landed(lists, add_only(jobs, f"sums_{n}"))
        output, input_grad = tail(
            act, d_hidden, mixed, earlier, tokens, cotangent, valid, gain, weights, w_proj, w_qkv, parts, streams
        )
        n = 0
        while flight:
            jobs, lists = jobs_of([(name,) for name in flight])
            landed(lists, add_only(jobs, f"rest_{n}"))
            n += 1

        value = final["feature"]
        value = value + partner(value)
        share = D // (parts * streams)
        feature_grad = lax.dynamic_slice(value, (0, stream * share), (1, share)).reshape(share)

        share_rows = D // parts
        half = share_rows // streams

        def keep_rows(piece):
            return lax.dynamic_slice_in_dim(piece, stream * half, half)

        def send_rows(piece):
            return lax.dynamic_slice_in_dim(piece, (1 - stream) * half, half)

        columns = {}
        for name, piece in final.items():
            at = 0
            for part in name.split("+"):
                columns[part] = piece[:, at : at + widths[part]]
                at += widths[part]
        pieces = [columns[f"in{n}"] for n in range(len(FF_PLAN))]
        pieces += [columns[f"qkv{n}"] for n in range(len(BACKWARD_PLAN))] + [columns["proj"]]
        mine = jnp.concatenate([keep_rows(p) for p in pieces], 1)
        other = partner(jnp.concatenate([send_rows(p) for p in pieces], 1))
        a = jnp.where(stream == 0, mine, other)
        b = jnp.where(stream == 0, other, mine)
        unit = units // parts
        in_grad = jnp.concatenate(
            [src[:, unit * i : unit * (i + 1)] for i in range(parts) for src in (a, b)], 1
        )
        qa, qb = a[:, units : units + 3 * D // streams], b[:, units : units + 3 * D // streams]
        wide = groups * PAIR
        calls = HEADS // streams // 2 // groups

        def third(src, which):
            return [src[:, (3 * n + which) * wide : (3 * n + which + 1) * wide] for n in range(calls)]

        qkv_grad = jnp.concatenate(sum([third(qa, w) + third(qb, w) for w in range(3)], []), 1)
        proj_grad = jnp.concatenate([a[:, units + 3 * D // streams :], b[:, units + 3 * D // streams :]], 1)
        out_grad = jnp.concatenate([columns[f"out{n}"] for n in range(len(OUT_PLAN))], 1)
        first_row = (chip * streams + stream) * half
        w_in_rows = lax.dynamic_slice_in_dim(w_in, first_row, half).astype(f32)
        w_qkv_rows = lax.dynamic_slice_in_dim(w_qkv, first_row, half).astype(f32)
        gain_rows = lax.dynamic_slice_in_dim(norm_gain, first_row, half)
        gain_grad = (jnp.sum(w_in_rows * in_grad, 1) + jnp.sum(w_qkv_rows * qkv_grad, 1)) / gain_rows
        return output, input_grad, gain_grad, qkv_grad, proj_grad, in_grad, out_grad, feature_grad

    both = P(("dp", "stream"), None)
    return jax.shard_map(
        body,
        mesh=mesh,
        in_specs=(P("dp", None), P(), P(), P(), P(), P(), P(), P("dp"), P("dp", None)),
        out_specs=(
            P("dp", None), P("dp", None), P(("dp", "stream")), both, both, both, both, P(("dp", "stream")),
        ),
        check_vma=False,
    )
```

```python
import math
from functools import partial

import jax
import jax.numpy as jnp
import numpy as np
from jax import lax
from jax.experimental import pallas as pl
from jax.experimental.pallas import tpu as pltpu
from jax.sharding import PartitionSpec as P

D = 1024
HEADS = 16
HEAD = 64
FF = 4096
ROT = 16
SLOT = 2048
EPSILON = 1e-05

f32 = jnp.float32
bf16 = jnp.bfloat16
VMEM_LIMIT = 60 * 1024 * 1024
BLK = 256
PAIR = 2 * HEAD


def dot(a, b):
    return lax.dot_general(a, b, (((1,), (0,)), ((), ())), preferred_element_type=f32)


def dot_nt(a, b):
    return lax.dot_general(a, b, (((1,), (1,)), ((), ())), preferred_element_type=f32)


def dot_tn(a, b):
    return lax.dot_general(a, b, (((0,), (0,)), ((), ())), preferred_element_type=f32)


def erf_inverse(y):
    x = 0.0
    for _ in range(200):
        step = (math.erf(x) - y) / (2.0 / math.sqrt(math.pi) * math.exp(-x * x))
        x -= max(-0.5, min(0.5, step))
    return x


def feature_table():
    i = np.arange(HEAD, dtype=np.float64)
    cos_table = np.cos(np.pi * (2.0 * i[:, None] + 1.0) * i[None, :] / (2.0 * HEAD))
    weights = np.where(i == 0, math.sqrt(1.0 / HEAD), math.sqrt(2.0 / HEAD))
    quantiles = math.sqrt(2.0) * np.array([erf_inverse(2.0 * (m + 0.5) / HEAD - 1.0) for m in range(HEAD)])
    return cos_table * (weights * 0.5 * quantiles)[None, :]


def split_table(table):
    high = table.astype(np.float32).astype(bf16)
    low = (table - high.astype(np.float64)).astype(np.float32).astype(bf16)
    return high, low


def attention_tables():
    half = ROT // 2
    pos = np.arange(SLOT, dtype=np.float32)
    inverse = (np.float32(10000.0) ** (-2.0 * np.arange(half, dtype=np.float32) / np.float32(ROT))).astype(np.float32)
    angles = (pos[:, None] * inverse[None, :]).astype(np.float32).astype(np.float64)
    cos_one = np.ones((SLOT, HEAD))
    sin_one = np.zeros((SLOT, HEAD))
    cos_one[:, :half] = np.cos(angles)
    cos_one[:, half:ROT] = np.cos(angles)
    sin_one[:, :half] = np.sin(angles)
    sin_one[:, half:ROT] = -np.sin(angles)
    cosine = np.concatenate([cos_one, cos_one], 1).astype(np.float32)
    sine = np.concatenate([sin_one, sin_one], 1).astype(np.float32)
    one = feature_table()
    pair = np.zeros((PAIR, PAIR))
    pair[:HEAD, :HEAD] = one
    pair[HEAD:, HEAD:] = one
    swapped = pair.copy()
    for base in (0, HEAD):
        swapped[base : base + half] = pair[base + half : base + ROT]
        swapped[base + half : base + ROT] = pair[base : base + half]
    both = np.concatenate([pair, swapped], 0)
    high, low = split_table(both)
    forward = np.concatenate([high, low], 1)
    back_high, back_low = split_table(np.concatenate([pair.T, swapped.T], 1))
    back_high2 = np.concatenate([back_high, back_high], 0)
    return cosine, sine, forward, back_high2, back_low


def params(**extra):
    return pltpu.CompilerParams(vmem_limit_bytes=VMEM_LIMIT, **extra)


ANY = pl.BlockSpec(memory_space=pl.ANY)
MESH = pl.DeviceIdType.MESH


def idiv(a, b):
    return lax.div(a, jnp.int32(b))


def irem(a, b):
    return lax.rem(a, jnp.int32(b))


FIRST_BITS = {
    "xy": ("xzy", "yzx"), "zz": ("zxy", "zyx"), "xx": ("xyz", "yxz"), "xz": ("xzy", "zyx"),
    "yz": ("yzx", "zxy"), "xp": ("xyz", "yzx"), "zx": ("zyx", "xyz"), "zy": ("zxy", "yxz"),
}


class Comm:
    def __init__(self, parts, streams):
        self.parts, self.streams = parts, streams
        self.steps = parts.bit_length() - 1
        self.kernels = 0

    def orders(self, kind):
        result = []
        for s in range(2):
            order = [1 << b for b in range(self.steps)]
            if self.steps >= 3:
                order[:3] = [1 << "xyz".index(axis) for axis in FIRST_BITS[kind][s]]
            result.append(order)
        return result

    def place(self, kinds, share, which=None):
        chip, core = lax.axis_index("dp"), lax.axis_index("stream")
        kinds = [kinds] if isinstance(kinds, str) else list(kinds)
        total = jnp.int32(0)
        for b in range(self.steps):
            mask = 1 << b
            weight = jnp.int32(0)
            for n, kind in enumerate(kinds):
                values = [1 << (self.steps - 1 - order.index(mask)) for order in self.orders(kind)]
                value = values[0] + core * (values[1] - values[0])
                weight = value if n == 0 else jnp.where(which == n, value, weight)
            own = irem(idiv(chip, mask), 2)
            theirs = (share >> b) & 1 if isinstance(share, int) else irem(idiv(share, mask), 2)
            total = total + weight * irem(own + theirs, 2)
        return total

    def partner(self, kind, step):
        chip, core = lax.axis_index("dp"), lax.axis_index("stream")
        chips = []
        for order in self.orders(kind):
            mask = order[step]
            chips.append(chip + mask - 2 * mask * irem(idiv(chip, mask), 2))
        return (chips[0] + core * (chips[1] - chips[0]), core)

    def other_core(self):
        return (lax.axis_index("dp"), 1 - lax.axis_index("stream"))


class Flow:
    def __init__(self, name, kind, first, shape, array=None, start=None, sums=(), ready=0):
        self.name, self.kind, self.first, self.shape, self.array = name, kind, first, tuple(shape), array
        self.start, self.sums, self.ready = start, tuple(sums), ready
        self.half = shape[0] // 2
        self.slots = sum(self.half >> k for k in range(len(self.sums)))

    def out_shape(self):
        return (self.shape[0] >> len(self.sums),) + self.shape[1:]

    def scratch(self):
        half, (_, rows, columns) = self.half, self.shape
        kept = [pltpu.VMEM((half, rows, columns), f32)] if self.array is not None else []
        count = max(len(self.sums), 1)
        return kept + [
            pltpu.VMEM((max(self.slots, 1), rows, columns), f32),
            pltpu.SemaphoreType.DMA((count,)),
            pltpu.SemaphoreType.DMA((count,)),
            pltpu.SemaphoreType.DMA((2,)),
        ]

    def bind(self, comm, own, source, out, scratch):
        self.comm, self.source, self.out = comm, source, out
        scratch = list(scratch)
        self.own = scratch.pop(0) if self.array is not None else own
        self.recv, self.send_sem, self.recv_sem, self.local_sem = scratch

    def offset(self, k):
        return sum(self.half >> j for j in range(k))

    def remote(self, k):
        count = self.half >> k
        if k == 0 and self.array is not None:
            source = self.source.at[pl.ds(count, count)]
        else:
            source = self.own.at[pl.ds(count, count)]
        return pltpu.make_async_remote_copy(
            src_ref=source,
            dst_ref=self.recv.at[pl.ds(self.offset(k), count)],
            send_sem=self.send_sem.at[k],
            recv_sem=self.recv_sem.at[k],
            device_id=self.comm.partner(self.kind, self.first + k),
            device_id_type=MESH,
        )

    def load(self):
        return pltpu.make_async_copy(self.source.at[pl.ds(0, self.half)], self.own, self.local_sem.at[0])

    def store(self):
        return pltpu.make_async_copy(
            self.own.at[pl.ds(0, self.shape[0] >> len(self.sums))], self.out, self.local_sem.at[1]
        )

    def moves(self):
        return self.start is not None

    def events(self, step, last):
        if not self.moves():
            when = self.ready

            @pl.when((step == when) if not last else (step < 0))
            def _():
                self.store().start()

            return

        if not last:

            @pl.when(step == self.start)
            def _():
                self.remote(0).start()
                if self.array is not None:
                    self.load().start()

        for k, at in enumerate(self.sums):
            if (at < 0) != last:
                continue

            @pl.when(step >= 0 if last else step == at)
            def _(k=k):
                self.remote(k).wait_recv()
                if k == 0 and self.array is not None:
                    self.load().wait()
                count = self.half >> k
                base = self.offset(k)

                def add(p, carry):
                    self.own[p] = self.own[p] + self.recv[base + p]
                    return carry

                lax.fori_loop(0, count, add, 0)
                if k + 1 < len(self.sums):
                    self.remote(k + 1).start()
                else:
                    self.store().start()

    def finish(self):
        if self.moves():
            for k in range(len(self.sums)):
                self.remote(k).wait_send()
        self.store().wait()


def with_comm(
    comm, kernel, steps, in_specs, out_specs, out_shape, flows, operands, scratch_shapes=(), inner=(), exchange=False,
    name=None, **call,
):
    base_in, base_out, base_scratch = len(in_specs), len(out_specs), len(scratch_shapes)
    every = list(flows) + [flow for flow, _, _ in inner]
    flow_scratch = [flow.scratch() if flow.moves() or flow.array is not None else [pltpu.SemaphoreType.DMA((2,))] for flow in every]
    remote = any(flow.moves() for flow in every)

    def run(*refs):
        refs = list(refs)

        def take(count):
            taken = refs[:count]
            del refs[:count]
            return taken

        own_in, flow_in = take(base_in), take(len(flows))
        own_out, flow_out = take(base_out), take(len(every))
        own_scratch = take(base_scratch)
        for n, flow in enumerate(every):
            got = take(len(flow_scratch[n]))
            if n < len(flows):
                flow.bind(comm, None, flow_in[n], flow_out[n], got)
            else:
                _, index, at = inner[n - len(flows)]
                if not flow.moves():
                    got = [None, None, None] + got
                own = own_scratch[index] if at is None else own_scratch[index].at[at]
                flow.bind(comm, own, None, flow_out[n], got)
        step = pl.program_id(0)
        if remote or exchange:

            @pl.when(step == 0)
            def _():
                barrier = pltpu.get_barrier_semaphore()
                chip, core = lax.axis_index("dp"), lax.axis_index("stream")
                others = []
                if remote:
                    for b in range(comm.steps):
                        mask = 1 << b
                        others.append((chip + mask - 2 * mask * irem(idiv(chip, mask), 2), core))
                if exchange:
                    others.append(comm.other_core())
                for other in others:
                    pl.semaphore_signal(barrier, inc=1, device_id=other, device_id_type=MESH)
                pl.semaphore_wait(barrier, len(others))

        for flow in every:
            flow.events(step, False)
        kernel(*own_in, *own_out, *own_scratch)

        @pl.when(step == steps - 1)
        def _():
            for flow in every:
                if flow.moves():
                    flow.events(step, True)
                elif flow.ready >= steps:
                    flow.store().start()
            for flow in every:
                flow.finish()

    extra = {}
    if remote or exchange:
        extra = dict(collective_id=comm.kernels, has_side_effects=True)
        comm.kernels += 1
    results = pl.pallas_call(
        run,
        grid=(steps,),
        in_specs=list(in_specs) + [ANY] * len(flows),
        out_specs=list(out_specs) + [ANY] * len(every),
        out_shape=list(out_shape) + [jax.ShapeDtypeStruct(flow.out_shape(), f32) for flow in every],
        scratch_shapes=list(scratch_shapes) + sum(flow_scratch, []),
        compiler_params=params(**extra),
        name=name,
        **call,
    )(*operands, *[flow.array for flow in flows])
    results = list(results)
    return results[:base_out], dict(zip([flow.name for flow in every], results[base_out:]))


def unit_strips(comm, w_in_ref, w_out_ref, first, units, gathered):
    if gathered:
        first = first if isinstance(first, int) else pl.multiple_of(first, 128)
        return [(w_in_ref.at[:, pl.ds(first, units)], w_out_ref.at[pl.ds(first, units), :], 0, units)]
    unit = FF // (comm.parts * comm.streams)
    core = lax.axis_index("stream")
    strips = []
    for n in range(units // unit):
        start = (idiv(jnp.int32(first), unit) + n) * comm.streams + core
        start = pl.multiple_of(start * unit, unit)
        strips.append((w_in_ref.at[:, pl.ds(start, unit)], w_out_ref.at[pl.ds(start, unit), :], n * unit, unit))
    return strips


def gather_units(comm, w_in, w_out):
    parts, streams = comm.parts, comm.streams
    unit = FF // (parts * streams)
    if unit % 128 == 0:
        return w_in, w_out, False
    core = lax.axis_index("stream")
    a = lax.dynamic_index_in_dim(w_in.reshape(D, parts, streams, unit), core, 2, False)
    b = lax.dynamic_index_in_dim(w_out.reshape(parts, streams, unit, D), core, 1, False)
    return a.reshape(D, parts * unit), b.reshape(parts * unit, D), True


def gelu_parts(x):
    density = jnp.exp(x * x * -0.5)
    t = 1.0 / (1.0 + (0.3275911 / math.sqrt(2.0)) * jnp.abs(x))
    poly = 1.061405429 * t - 1.453152027
    poly = poly * t + 1.421413741
    poly = poly * t - 0.284496736
    poly = (poly * t + 0.254829592) * t
    tail = 0.5 * poly * density
    cdf = jnp.where(x >= 0, 1.0 - tail, tail)
    return x * cdf, cdf + x * density * (1.0 / math.sqrt(2.0 * math.pi))


TILE = 256
UNITS = 512
CHUNK_STEPS = 6
OUT_COLUMNS = 256


def front_kernel(
    comm, kinds, out_kinds, gathered,
    tok_hbm, cot_hbm, valid_ref, gain_ref, win_hbm, wout_hbm,
    normed_hbm, g_hbm, act_hbm, dh_hbm,
    normed, g, win, wout, h_a, h_b, d_a, d_b, act, d_hidden, in_own, out_own,
    tok_sem, cot_sem, in_sem, out_sem, normed_sem, g_sem, act_sem, dh_sem,
):
    step = pl.program_id(0)
    rows = normed.shape[0]
    chunks = act.shape[0]
    tile = 2 * TILE
    tiles = rows // tile
    chunk = idiv(step, CHUNK_STEPS)
    phase = irem(step, CHUNK_STEPS)
    working = chunk < chunks
    slot = irem(chunk, 2)

    def tile_rows(i):
        return pl.ds(pl.multiple_of(i * tile, tile), tile)

    def row_load(i, hbm, vmem, sem):
        return pltpu.make_async_copy(hbm.at[tile_rows(i), :], vmem.at[tile_rows(i), :], sem.at[i])

    def row_store(i, vmem, hbm, sem):
        return pltpu.make_async_copy(vmem.at[tile_rows(i), :], hbm.at[tile_rows(i), :], sem.at[i])

    def weight_loads(c):
        s = irem(jnp.int32(c), 2)
        loads = []
        for n, (a, b, at, size) in enumerate(unit_strips(comm, win_hbm, wout_hbm, c * UNITS, UNITS, gathered)):
            loads.append(pltpu.make_async_copy(a, win.at[s, :, pl.ds(at, size)], in_sem.at[s, n]))
            loads.append(pltpu.make_async_copy(b, wout.at[s, pl.ds(at, size), :], out_sem.at[s, n]))
        return loads

    def low_stores(c):
        columns = pl.ds(pl.multiple_of(c * UNITS, UNITS), UNITS)
        here = pl.ds(TILE, rows)
        return (
            pltpu.make_async_copy(act.at[c, here, :], act_hbm.at[:, columns], act_sem.at[c]),
            pltpu.make_async_copy(d_hidden.at[irem(c, 2), here, :], dh_hbm.at[:, columns], dh_sem.at[c]),
        )

    @pl.when(step == 0)
    def _():
        row_load(0, tok_hbm, normed, tok_sem).start()
        row_load(0, cot_hbm, g, cot_sem).start()
        for load in weight_loads(0):
            load.start()
        for i in range(1, tiles):
            row_load(i, tok_hbm, normed, tok_sem).start()
            row_load(i, cot_hbm, g, cot_sem).start()

    @pl.when(working & (chunk == 0) & (phase < tiles))
    def _():
        row_load(phase, tok_hbm, normed, tok_sem).wait()
        row_load(phase, cot_hbm, g, cot_sem).wait()
        here = tile_rows(phase)
        x = normed[here, :].astype(f32)
        centered = x - jnp.mean(x, axis=-1, keepdims=True)
        var = jnp.mean(centered * centered, axis=-1, keepdims=True)
        normed[here, :] = (centered * lax.rsqrt(var + EPSILON) * gain_ref[...]).astype(bf16)
        g[here, :] = (g[here, :].astype(f32) * valid_ref[here, :]).astype(bf16)
        row_store(phase, normed, normed_hbm, normed_sem).start()
        row_store(phase, g, g_hbm, g_sem).start()

    @pl.when(working & (phase == 0))
    def _():
        for load in weight_loads(chunk):
            load.wait()

    @pl.when((phase == 0) & (chunk + 1 < chunks))
    def _():
        for load in weight_loads(chunk + 1):
            load.start()

    def finish_tile(h, d, place):
        value, slope = gelu_parts(h[...])
        here = pl.ds(pl.multiple_of(place, TILE), TILE)
        act[chunk, here, :] = value.astype(bf16)
        d_hidden[slot, here, :] = (d[...] * slope).astype(bf16)

    @pl.when(working & (phase < tiles))
    def _():
        first = pl.multiple_of(phase * tile, tile)
        here_a, here_b = pl.ds(first, TILE), pl.ds(first + TILE, TILE)
        finish_tile(h_b, d_b, phase * tile)
        h_a[...] = dot(normed[here_a, :], win[slot])
        d_a[...] = dot_nt(g[here_a, :], wout[slot])
        finish_tile(h_a, d_a, phase * tile + TILE)
        h_b[...] = dot(normed[here_b, :], win[slot])
        d_b[...] = dot_nt(g[here_b, :], wout[slot])

    share_rows = D // comm.parts
    wide = D // 2
    for m in range(2):

        @pl.when(working & (phase == tiles + m))
        def _(m=m):
            if m == 0:
                finish_tile(h_b, d_b, rows)
                for copy in low_stores(chunk):
                    copy.start()
            made = dot_tn(normed[:, m * wide : (m + 1) * wide], d_hidden[slot, TILE : TILE + rows, :])
            for n in range(wide // share_rows):
                share = m * (wide // share_rows) + n
                in_own[chunk, comm.place(kinds, share, chunk)] = made[n * share_rows : (n + 1) * share_rows, :]
            if m == 1:
                low_stores(chunk)[1].wait()

    unit_rows = FF // comm.streams // comm.parts
    blocks = D // OUT_COLUMNS
    for block in range(blocks):

        @pl.when(step == chunks * CHUNK_STEPS + block)
        def _(block=block):
            right = g[:, block * OUT_COLUMNS : (block + 1) * OUT_COLUMNS]
            for c in range(chunks):
                made = dot_tn(act[c, TILE : TILE + rows, :], right)
                for n in range(UNITS // unit_rows):
                    share = c * (UNITS // unit_rows) + n
                    out_own[block, comm.place(out_kinds[block], share)] = made[n * unit_rows : (n + 1) * unit_rows, :]

    @pl.when(step == pl.num_programs(0) - 1)
    def _():
        for i in range(tiles):
            row_store(i, normed, normed_hbm, normed_sem).wait()
            row_store(i, g, g_hbm, g_sem).wait()
        for c in range(chunks):
            low_stores(jnp.int32(c))[0].wait()


def front(comm, tokens, cotangent, valid, gain, weights, plan):
    w_in, w_out, gathered = weights
    rows = tokens.shape[0]
    units = FF // comm.streams
    chunks, blocks = units // UNITS, D // OUT_COLUMNS
    tiles = rows // (2 * TILE)
    parts = comm.parts
    strips = 1 if gathered else UNITS // (units // parts)
    share_rows, unit_rows = D // parts, units // parts
    kinds = [KIND[f"in{c}"] for c in range(chunks)]
    out_kinds = [KIND[f"o{b}"] for b in range(blocks)]
    steps = chunks * CHUNK_STEPS + blocks
    inner = []
    for c in range(chunks):
        start, sums = plan.get(f"in{c}", (None, ()))
        shape = (parts, share_rows, UNITS)
        flow = Flow(f"in{c}", kinds[c], 0, shape, None, start, sums, (c + 1) * CHUNK_STEPS)
        inner.append((flow, 10, c))
    for b in range(blocks):
        start, sums = plan.get(f"o{b}", (None, ()))
        shape = (parts, unit_rows, OUT_COLUMNS)
        flow = Flow(f"o{b}", out_kinds[b], 0, shape, None, start, sums, chunks * CHUNK_STEPS + b + 1)
        inner.append((flow, 11, b))
    low = jax.ShapeDtypeStruct((rows, D), bf16)
    wide = jax.ShapeDtypeStruct((rows, units), bf16)
    return with_comm(
        comm,
        partial(front_kernel, comm, kinds, out_kinds, gathered),
        steps,
        [ANY, ANY, pl.BlockSpec((rows, 1), lambda i: (0, 0)), pl.BlockSpec((1, D), lambda i: (0, 0)), ANY, ANY],
        [ANY] * 4,
        [low, low, wide, wide],
        [],
        [tokens, cotangent, valid, gain, w_in, w_out],
        [
            pltpu.VMEM((rows, D), bf16),
            pltpu.VMEM((rows, D), bf16),
            pltpu.VMEM((2, D, UNITS), bf16),
            pltpu.VMEM((2, UNITS, D), bf16),
            pltpu.VMEM((TILE, UNITS), f32),
            pltpu.VMEM((TILE, UNITS), f32),
            pltpu.VMEM((TILE, UNITS), f32),
            pltpu.VMEM((TILE, UNITS), f32),
            pltpu.VMEM((chunks, rows + TILE, UNITS), bf16),
            pltpu.VMEM((2, rows + TILE, UNITS), bf16),
            pltpu.VMEM((chunks, parts, share_rows, UNITS), f32),
            pltpu.VMEM((blocks, parts, unit_rows, OUT_COLUMNS), f32),
            pltpu.SemaphoreType.DMA((tiles,)),
            pltpu.SemaphoreType.DMA((tiles,)),
            pltpu.SemaphoreType.DMA((2, strips)),
            pltpu.SemaphoreType.DMA((2, strips)),
            pltpu.SemaphoreType.DMA((tiles,)),
            pltpu.SemaphoreType.DMA((tiles,)),
            pltpu.SemaphoreType.DMA((chunks,)),
            pltpu.SemaphoreType.DMA((chunks,)),
        ],
        inner,
        name="front",
        cost_estimate=pl.CostEstimate(
            flops=8 * rows * D * units, bytes_accessed=12 * rows * D + 8 * units * D, transcendentals=rows * units
        ),
    )


def causal_mask(transposed):
    row = lax.broadcasted_iota(jnp.int32, (BLK, BLK), 0)
    col = lax.broadcasted_iota(jnp.int32, (BLK, BLK), 1)
    return col >= row if transposed else row >= col


def head_masks():
    lane = lax.broadcasted_iota(jnp.int32, (1, PAIR), 1)
    first = lane < HEAD
    m0 = jnp.where(first, 1.0, 0.0)
    return m0.astype(bf16), (1.0 - m0).astype(bf16)


def state_mask():
    row = lax.broadcasted_iota(jnp.int32, (PAIR, 2 * PAIR), 0)
    col = lax.broadcasted_iota(jnp.int32, (PAIR, 2 * PAIR), 1)
    return (row < HEAD) == (col < PAIR)


def forward_kernel(
    comm, groups, kind,
    normed_ref, wq_ref, wk_ref, wv_ref, cos_ref, sin_ref, fw_ref, map_ref, valid_ref, right_ref,
    q_ref, k_ref, v_ref, mix_ref, den_ref, state_ref,
    state, mixed_all, sent, arrived, proj_own, send_sem, recv_sem,
):
    step = pl.program_id(0)
    blocks = sent.shape[0]

    def to_partner(i):
        return pltpu.make_async_remote_copy(
            src_ref=sent.at[i],
            dst_ref=arrived.at[i],
            send_sem=send_sem.at[i],
            recv_sem=recv_sem.at[i],
            device_id=comm.other_core(),
            device_id_type=MESH,
        )

    @pl.when(step == 0)
    def _():
        state[...] = jnp.zeros_like(state)

    @pl.when(step < blocks)
    def _():
        rows = normed_ref[...]
        queries_all, keys_all, values_all = dot(rows, wq_ref[...]), dot(rows, wk_ref[...]), dot(rows, wv_ref[...])
        cosine, sine = cos_ref[...], sin_ref[...]
        valid = valid_ref[...]
        m0, m1 = head_masks()
        causal = causal_mask(False)
        keep_state = state_mask()
        first = lax.broadcasted_iota(jnp.int32, (BLK, PAIR), 1) < HEAD
        place = pl.ds(pl.multiple_of(step * BLK, BLK), BLK)
        for group in range(groups):
            here = slice(group * PAIR, (group + 1) * PAIR)
            queries, keys = queries_all[:, here], keys_all[:, here]
            turned = jnp.concatenate(
                [
                    jnp.concatenate([queries * cosine, queries * sine], 1),
                    jnp.concatenate([keys * cosine, keys * sine], 1),
                ],
                0,
            )
            high = turned.astype(bf16)
            low = (turned - high.astype(f32)).astype(bf16)
            main = dot(high, map_ref[...])
            exponent = main[:, :PAIR] + main[:, PAIR:] + dot(low, map_ref[:, :PAIR])
            phi = jnp.exp(exponent) * fw_ref[:, here]
            q = phi[:BLK].astype(bf16)
            k = (phi[BLK:] * valid).astype(bf16)
            v = values_all[:, here].astype(bf16)
            q_ref[:, here] = q
            k_ref[:, here] = k
            v_ref[:, here] = v
            v0, v1 = v * m0 + m1, v * m1 + m0
            s0 = jnp.where(causal, dot_nt(q * m0, k), 0.0).astype(bf16)
            s1 = jnp.where(causal, dot_nt(q * m1, k), 0.0).astype(bf16)
            before = jnp.where(keep_state, state[group], 0.0).astype(bf16)
            state_ref[group, 0] = before
            far = dot(q, before)
            o0 = dot(s0, v0) + far[:, :PAIR]
            o1 = dot(s1, v1) + far[:, PAIR:]
            numerator = jnp.where(first, o0, o1)
            denominator = pltpu.roll(jnp.where(first, o1, o0), HEAD, 1)
            mixed = (numerator / denominator).astype(bf16)
            mix_ref[:, here] = mixed
            mixed_all[place, here] = mixed
            sent[step, :, here] = mixed.astype(f32)
            den_ref[:, here] = denominator
            state[group] += dot_tn(k, jnp.concatenate([v0, v1], 1))
        to_partner(step).start()

    share_rows = D // comm.parts
    width = groups * PAIR
    core = lax.axis_index("stream")
    for side in range(2):

        @pl.when(step == blocks + side)
        def _(side=side):
            if side == 0:
                left = mixed_all[...]
                base = core * (width // share_rows)
            else:
                for i in range(blocks):
                    to_partner(i).wait_recv()
                left = arrived[...].reshape(blocks * BLK, width).astype(bf16)
                base = (1 - core) * (width // share_rows)
            made = dot_tn(left, right_ref[...])
            for n in range(width // share_rows):
                proj_own[comm.place(kind, base + n)] = made[n * share_rows : (n + 1) * share_rows, :]
            if side == 1:
                for i in range(blocks):
                    to_partner(i).wait_send()


def forward(comm, normed, g, w_qkv, cosine, sine, fw, table, valid, flows, plan):
    rows = normed.shape[0]
    streams, parts = comm.streams, comm.parts
    groups = HEADS // streams // 2
    width = groups * PAIR
    blocks = rows // BLK

    def at(i):
        return jnp.minimum(i, blocks - 1)

    row_spec = pl.BlockSpec((BLK, width), lambda i: (at(i), 0))
    table_spec = pl.BlockSpec((BLK, PAIR), lambda i: (at(i), 0))
    low = jax.ShapeDtypeStruct((rows, width), bf16)

    def weight_spec(which):
        return pl.BlockSpec((D, width), lambda i: (0, which * streams + lax.axis_index("stream")))

    start, sums = plan.get("pr", (None, ()))
    kind = KIND["pr"]
    columns = D // streams
    inner = [(Flow("pr", kind, 0, (parts, D // parts, columns), None, start, sums, blocks + 2), 4, None)]
    return with_comm(
        comm,
        partial(forward_kernel, comm, groups, kind),
        blocks + 2,
        [
            pl.BlockSpec((BLK, D), lambda i: (at(i), 0)),
            weight_spec(0),
            weight_spec(1),
            weight_spec(2),
            table_spec,
            table_spec,
            pl.BlockSpec((1, width), lambda i: (0, lax.axis_index("stream"))),
            pl.BlockSpec((2 * PAIR, 2 * PAIR), lambda i: (0, 0)),
            pl.BlockSpec((BLK, 1), lambda i: (at(i), 0)),
            pl.BlockSpec((rows, columns), lambda i: (0, lax.axis_index("stream"))),
        ],
        [row_spec, row_spec, row_spec, row_spec, row_spec,
         pl.BlockSpec((groups, 1, PAIR, 2 * PAIR), lambda i: (0, at(i), 0, 0))],
        [low, low, low, low, jax.ShapeDtypeStruct((rows, width), f32),
         jax.ShapeDtypeStruct((groups, blocks, PAIR, 2 * PAIR), bf16)],
        flows,
        [normed, w_qkv, w_qkv, w_qkv, cosine, sine, fw, table, valid, g],
        [
            pltpu.VMEM((groups, PAIR, 2 * PAIR), f32),
            pltpu.VMEM((rows, width), bf16),
            pltpu.VMEM((blocks, BLK, width), f32),
            pltpu.VMEM((blocks, BLK, width), f32),
            pltpu.VMEM((parts, D // parts, columns), f32),
            pltpu.SemaphoreType.DMA((blocks,)),
            pltpu.SemaphoreType.DMA((blocks,)),
        ],
        inner,
        exchange=True,
        name="attention_forward",
        cost_estimate=pl.CostEstimate(
            flops=groups * blocks * 2 * 65536 * 5000,
            bytes_accessed=rows * D * 2 + 3 * D * width * 2 + rows * width * 16,
            transcendentals=2 * rows * width,
        ),
    )


GROUPS = 2
BACK_STEPS = 2


def backward_kernel(
    comm, blocks, kinds, feature_kind,
    g_ref, wp_ref, q_ref, k_ref, v_ref, mix_ref, den_ref, state_ref, cos_ref, sin_ref, back_ref, back_low_ref,
    sums_ref, fw_ref, normed_hbm,
    dq_ref, dk_ref, dv_ref,
    later, d_all, normed, fg, qkv_own, feature_own, load_sem,
):
    step = pl.program_id(0)
    per = blocks + BACK_STEPS
    call, phase = idiv(step, per), irem(step, per)
    width = GROUPS * PAIR
    load = pltpu.make_async_copy(normed_hbm, normed, load_sem)

    @pl.when(step == 0)
    def _():
        load.start()
        feature_own[...] = jnp.zeros_like(feature_own)

    @pl.when(phase == 0)
    def _():
        later[...] = jnp.zeros_like(later)
        fg[...] = jnp.zeros_like(fg)

    @pl.when(phase < blocks)
    def _():
        m0, m1 = head_masks()
        first = lax.broadcasted_iota(jnp.int32, (BLK, PAIR), 1) < HEAD
        left = lax.broadcasted_iota(jnp.int32, (PAIR, PAIR), 1) < HEAD
        own = (lax.broadcasted_iota(jnp.int32, (PAIR, PAIR), 0) < HEAD) == left
        causal, flipped = causal_mask(False), causal_mask(True)
        keep_state = state_mask()
        cosine, sine = cos_ref[...], sin_ref[...]
        d_mixed_all = dot_nt(g_ref[...], wp_ref[...])
        place = pl.ds(pl.multiple_of((blocks - 1 - phase) * BLK, BLK), BLK)
        for group in range(GROUPS):
            here = slice(group * PAIR, (group + 1) * PAIR)
            numer = d_mixed_all[:, here] / den_ref[:, here]
            product = numer * mix_ref[:, here].astype(f32)
            p_high = product.astype(bf16)
            p_low = (product - p_high.astype(f32)).astype(bf16)
            sums = dot(jnp.concatenate([p_high, p_low], 1), sums_ref[...])
            d_o0 = jnp.where(first, numer, -sums).astype(bf16)
            d_o1 = jnp.where(first, -sums, numer).astype(bf16)
            low = numer.astype(bf16)
            dn0, dn1 = low * m0, low * m1
            q, k, v = q_ref[:, here], k_ref[:, here], v_ref[:, here]
            q0, q1 = q * m0, q * m1
            v0, v1 = v * m0 + m1, v * m1 + m0
            ds0 = jnp.where(causal, dot_nt(d_o0, v0), 0.0).astype(bf16)
            ds1 = jnp.where(causal, dot_nt(d_o1, v1), 0.0).astype(bf16)
            st0 = jnp.where(flipped, dot_nt(k, q0), 0.0).astype(bf16)
            st1 = jnp.where(flipped, dot_nt(k, q1), 0.0).astype(bf16)
            dst0 = jnp.where(flipped, dot_nt(v0, d_o0), 0.0).astype(bf16)
            dst1 = jnp.where(flipped, dot_nt(v1, d_o1), 0.0).astype(bf16)
            d_o = jnp.concatenate([d_o0, d_o1], 1)
            behind = later[group]
            after = jnp.where(keep_state, behind, 0.0).astype(bf16)
            after_v = jnp.where(own, jnp.where(left, behind[:, :PAIR], behind[:, PAIR:]), 0.0).astype(bf16)
            k0, k1 = k * m0, k * m1
            d_q = dot_nt(d_o, state_ref[group, 0]) + dot(ds0, k0) + dot(ds1, k1)
            d_k = dot_nt(jnp.concatenate([v0, v1], 1), after) + dot(dst0, q0) + dot(dst1, q1)
            d_v = dot(k, after_v) + dot(st0, dn0) + dot(st1, dn1)
            later[group] += dot_tn(q, d_o)
            e_q = d_q * q.astype(f32)
            e_k = d_k * k.astype(f32)
            both = jnp.concatenate([e_q, e_k], 0)
            fg[:, here] += jnp.sum((e_q + e_k).reshape(BLK // 8, 8, PAIR), axis=0)
            high = both.astype(bf16)
            lower = (both - high.astype(f32)).astype(bf16)
            turned = dot(jnp.concatenate([high, lower], 1), back_ref[...]) + dot(high, back_low_ref[...])
            dq = (turned[:BLK, :PAIR] * cosine + turned[:BLK, PAIR:] * sine).astype(bf16)
            dk = (turned[BLK:, :PAIR] * cosine + turned[BLK:, PAIR:] * sine).astype(bf16)
            dv = d_v.astype(bf16)
            dq_ref[:, here] = dq
            dk_ref[:, here] = dk
            dv_ref[:, here] = dv
            d_all[place, group * PAIR : (group + 1) * PAIR] = dq
            d_all[place, width + group * PAIR : width + (group + 1) * PAIR] = dk
            d_all[place, 2 * width + group * PAIR : 2 * width + (group + 1) * PAIR] = dv

    @pl.when(step == blocks)
    def _():
        load.wait()

    share_rows = D // comm.parts
    wide = D // BACK_STEPS
    for m in range(BACK_STEPS):

        @pl.when(phase == blocks + m)
        def _(m=m):
            made = dot_tn(normed[:, m * wide : (m + 1) * wide], d_all[...])
            for n in range(wide // share_rows):
                share = m * (wide // share_rows) + n
                qkv_own[call, comm.place(kinds, share, call)] = made[n * share_rows : (n + 1) * share_rows, :]
            if m == 0:
                total = jnp.sum(fg[...], axis=0, keepdims=True) / fw_ref[...]
                size = D // comm.parts
                core = lax.axis_index("stream")
                for n in range(width // size):
                    pair, inside = divmod(n * size, PAIR)
                    row = total[:, pair * PAIR : (pair + 1) * PAIR]
                    row = jnp.broadcast_to(row, (8, PAIR))
                    if inside:
                        row = pltpu.roll(row, PAIR - inside, 1)
                    share = core * (D // comm.streams // size) + call * (width // size) + n
                    feature_own[comm.place(feature_kind, share)] = row


def backward(comm, normed, g, w_proj, kept, cosine, sine, backs, sums, fw, flows, plan):
    q, k, v, mixed, den, states = kept
    rows = g.shape[0]
    streams, parts = comm.streams, comm.parts
    calls = HEADS // streams // 2 // GROUPS
    blocks = rows // BLK
    per = blocks + BACK_STEPS
    width = GROUPS * PAIR

    def at(i):
        return jnp.maximum(blocks - 1 - irem(i, per), 0)

    def call(i):
        return idiv(i, per)

    row_spec = pl.BlockSpec((BLK, width), lambda i: (at(i), call(i)))
    table_spec = pl.BlockSpec((BLK, PAIR), lambda i: (at(i), 0))
    low = jax.ShapeDtypeStruct((rows, calls * width), bf16)
    inner = []
    for c in range(calls):
        start, when = plan.get(f"q{c}", (None, ()))
        shape = (parts, D // parts, 3 * width)
        inner.append((Flow(f"q{c}", KIND[f"q{c}"], 0, shape, None, start, when, (c + 1) * per), 4, c))
    inner.append((Flow("feature", KIND["feature"], 0, (parts, 8, PAIR), None, None, (), calls * per), 5, None))
    return with_comm(
        comm,
        partial(backward_kernel, comm, blocks, [KIND[f"q{c}"] for c in range(calls)], KIND["feature"]),
        calls * per,
        [
            pl.BlockSpec((BLK, D), lambda i: (at(i), 0)),
            pl.BlockSpec((width, D), lambda i: (lax.axis_index("stream") * calls + call(i), 0)),
            row_spec,
            row_spec,
            row_spec,
            row_spec,
            row_spec,
            pl.BlockSpec((GROUPS, 1, PAIR, 2 * PAIR), lambda i: (call(i), at(i), 0, 0)),
            table_spec,
            table_spec,
            pl.BlockSpec((2 * PAIR, 2 * PAIR), lambda i: (0, 0)),
            pl.BlockSpec((PAIR, 2 * PAIR), lambda i: (0, 0)),
            pl.BlockSpec((2 * PAIR, PAIR), lambda i: (0, 0)),
            pl.BlockSpec((1, width), lambda i: (0, lax.axis_index("stream") * calls + call(i))),
            ANY,
        ],
        [row_spec, row_spec, row_spec],
        [low, low, low],
        flows,
        [g, w_proj, q, k, v, mixed, den, states, cosine, sine, *backs, sums, fw, normed],
        [
            pltpu.VMEM((GROUPS, PAIR, 2 * PAIR), f32),
            pltpu.VMEM((rows, 3 * width), bf16),
            pltpu.VMEM((rows, D), bf16),
            pltpu.VMEM((8, width), f32),
            pltpu.VMEM((calls, parts, D // parts, 3 * width), f32),
            pltpu.VMEM((parts, 8, PAIR), f32),
            pltpu.SemaphoreType.DMA,
        ],
        inner,
        name="attention_backward",
        cost_estimate=pl.CostEstimate(
            flops=2 * 65536 * GROUPS * calls * (blocks * 6500 + 16384),
            bytes_accessed=2 * (2 * rows * D + width * D + rows * width * 24),
            transcendentals=0,
        ),
    )


def tail_kernel(
    comm, tiles, gathered,
    act_ref, dh_ref, mix_ref, dq_ref, dk_ref, dv_ref, tok_ref, cot_ref, valid_ref, gain_ref,
    wproj_ref, wq_ref, wk_ref, wv_ref, win_hbm, wout_hbm,
    out_ref, grad_ref,
    win, wout, mine, arrived, in_sem, out_sem, send_sem, recv_sem,
):
    step = pl.program_id(0)
    units = win.shape[1]
    strips = unit_strips(comm, win_hbm, wout_hbm, 0, units, gathered)
    loads = []
    for n, (a, b, at, size) in enumerate(strips):
        loads.append(pltpu.make_async_copy(a, win.at[:, pl.ds(at, size)], in_sem.at[n]))
        loads.append(pltpu.make_async_copy(b, wout.at[pl.ds(at, size), :], out_sem.at[n]))

    def send(i):
        return pltpu.make_async_remote_copy(
            src_ref=mine.at[irem(i, 2)],
            dst_ref=arrived.at[i],
            send_sem=send_sem.at[i],
            recv_sem=recv_sem.at[i],
            device_id=comm.other_core(),
            device_id_type=MESH,
        )

    @pl.when(step == 0)
    def _():
        for load in loads:
            load.start()
        for load in loads:
            load.wait()

    @pl.when((step >= 2) & (step < tiles))
    def _():
        send(step - 2).wait_send()

    @pl.when(step < tiles)
    def _():
        slot = irem(step, 2)
        mine[slot, 0] = dot(act_ref[...], wout[...]) + dot(mix_ref[...], wproj_ref[...])
        d_normed = dot_nt(dh_ref[...], win[...]) + dot_nt(dq_ref[...], wq_ref[...])
        d_normed += dot_nt(dk_ref[...], wk_ref[...]) + dot_nt(dv_ref[...], wv_ref[...])
        mine[slot, 1] = d_normed
        send(step).start()

    @pl.when(step >= 1)
    def _():
        send(step - 1).wait_recv()
        slot = irem(step + 1, 2)
        x = tok_ref[...].astype(f32)
        centered = x - jnp.mean(x, axis=-1, keepdims=True)
        var = jnp.mean(centered * centered, axis=-1, keepdims=True)
        inv_std = lax.rsqrt(var + EPSILON)
        unit = centered * inv_std
        out_ref[...] = (x + (mine[slot, 0] + arrived[step - 1, 0]) * valid_ref[...]).astype(bf16)
        scaled = (mine[slot, 1] + arrived[step - 1, 1]) * gain_ref[...]
        mean = jnp.mean(scaled, axis=-1, keepdims=True)
        cross = jnp.mean(scaled * unit, axis=-1, keepdims=True)
        grad_ref[...] = (cot_ref[...].astype(f32) + inv_std * (scaled - mean - unit * cross)).astype(bf16)

    @pl.when(step == tiles)
    def _():
        send(tiles - 2).wait_send()
        send(tiles - 1).wait_send()


def tail(comm, active, d_hidden, mixed, d_qkv, tokens, cotangent, valid, gain, weights, w_proj, w_qkv, flows):
    w_in, w_out, gathered = weights
    rows, units = active.shape
    width = mixed.shape[1]
    tiles = rows // TILE
    strips = 1 if gathered else comm.parts
    streams = comm.streams

    def now(i):
        return (jnp.minimum(i, tiles - 1), 0)

    def before(i):
        return (jnp.maximum(i - 1, 0), 0)

    def weight(which):
        return pl.BlockSpec((D, width), lambda i: (0, which * streams + lax.axis_index("stream")))

    shape = jax.ShapeDtypeStruct((rows, D), bf16)
    return with_comm(
        comm,
        partial(tail_kernel, comm, tiles, gathered),
        tiles + 1,
        [
            pl.BlockSpec((TILE, units), now),
            pl.BlockSpec((TILE, units), now),
            pl.BlockSpec((TILE, width), now),
            pl.BlockSpec((TILE, width), now),
            pl.BlockSpec((TILE, width), now),
            pl.BlockSpec((TILE, width), now),
            pl.BlockSpec((TILE, D), before),
            pl.BlockSpec((TILE, D), before),
            pl.BlockSpec((TILE, 1), before),
            pl.BlockSpec((1, D), lambda i: (0, 0)),
            pl.BlockSpec((width, D), lambda i: (lax.axis_index("stream"), 0)),
            weight(0),
            weight(1),
            weight(2),
            ANY,
            ANY,
        ],
        [pl.BlockSpec((TILE, D), before), pl.BlockSpec((TILE, D), before)],
        [shape, shape],
        flows,
        [active, d_hidden, mixed, *d_qkv, tokens, cotangent, valid, gain, w_proj, w_qkv, w_qkv, w_qkv, w_in, w_out],
        [
            pltpu.VMEM((D, units), bf16),
            pltpu.VMEM((units, D), bf16),
            pltpu.VMEM((2, 2, TILE, D), f32),
            pltpu.VMEM((tiles, 2, TILE, D), f32),
            pltpu.SemaphoreType.DMA((strips,)),
            pltpu.SemaphoreType.DMA((strips,)),
            pltpu.SemaphoreType.DMA((tiles,)),
            pltpu.SemaphoreType.DMA((tiles,)),
        ],
        exchange=True,
        name="tail",
        cost_estimate=pl.CostEstimate(
            flops=2 * rows * D * (2 * units + 4 * width),
            bytes_accessed=2 * (rows + D) * (2 * units + 4 * width) + 8 * rows * D,
            transcendentals=0,
        ),
    )


KIND = {
    "in0": "xp", "in1": "zx", "in2": "yz", "in3": "zx", "o0": "zy", "o1": "xx", "o2": "xp", "o3": "zz",
    "pr": "xp", "q0": "xp", "q1": "xx", "feature": "xy",
}
FRONT = {"in0": (6, (13, 20, 25, 27)), "in1": (12, (23,)), "in2": (18, (-1,))}
FORWARD = {"in1": (0, (7, 9)), "in2": (0, (5, 8)), "in3": (0, (9,)), "o0": (0, (9,)), "o1": (0, (9,))}
BACKWARD = {
    "in1": (0, (5,)), "in2": (0, (5,)), "in3": (0, (6, 11, 16)), "o0": (0, (6, 11, 16)), "o2": (0, (10, 19)),
    "o3": (4, (19,)), "pr": (8, (15, 19)), "q0": (14, (19,)),
}
TAIL = {
    "o1": (0, (4, 8, -1)), "o2": (0, (3, 7)), "pr": (0, (3, 7)), "q0": (0, (7, -1)), "q1": (3, (8, -1)),
    "feature": (0, (1, 3, 5, 7)),
}


def solution(mesh):
    comm = Comm(mesh.shape["dp"], mesh.shape["stream"])
    parts, streams = comm.parts, comm.streams
    cosine_np, sine_np, map_np, back_high_np, back_low_np = attention_tables()
    sums_np = np.zeros((2 * PAIR, PAIR), np.float32)
    for base in (0, PAIR):
        sums_np[base : base + HEAD, HEAD] = 1.0
        sums_np[base + HEAD : base + PAIR, 0] = 1.0

    def partner(value):
        pairs = []
        for d in range(parts):
            for s in range(streams):
                pairs.append((d * streams + s, d * streams + (s ^ 1)))
        return lax.ppermute(value, ("dp", "stream"), pairs)

    def body(tokens, norm_gain, w_qkv, w_proj, w_in, w_out, feature_weight, lengths, cotangent):
        comm.kernels = 0
        rows = tokens.shape[0]
        chip = lax.axis_index("dp")
        stream = lax.axis_index("stream")
        gain = norm_gain.reshape(1, D)
        fw = feature_weight.reshape(1, D)
        cosine, sine = jnp.asarray(cosine_np), jnp.asarray(sine_np)
        valid = (jnp.arange(rows) < lengths[0]).astype(f32).reshape(rows, 1)
        weights = gather_units(comm, w_in, w_out)
        units = FF // streams
        done = {}

        def flows_of(plan):
            flows = []
            for name, (start, sums) in plan.items():
                if name in done and done[name][0] < comm.steps:
                    taken, array = done[name]
                    sums = sums[: comm.steps - taken]
                    flows.append(Flow(name, KIND[name], taken, array.shape, array, start, sums))
            return flows

        def landed(shares, plan):
            for name, array in shares.items():
                taken = done[name][0] if name in done else 0
                done[name] = (taken + (len(plan[name][1][: comm.steps - taken]) if name in plan else 0), array)

        (normed, g, act, d_hidden), shares = front(comm, tokens, cotangent, valid, gain, weights, FRONT)
        landed(shares, FRONT)
        kept, shares = forward(
            comm, normed, g, w_qkv, cosine, sine, fw, jnp.asarray(map_np), valid, flows_of(FORWARD), FORWARD
        )
        landed(shares, FORWARD)
        backs = (jnp.asarray(back_high_np), jnp.asarray(back_low_np))
        d_qkv, shares = backward(
            comm, normed, g, w_proj, kept, cosine, sine, backs, jnp.asarray(sums_np, bf16), fw,
            flows_of(BACKWARD), BACKWARD,
        )
        landed(shares, BACKWARD)
        (output, input_grad), shares = tail(
            comm, act, d_hidden, kept[3], d_qkv, tokens, cotangent, valid, gain, weights, w_proj, w_qkv,
            flows_of(TAIL),
        )
        landed(shares, TAIL)
        left = {}
        for name, (taken, _) in done.items():
            if taken < comm.steps:
                left[name] = (0, tuple(range(1, comm.steps - taken + 1)))
        if left:
            length = 1 + max(len(sums) for _, sums in left.values())
            _, shares = with_comm(
                comm, lambda *refs: None, length, [], [], [], flows_of(left), [], name="rest"
            )
            landed(shares, left)
        final = {name: array[0] for name, (_, array) in done.items()}

        value = final["feature"]
        value = value + partner(value)
        share = D // (parts * streams)
        feature_grad = lax.dynamic_slice(value, (0, stream * share), (1, share)).reshape(share)

        half = D // parts // streams
        names = [f"in{c}" for c in range(units // UNITS)]
        names += [f"q{c}" for c in range(HEADS // streams // 2 // GROUPS)] + ["pr"]
        mine = jnp.concatenate([lax.dynamic_slice_in_dim(final[n], stream * half, half) for n in names], 1)
        other = partner(
            jnp.concatenate([lax.dynamic_slice_in_dim(final[n], (1 - stream) * half, half) for n in names], 1)
        )
        a = jnp.where(stream == 0, mine, other)
        b = jnp.where(stream == 0, other, mine)
        unit = units // parts
        in_grad = jnp.concatenate(
            [src[:, unit * i : unit * (i + 1)] for i in range(parts) for src in (a, b)], 1
        )
        qa, qb = a[:, units : units + 3 * D // streams], b[:, units : units + 3 * D // streams]
        wide = GROUPS * PAIR
        calls = HEADS // streams // 2 // GROUPS

        def third(src, which):
            return [src[:, (3 * n + which) * wide : (3 * n + which + 1) * wide] for n in range(calls)]

        qkv_grad = jnp.concatenate(sum([third(qa, w) + third(qb, w) for w in range(3)], []), 1)
        proj_grad = jnp.concatenate([a[:, units + 3 * D // streams :], b[:, units + 3 * D // streams :]], 1)
        out_grad = jnp.concatenate([final[f"o{n}"] for n in range(D // OUT_COLUMNS)], 1)
        first_row = (chip * streams + stream) * half
        w_in_rows = lax.dynamic_slice_in_dim(w_in, first_row, half).astype(f32)
        w_qkv_rows = lax.dynamic_slice_in_dim(w_qkv, first_row, half).astype(f32)
        gain_rows = lax.dynamic_slice_in_dim(norm_gain, first_row, half)
        gain_grad = (jnp.sum(w_in_rows * in_grad, 1) + jnp.sum(w_qkv_rows * qkv_grad, 1)) / gain_rows
        return output, input_grad, gain_grad, qkv_grad, proj_grad, in_grad, out_grad, feature_grad

    both = P(("dp", "stream"), None)
    return jax.shard_map(
        body,
        mesh=mesh,
        in_specs=(P("dp", None), P(), P(), P(), P(), P(), P(), P("dp"), P("dp", None)),
        out_specs=(
            P("dp", None), P("dp", None), P(("dp", "stream")), both, both, both, both, P(("dp", "stream")),
        ),
        check_vma=False,
    )
```

```python
import math
from functools import partial

import jax
import jax.numpy as jnp
import numpy as np
from jax import lax
from jax.experimental import pallas as pl
from jax.experimental.pallas import tpu as pltpu
from jax.sharding import PartitionSpec as P

D = 1024
HEADS = 16
HEAD = 64
FF = 4096
ROT = 16
SLOT = 2048
EPSILON = 1e-05

f32 = jnp.float32
bf16 = jnp.bfloat16
VMEM_LIMIT = 60 * 1024 * 1024
BLK = 256
PAIR = 2 * HEAD


def dot(a, b):
    return lax.dot_general(a, b, (((1,), (0,)), ((), ())), preferred_element_type=f32)


def dot_nt(a, b):
    return lax.dot_general(a, b, (((1,), (1,)), ((), ())), preferred_element_type=f32)


def dot_tn(a, b):
    return lax.dot_general(a, b, (((0,), (0,)), ((), ())), preferred_element_type=f32)


def erf_inverse(y):
    x = 0.0
    for _ in range(200):
        step = (math.erf(x) - y) / (2.0 / math.sqrt(math.pi) * math.exp(-x * x))
        x -= max(-0.5, min(0.5, step))
    return x


def feature_table():
    i = np.arange(HEAD, dtype=np.float64)
    cos_table = np.cos(np.pi * (2.0 * i[:, None] + 1.0) * i[None, :] / (2.0 * HEAD))
    weights = np.where(i == 0, math.sqrt(1.0 / HEAD), math.sqrt(2.0 / HEAD))
    quantiles = math.sqrt(2.0) * np.array([erf_inverse(2.0 * (m + 0.5) / HEAD - 1.0) for m in range(HEAD)])
    return cos_table * (weights * 0.5 * quantiles)[None, :]


def split_table(table):
    high = table.astype(np.float32).astype(bf16)
    low = (table - high.astype(np.float64)).astype(np.float32).astype(bf16)
    return high, low


def attention_tables():
    half = ROT // 2
    pos = np.arange(SLOT, dtype=np.float32)
    inverse = (np.float32(10000.0) ** (-2.0 * np.arange(half, dtype=np.float32) / np.float32(ROT))).astype(np.float32)
    angles = (pos[:, None] * inverse[None, :]).astype(np.float32).astype(np.float64)
    cos_one = np.ones((SLOT, HEAD))
    sin_one = np.zeros((SLOT, HEAD))
    cos_one[:, :half] = np.cos(angles)
    cos_one[:, half:ROT] = np.cos(angles)
    sin_one[:, :half] = np.sin(angles)
    sin_one[:, half:ROT] = -np.sin(angles)
    cosine = np.concatenate([cos_one, cos_one], 1).astype(np.float32)
    sine = np.concatenate([sin_one, sin_one], 1).astype(np.float32)
    one = feature_table()
    pair = np.zeros((PAIR, PAIR))
    pair[:HEAD, :HEAD] = one
    pair[HEAD:, HEAD:] = one
    swapped = pair.copy()
    for base in (0, HEAD):
        swapped[base : base + half] = pair[base + half : base + ROT]
        swapped[base + half : base + ROT] = pair[base : base + half]
    both = np.concatenate([pair, swapped], 0)
    high, low = split_table(both)
    forward = np.concatenate([high, low], 1)
    back_high, back_low = split_table(np.concatenate([pair.T, swapped.T], 1))
    back_high2 = np.concatenate([back_high, back_high], 0)
    return cosine, sine, forward, back_high2, back_low


def params(**extra):
    return pltpu.CompilerParams(vmem_limit_bytes=VMEM_LIMIT, **extra)


ANY = pl.BlockSpec(memory_space=pl.ANY)
MESH = pl.DeviceIdType.MESH


def idiv(a, b):
    return lax.div(a, jnp.int32(b))


def irem(a, b):
    return lax.rem(a, jnp.int32(b))


FIRST_BITS = {
    "xy": ("xzy", "yzx"), "zz": ("zxy", "zyx"), "xx": ("xyz", "yxz"), "xz": ("xzy", "zyx"),
    "yz": ("yzx", "zxy"), "xp": ("xyz", "yzx"), "zx": ("zyx", "xyz"), "zy": ("zxy", "yxz"),
}


class Comm:
    def __init__(self, parts, streams):
        self.parts, self.streams = parts, streams
        self.steps = parts.bit_length() - 1
        self.kernels = 0

    def orders(self, kind):
        result = []
        for s in range(2):
            order = [1 << b for b in range(self.steps)]
            if self.steps >= 3:
                order[:3] = [1 << "xyz".index(axis) for axis in FIRST_BITS[kind][s]]
            result.append(order)
        return result

    def place(self, kinds, share, which=None):
        chip, core = lax.axis_index("dp"), lax.axis_index("stream")
        kinds = [kinds] if isinstance(kinds, str) else list(kinds)
        total = jnp.int32(0)
        for b in range(self.steps):
            mask = 1 << b
            weight = jnp.int32(0)
            for n, kind in enumerate(kinds):
                values = [1 << (self.steps - 1 - order.index(mask)) for order in self.orders(kind)]
                value = values[0] + core * (values[1] - values[0])
                weight = value if n == 0 else jnp.where(which == n, value, weight)
            own = irem(idiv(chip, mask), 2)
            theirs = (share >> b) & 1 if isinstance(share, int) else irem(idiv(share, mask), 2)
            total = total + weight * irem(own + theirs, 2)
        return total

    def partner(self, kind, step):
        chip, core = lax.axis_index("dp"), lax.axis_index("stream")
        chips = []
        for order in self.orders(kind):
            mask = order[step]
            chips.append(chip + mask - 2 * mask * irem(idiv(chip, mask), 2))
        return (chips[0] + core * (chips[1] - chips[0]), core)

    def other_core(self):
        return (lax.axis_index("dp"), 1 - lax.axis_index("stream"))


class Flow:
    def __init__(self, name, kind, first, shape, array=None, start=None, sums=(), ready=0):
        self.name, self.kind, self.first, self.shape, self.array = name, kind, first, tuple(shape), array
        self.start, self.sums, self.ready = start, tuple(sums), ready
        self.half = shape[0] // 2
        self.slots = sum(self.half >> k for k in range(len(self.sums)))

    def out_shape(self):
        return (self.shape[0] >> len(self.sums),) + self.shape[1:]

    def scratch(self):
        half, (_, rows, columns) = self.half, self.shape
        kept = [pltpu.VMEM((2 * half, rows, columns), f32)] if self.array is not None else []
        count = max(len(self.sums), 1)
        return kept + [
            pltpu.VMEM((max(self.slots, 1), rows, columns), f32),
            pltpu.SemaphoreType.DMA((count,)),
            pltpu.SemaphoreType.DMA((count,)),
            pltpu.SemaphoreType.DMA((2,)),
        ]

    def bind(self, comm, own, source, out, scratch):
        self.comm, self.source, self.out = comm, source, out
        scratch = list(scratch)
        self.own = scratch.pop(0) if self.array is not None else own
        self.recv, self.send_sem, self.recv_sem, self.local_sem = scratch

    def offset(self, k):
        return sum(self.half >> j for j in range(k))

    def remote(self, k):
        count = self.half >> k
        return pltpu.make_async_remote_copy(
            src_ref=self.own.at[pl.ds(count, count)],
            dst_ref=self.recv.at[pl.ds(self.offset(k), count)],
            send_sem=self.send_sem.at[k],
            recv_sem=self.recv_sem.at[k],
            device_id=self.comm.partner(self.kind, self.first + k),
            device_id_type=MESH,
        )

    def load(self):
        return pltpu.make_async_copy(self.source, self.own, self.local_sem.at[0])

    def store(self):
        return pltpu.make_async_copy(
            self.own.at[pl.ds(0, self.shape[0] >> len(self.sums))], self.out, self.local_sem.at[1]
        )

    def moves(self):
        return self.start is not None

    def events(self, step, last):
        if not self.moves():
            when = self.ready

            @pl.when((step == when) if not last else (step < 0))
            def _():
                self.store().start()

            return

        if not last:

            if self.array is not None and self.start > 0:

                @pl.when(step == self.start - 1)
                def _():
                    self.load().start()

            @pl.when(step == self.start)
            def _():
                if self.array is not None:
                    self.load().wait()
                self.remote(0).start()

        for k, at in enumerate(self.sums):
            if (at < 0) != last:
                continue

            @pl.when(step >= 0 if last else step == at)
            def _(k=k):
                self.remote(k).wait_recv()
                count = self.half >> k
                base = self.offset(k)

                def add(p, carry):
                    self.own[p] = self.own[p] + self.recv[base + p]
                    return carry

                lax.fori_loop(0, count, add, 0)
                if k + 1 < len(self.sums):
                    self.remote(k + 1).start()
                else:
                    self.store().start()

    def finish(self):
        if self.moves():
            for k in range(len(self.sums)):
                self.remote(k).wait_send()
        self.store().wait()


def with_comm(
    comm, kernel, steps, in_specs, out_specs, out_shape, flows, operands, scratch_shapes=(), inner=(), exchange=False,
    name=None, **call,
):
    base_in, base_out, base_scratch = len(in_specs), len(out_specs), len(scratch_shapes)
    every = list(flows) + [flow for flow, _, _ in inner]
    flow_scratch = [flow.scratch() if flow.moves() or flow.array is not None else [pltpu.SemaphoreType.DMA((2,))] for flow in every]
    remote = any(flow.moves() for flow in every)

    def run(*refs):
        refs = list(refs)

        def take(count):
            taken = refs[:count]
            del refs[:count]
            return taken

        own_in, flow_in = take(base_in), take(len(flows))
        own_out, flow_out = take(base_out), take(len(every))
        own_scratch = take(base_scratch)
        for n, flow in enumerate(every):
            got = take(len(flow_scratch[n]))
            if n < len(flows):
                flow.bind(comm, None, flow_in[n], flow_out[n], got)
            else:
                _, index, at = inner[n - len(flows)]
                if not flow.moves():
                    got = [None, None, None] + got
                own = own_scratch[index] if at is None else own_scratch[index].at[at]
                flow.bind(comm, own, None, flow_out[n], got)
        step = pl.program_id(0)
        if remote or exchange:

            @pl.when(step == 0)
            def _():
                for flow in every:
                    if flow.array is not None and flow.start == 0:
                        flow.load().start()
                barrier = pltpu.get_barrier_semaphore()
                chip, core = lax.axis_index("dp"), lax.axis_index("stream")
                others = []
                if remote:
                    for b in range(comm.steps):
                        mask = 1 << b
                        others.append((chip + mask - 2 * mask * irem(idiv(chip, mask), 2), core))
                if exchange:
                    others.append(comm.other_core())
                for other in others:
                    pl.semaphore_signal(barrier, inc=1, device_id=other, device_id_type=MESH)
                pl.semaphore_wait(barrier, len(others))

        for flow in every:
            flow.events(step, False)
        kernel(*own_in, *own_out, *own_scratch)

        @pl.when(step == steps - 1)
        def _():
            for flow in every:
                if flow.moves():
                    flow.events(step, True)
                elif flow.ready >= steps:
                    flow.store().start()
            for flow in every:
                flow.finish()

    extra = {}
    if remote or exchange:
        extra = dict(collective_id=comm.kernels, has_side_effects=True)
        comm.kernels += 1
    results = pl.pallas_call(
        run,
        grid=(steps,),
        in_specs=list(in_specs) + [ANY] * len(flows),
        out_specs=list(out_specs) + [ANY] * len(every),
        out_shape=list(out_shape) + [jax.ShapeDtypeStruct(flow.out_shape(), f32) for flow in every],
        scratch_shapes=list(scratch_shapes) + sum(flow_scratch, []),
        compiler_params=params(**extra),
        name=name,
        **call,
    )(*operands, *[flow.array for flow in flows])
    results = list(results)
    return results[:base_out], dict(zip([flow.name for flow in every], results[base_out:]))


def unit_strips(comm, w_in_ref, w_out_ref, first, units, gathered):
    if gathered:
        first = first if isinstance(first, int) else pl.multiple_of(first, 128)
        return [(w_in_ref.at[:, pl.ds(first, units)], w_out_ref.at[pl.ds(first, units), :], 0, units)]
    unit = FF // (comm.parts * comm.streams)
    core = lax.axis_index("stream")
    strips = []
    for n in range(units // unit):
        start = (idiv(jnp.int32(first), unit) + n) * comm.streams + core
        start = pl.multiple_of(start * unit, unit)
        strips.append((w_in_ref.at[:, pl.ds(start, unit)], w_out_ref.at[pl.ds(start, unit), :], n * unit, unit))
    return strips


def gather_units(comm, w_in, w_out):
    parts, streams = comm.parts, comm.streams
    unit = FF // (parts * streams)
    if unit % 128 == 0:
        return w_in, w_out, False
    core = lax.axis_index("stream")
    a = lax.dynamic_index_in_dim(w_in.reshape(D, parts, streams, unit), core, 2, False)
    b = lax.dynamic_index_in_dim(w_out.reshape(parts, streams, unit, D), core, 1, False)
    return a.reshape(D, parts * unit), b.reshape(parts * unit, D), True


def gelu_parts(x):
    cdf = 0.5 + 0.5 * lax.erf(x * math.sqrt(0.5))
    return x * cdf, cdf + x * jnp.exp(x * x * -0.5) * (1.0 / math.sqrt(2.0 * math.pi))


TILE = 256
UNITS = 512
FRONT_TILE = 1024
CHUNK_STEPS = SLOT // FRONT_TILE + 1
OUT_COLUMNS = 256


def front_kernel(
    comm, kinds, out_kinds, gathered,
    tok_hbm, cot_hbm, valid_ref, gain_ref, win_hbm, wout_hbm,
    normed_hbm, g_hbm, act_hbm, dh_hbm,
    normed, g, win, wout, act, d_hidden, in_own, out_own,
    tok_sem, cot_sem, in_sem, out_sem, normed_sem, g_sem, act_sem, dh_sem,
):
    step = pl.program_id(0)
    rows = normed.shape[0]
    chunks = act.shape[0]
    tile = FRONT_TILE
    tiles = rows // tile
    chunk = idiv(step, CHUNK_STEPS)
    phase = irem(step, CHUNK_STEPS)
    working = chunk < chunks
    slot = irem(chunk, 2)

    def tile_rows(i):
        return pl.ds(pl.multiple_of(i * tile, tile), tile)

    def row_load(i, hbm, vmem, sem):
        return pltpu.make_async_copy(hbm.at[tile_rows(i), :], vmem.at[tile_rows(i), :], sem.at[i])

    def row_store(i, vmem, hbm, sem):
        return pltpu.make_async_copy(vmem.at[tile_rows(i), :], hbm.at[tile_rows(i), :], sem.at[i])

    def weight_loads(c):
        s = irem(jnp.int32(c), 2)
        loads = []
        for n, (a, b, at, size) in enumerate(unit_strips(comm, win_hbm, wout_hbm, c * UNITS, UNITS, gathered)):
            loads.append(pltpu.make_async_copy(a, win.at[s, :, pl.ds(at, size)], in_sem.at[s, n]))
            loads.append(pltpu.make_async_copy(b, wout.at[s, pl.ds(at, size), :], out_sem.at[s, n]))
        return loads

    def low_stores(c):
        columns = pl.ds(pl.multiple_of(c * UNITS, UNITS), UNITS)
        return (
            pltpu.make_async_copy(act.at[c], act_hbm.at[:, columns], act_sem.at[c]),
            pltpu.make_async_copy(d_hidden.at[irem(c, 2)], dh_hbm.at[:, columns], dh_sem.at[c]),
        )

    @pl.when(step == 0)
    def _():
        row_load(0, tok_hbm, normed, tok_sem).start()
        row_load(0, cot_hbm, g, cot_sem).start()
        for load in weight_loads(0):
            load.start()
        for i in range(1, tiles):
            row_load(i, tok_hbm, normed, tok_sem).start()
            row_load(i, cot_hbm, g, cot_sem).start()

    @pl.when(working & (chunk == 0) & (phase < tiles))
    def _():
        row_load(phase, tok_hbm, normed, tok_sem).wait()
        row_load(phase, cot_hbm, g, cot_sem).wait()
        here = tile_rows(phase)
        x = normed[here, :].astype(f32)
        centered = x - jnp.mean(x, axis=-1, keepdims=True)
        var = jnp.mean(centered * centered, axis=-1, keepdims=True)
        normed[here, :] = (centered * lax.rsqrt(var + EPSILON) * gain_ref[...]).astype(bf16)
        g[here, :] = (g[here, :].astype(f32) * valid_ref[here, :]).astype(bf16)
        row_store(phase, normed, normed_hbm, normed_sem).start()
        row_store(phase, g, g_hbm, g_sem).start()

    @pl.when(working & (phase == 0))
    def _():
        for load in weight_loads(chunk):
            load.wait()

    @pl.when((phase == 0) & (chunk + 1 < chunks))
    def _():
        for load in weight_loads(chunk + 1):
            load.start()

    @pl.when(working & (phase < tiles))
    def _():
        here = tile_rows(phase)
        hidden = dot(normed[here, :], win[slot])
        d_active = dot_nt(g[here, :], wout[slot])
        value, slope = gelu_parts(hidden)
        act[chunk, here, :] = value.astype(bf16)
        d_hidden[slot, here, :] = (d_active * slope).astype(bf16)

    share_rows = D // comm.parts

    @pl.when(working & (phase == tiles))
    def _():
        for copy in low_stores(chunk):
            copy.start()
        made = dot_tn(normed[...], d_hidden[slot])
        for share in range(comm.parts):
            in_own[chunk, comm.place(kinds, share, chunk)] = made[share * share_rows : (share + 1) * share_rows, :]
        low_stores(chunk)[1].wait()

    unit_rows = FF // comm.streams // comm.parts
    blocks = D // OUT_COLUMNS
    for block in range(blocks):

        @pl.when(step == chunks * CHUNK_STEPS + block)
        def _(block=block):
            right = g[:, block * OUT_COLUMNS : (block + 1) * OUT_COLUMNS]
            for c in range(chunks):
                made = dot_tn(act[c], right)
                for n in range(UNITS // unit_rows):
                    share = c * (UNITS // unit_rows) + n
                    out_own[block, comm.place(out_kinds[block], share)] = made[n * unit_rows : (n + 1) * unit_rows, :]

    @pl.when(step == pl.num_programs(0) - 1)
    def _():
        for i in range(tiles):
            row_store(i, normed, normed_hbm, normed_sem).wait()
            row_store(i, g, g_hbm, g_sem).wait()
        for c in range(chunks):
            low_stores(jnp.int32(c))[0].wait()


def front(comm, tokens, cotangent, valid, gain, weights, plan):
    w_in, w_out, gathered = weights
    rows = tokens.shape[0]
    units = FF // comm.streams
    chunks, blocks = units // UNITS, D // OUT_COLUMNS
    tiles = rows // FRONT_TILE
    parts = comm.parts
    strips = 1 if gathered else UNITS // (units // parts)
    share_rows, unit_rows = D // parts, units // parts
    kinds = [KIND[f"in{c}"] for c in range(chunks)]
    out_kinds = [KIND[f"o{b}"] for b in range(blocks)]
    steps = chunks * CHUNK_STEPS + blocks
    inner = []
    for c in range(chunks):
        start, sums = plan.get(f"in{c}", (None, ()))
        shape = (parts, share_rows, UNITS)
        flow = Flow(f"in{c}", kinds[c], 0, shape, None, start, sums, (c + 1) * CHUNK_STEPS)
        inner.append((flow, 6, c))
    for b in range(blocks):
        start, sums = plan.get(f"o{b}", (None, ()))
        shape = (parts, unit_rows, OUT_COLUMNS)
        flow = Flow(f"o{b}", out_kinds[b], 0, shape, None, start, sums, chunks * CHUNK_STEPS + b + 1)
        inner.append((flow, 7, b))
    low = jax.ShapeDtypeStruct((rows, D), bf16)
    wide = jax.ShapeDtypeStruct((rows, units), bf16)
    return with_comm(
        comm,
        partial(front_kernel, comm, kinds, out_kinds, gathered),
        steps,
        [ANY, ANY, pl.BlockSpec((rows, 1), lambda i: (0, 0)), pl.BlockSpec((1, D), lambda i: (0, 0)), ANY, ANY],
        [ANY] * 4,
        [low, low, wide, wide],
        [],
        [tokens, cotangent, valid, gain, w_in, w_out],
        [
            pltpu.VMEM((rows, D), bf16),
            pltpu.VMEM((rows, D), bf16),
            pltpu.VMEM((2, D, UNITS), bf16),
            pltpu.VMEM((2, UNITS, D), bf16),
            pltpu.VMEM((chunks, rows, UNITS), bf16),
            pltpu.VMEM((2, rows, UNITS), bf16),
            pltpu.VMEM((chunks, parts, share_rows, UNITS), f32),
            pltpu.VMEM((blocks, parts, unit_rows, OUT_COLUMNS), f32),
            pltpu.SemaphoreType.DMA((tiles,)),
            pltpu.SemaphoreType.DMA((tiles,)),
            pltpu.SemaphoreType.DMA((2, strips)),
            pltpu.SemaphoreType.DMA((2, strips)),
            pltpu.SemaphoreType.DMA((tiles,)),
            pltpu.SemaphoreType.DMA((tiles,)),
            pltpu.SemaphoreType.DMA((chunks,)),
            pltpu.SemaphoreType.DMA((chunks,)),
        ],
        inner,
        name="front",
        cost_estimate=pl.CostEstimate(
            flops=8 * rows * D * units, bytes_accessed=12 * rows * D + 8 * units * D, transcendentals=rows * units
        ),
    )


def causal_mask(transposed):
    row = lax.broadcasted_iota(jnp.int32, (BLK, BLK), 0)
    col = lax.broadcasted_iota(jnp.int32, (BLK, BLK), 1)
    return col >= row if transposed else row >= col


def head_masks():
    lane = lax.broadcasted_iota(jnp.int32, (1, PAIR), 1)
    first = lane < HEAD
    m0 = jnp.where(first, 1.0, 0.0)
    return m0.astype(bf16), (1.0 - m0).astype(bf16)


def state_mask():
    row = lax.broadcasted_iota(jnp.int32, (PAIR, 2 * PAIR), 0)
    col = lax.broadcasted_iota(jnp.int32, (PAIR, 2 * PAIR), 1)
    return (row < HEAD) == (col < PAIR)


def forward_kernel(
    comm, groups, kind,
    normed_ref, wq_ref, wk_ref, wv_ref, cos_ref, sin_ref, fw_ref, map_ref, valid_ref, right_ref,
    q_ref, k_ref, v_ref, mix_ref, den_ref, state_ref,
    state, mixed_all, sent, arrived, proj_own, send_sem, recv_sem,
):
    step = pl.program_id(0)
    blocks = sent.shape[0]

    def to_partner(i):
        return pltpu.make_async_remote_copy(
            src_ref=sent.at[i],
            dst_ref=arrived.at[i],
            send_sem=send_sem.at[i],
            recv_sem=recv_sem.at[i],
            device_id=comm.other_core(),
            device_id_type=MESH,
        )

    @pl.when(step == 0)
    def _():
        state[...] = jnp.zeros_like(state)

    @pl.when(step < blocks)
    def _():
        rows = normed_ref[...]
        queries_all, keys_all, values_all = dot(rows, wq_ref[...]), dot(rows, wk_ref[...]), dot(rows, wv_ref[...])
        cosine, sine = cos_ref[...], sin_ref[...]
        valid = valid_ref[...]
        m0, m1 = head_masks()
        causal = causal_mask(False)
        keep_state = state_mask()
        first = lax.broadcasted_iota(jnp.int32, (BLK, PAIR), 1) < HEAD
        place = pl.ds(pl.multiple_of(step * BLK, BLK), BLK)
        each = range(groups)
        lanes = [slice(group * PAIR, (group + 1) * PAIR) for group in each]
        turned = [
            jnp.concatenate(
                [
                    jnp.concatenate([queries_all[:, here] * cosine, queries_all[:, here] * sine], 1),
                    jnp.concatenate([keys_all[:, here] * cosine, keys_all[:, here] * sine], 1),
                ],
                0,
            )
            for here in lanes
        ]
        high = [t.astype(bf16) for t in turned]
        low = [(t - h.astype(f32)).astype(bf16) for t, h in zip(turned, high)]
        main = [dot(h, map_ref[...]) for h in high]
        rest = [dot(l, map_ref[:, :PAIR]) for l in low]
        phi = [
            jnp.exp(m[:, :PAIR] + m[:, PAIR:] + r) * fw_ref[:, here] for m, r, here in zip(main, rest, lanes)
        ]
        q = [f[:BLK].astype(bf16) for f in phi]
        k = [(f[BLK:] * valid).astype(bf16) for f in phi]
        v = [values_all[:, here].astype(bf16) for here in lanes]
        for n in each:
            q_ref[:, lanes[n]] = q[n]
            k_ref[:, lanes[n]] = k[n]
            v_ref[:, lanes[n]] = v[n]
        v0 = [x * m0 + m1 for x in v]
        v1 = [x * m1 + m0 for x in v]
        s0 = [jnp.where(causal, dot_nt(q[n] * m0, k[n]), 0.0).astype(bf16) for n in each]
        s1 = [jnp.where(causal, dot_nt(q[n] * m1, k[n]), 0.0).astype(bf16) for n in each]
        before = [jnp.where(keep_state, state[n], 0.0).astype(bf16) for n in each]
        far = [dot(q[n], before[n]) for n in each]
        o0 = [dot(s0[n], v0[n]) + far[n][:, :PAIR] for n in each]
        o1 = [dot(s1[n], v1[n]) + far[n][:, PAIR:] for n in each]
        for n in each:
            state_ref[n, 0] = before[n]
            state[n] += dot_tn(k[n], jnp.concatenate([v0[n], v1[n]], 1))
        for n in each:
            here = lanes[n]
            numerator = jnp.where(first, o0[n], o1[n])
            denominator = pltpu.roll(jnp.where(first, o1[n], o0[n]), HEAD, 1)
            mixed = (numerator / denominator).astype(bf16)
            mix_ref[:, here] = mixed
            mixed_all[place, here] = mixed
            sent[step, :, here] = mixed.astype(f32)
            den_ref[:, here] = denominator
        to_partner(step).start()

    share_rows = D // comm.parts
    width = groups * PAIR
    core = lax.axis_index("stream")
    for side in range(2):

        @pl.when(step == blocks + side)
        def _(side=side):
            if side == 0:
                left = mixed_all[...]
                base = core * (width // share_rows)
            else:
                for i in range(blocks):
                    to_partner(i).wait_recv()
                left = arrived[...].reshape(blocks * BLK, width).astype(bf16)
                base = (1 - core) * (width // share_rows)
            made = dot_tn(left, right_ref[...])
            for n in range(width // share_rows):
                proj_own[comm.place(kind, base + n)] = made[n * share_rows : (n + 1) * share_rows, :]
            if side == 1:
                for i in range(blocks):
                    to_partner(i).wait_send()


def forward(comm, normed, g, w_qkv, cosine, sine, fw, table, valid, flows, plan):
    rows = normed.shape[0]
    streams, parts = comm.streams, comm.parts
    groups = HEADS // streams // 2
    width = groups * PAIR
    blocks = rows // BLK

    def at(i):
        return jnp.minimum(i, blocks - 1)

    row_spec = pl.BlockSpec((BLK, width), lambda i: (at(i), 0))
    table_spec = pl.BlockSpec((BLK, PAIR), lambda i: (at(i), 0))
    low = jax.ShapeDtypeStruct((rows, width), bf16)

    def weight_spec(which):
        return pl.BlockSpec((D, width), lambda i: (0, which * streams + lax.axis_index("stream")))

    start, sums = plan.get("pr", (None, ()))
    kind = KIND["pr"]
    columns = D // streams
    inner = [(Flow("pr", kind, 0, (parts, D // parts, columns), None, start, sums, blocks + 2), 4, None)]
    return with_comm(
        comm,
        partial(forward_kernel, comm, groups, kind),
        blocks + 2,
        [
            pl.BlockSpec((BLK, D), lambda i: (at(i), 0)),
            weight_spec(0),
            weight_spec(1),
            weight_spec(2),
            table_spec,
            table_spec,
            pl.BlockSpec((1, width), lambda i: (0, lax.axis_index("stream"))),
            pl.BlockSpec((2 * PAIR, 2 * PAIR), lambda i: (0, 0)),
            pl.BlockSpec((BLK, 1), lambda i: (at(i), 0)),
            pl.BlockSpec((rows, columns), lambda i: (0, lax.axis_index("stream"))),
        ],
        [row_spec, row_spec, row_spec, row_spec, row_spec,
         pl.BlockSpec((groups, 1, PAIR, 2 * PAIR), lambda i: (0, at(i), 0, 0))],
        [low, low, low, low, jax.ShapeDtypeStruct((rows, width), f32),
         jax.ShapeDtypeStruct((groups, blocks, PAIR, 2 * PAIR), bf16)],
        flows,
        [normed, w_qkv, w_qkv, w_qkv, cosine, sine, fw, table, valid, g],
        [
            pltpu.VMEM((groups, PAIR, 2 * PAIR), f32),
            pltpu.VMEM((rows, width), bf16),
            pltpu.VMEM((blocks, BLK, width), f32),
            pltpu.VMEM((blocks, BLK, width), f32),
            pltpu.VMEM((parts, D // parts, columns), f32),
            pltpu.SemaphoreType.DMA((blocks,)),
            pltpu.SemaphoreType.DMA((blocks,)),
        ],
        inner,
        exchange=True,
        name="attention_forward",
        cost_estimate=pl.CostEstimate(
            flops=groups * blocks * 2 * 65536 * 5000,
            bytes_accessed=rows * D * 2 + 3 * D * width * 2 + rows * width * 16,
            transcendentals=2 * rows * width,
        ),
    )


GROUPS = 2
BACK_STEPS = 2


def backward_kernel(
    comm, blocks, kinds, feature_kind,
    g_ref, wp_ref, q_ref, k_ref, v_ref, mix_ref, den_ref, state_ref, cos_ref, sin_ref, back_ref, back_low_ref,
    sums_ref, fw_ref, normed_hbm,
    dq_ref, dk_ref, dv_ref,
    later, d_all, normed, fg, qkv_own, feature_own, load_sem,
):
    step = pl.program_id(0)
    per = blocks + BACK_STEPS
    call, phase = idiv(step, per), irem(step, per)
    width = GROUPS * PAIR
    load = pltpu.make_async_copy(normed_hbm, normed, load_sem)

    @pl.when(step == 0)
    def _():
        load.start()
        feature_own[...] = jnp.zeros_like(feature_own)

    @pl.when(phase == 0)
    def _():
        later[...] = jnp.zeros_like(later)
        fg[...] = jnp.zeros_like(fg)

    @pl.when(phase < blocks)
    def _():
        m0, m1 = head_masks()
        first = lax.broadcasted_iota(jnp.int32, (BLK, PAIR), 1) < HEAD
        left = lax.broadcasted_iota(jnp.int32, (PAIR, PAIR), 1) < HEAD
        own = (lax.broadcasted_iota(jnp.int32, (PAIR, PAIR), 0) < HEAD) == left
        causal, flipped = causal_mask(False), causal_mask(True)
        keep_state = state_mask()
        cosine, sine = cos_ref[...], sin_ref[...]
        d_mixed_all = dot_nt(g_ref[...], wp_ref[...])
        place = pl.ds(pl.multiple_of((blocks - 1 - phase) * BLK, BLK), BLK)
        each = range(GROUPS)
        lanes = [slice(group * PAIR, (group + 1) * PAIR) for group in each]
        q = [q_ref[:, here] for here in lanes]
        k = [k_ref[:, here] for here in lanes]
        v = [v_ref[:, here] for here in lanes]
        q0, q1 = [x * m0 for x in q], [x * m1 for x in q]
        k0, k1 = [x * m0 for x in k], [x * m1 for x in k]
        v0, v1 = [x * m0 + m1 for x in v], [x * m1 + m0 for x in v]
        st0 = [jnp.where(flipped, dot_nt(k[n], q0[n]), 0.0).astype(bf16) for n in each]
        st1 = [jnp.where(flipped, dot_nt(k[n], q1[n]), 0.0).astype(bf16) for n in each]
        numer = [d_mixed_all[:, here] / den_ref[:, here] for here in lanes]
        product = [numer[n] * mix_ref[:, lanes[n]].astype(f32) for n in each]
        p_high = [x.astype(bf16) for x in product]
        p_low = [(x - h.astype(f32)).astype(bf16) for x, h in zip(product, p_high)]
        sums = [dot(jnp.concatenate([p_high[n], p_low[n]], 1), sums_ref[...]) for n in each]
        behind = [later[n] for n in each]
        after = [jnp.where(keep_state, x, 0.0).astype(bf16) for x in behind]
        after_v = [
            jnp.where(own, jnp.where(left, x[:, :PAIR], x[:, PAIR:]), 0.0).astype(bf16) for x in behind
        ]
        d_v = [dot(k[n], after_v[n]) for n in each]
        d_k = [dot_nt(jnp.concatenate([v0[n], v1[n]], 1), after[n]) for n in each]
        d_o0 = [jnp.where(first, numer[n], -sums[n]).astype(bf16) for n in each]
        d_o1 = [jnp.where(first, -sums[n], numer[n]).astype(bf16) for n in each]
        d_o = [jnp.concatenate([d_o0[n], d_o1[n]], 1) for n in each]
        low = [x.astype(bf16) for x in numer]
        ds0 = [jnp.where(causal, dot_nt(d_o0[n], v0[n]), 0.0).astype(bf16) for n in each]
        ds1 = [jnp.where(causal, dot_nt(d_o1[n], v1[n]), 0.0).astype(bf16) for n in each]
        dst0 = [jnp.where(flipped, dot_nt(v0[n], d_o0[n]), 0.0).astype(bf16) for n in each]
        dst1 = [jnp.where(flipped, dot_nt(v1[n], d_o1[n]), 0.0).astype(bf16) for n in each]
        d_q = [dot_nt(d_o[n], state_ref[n, 0]) for n in each]
        d_v = [d_v[n] + dot(st0[n], low[n] * m0) + dot(st1[n], low[n] * m1) for n in each]
        d_q = [d_q[n] + dot(ds0[n], k0[n]) + dot(ds1[n], k1[n]) for n in each]
        d_k = [d_k[n] + dot(dst0[n], q0[n]) + dot(dst1[n], q1[n]) for n in each]
        for n in each:
            later[n] += dot_tn(q[n], d_o[n])
        e_q = [d_q[n] * q[n].astype(f32) for n in each]
        e_k = [d_k[n] * k[n].astype(f32) for n in each]
        both = [jnp.concatenate([e_q[n], e_k[n]], 0) for n in each]
        high = [x.astype(bf16) for x in both]
        lower = [(x - h.astype(f32)).astype(bf16) for x, h in zip(both, high)]
        turned = [
            dot(jnp.concatenate([high[n], lower[n]], 1), back_ref[...]) + dot(high[n], back_low_ref[...])
            for n in each
        ]
        for n in each:
            here = lanes[n]
            fg[:, here] += jnp.sum((e_q[n] + e_k[n]).reshape(BLK // 8, 8, PAIR), axis=0)
            dv = d_v[n].astype(bf16)
            dq = (turned[n][:BLK, :PAIR] * cosine + turned[n][:BLK, PAIR:] * sine).astype(bf16)
            dk = (turned[n][BLK:, :PAIR] * cosine + turned[n][BLK:, PAIR:] * sine).astype(bf16)
            dq_ref[:, here] = dq
            dk_ref[:, here] = dk
            dv_ref[:, here] = dv
            d_all[place, n * PAIR : (n + 1) * PAIR] = dq
            d_all[place, width + n * PAIR : width + (n + 1) * PAIR] = dk
            d_all[place, 2 * width + n * PAIR : 2 * width + (n + 1) * PAIR] = dv

    @pl.when(step == blocks)
    def _():
        load.wait()

    share_rows = D // comm.parts
    wide = D // BACK_STEPS
    for m in range(BACK_STEPS):

        @pl.when(phase == blocks + m)
        def _(m=m):
            made = dot_tn(normed[:, m * wide : (m + 1) * wide], d_all[...])
            for n in range(wide // share_rows):
                share = m * (wide // share_rows) + n
                qkv_own[call, comm.place(kinds, share, call)] = made[n * share_rows : (n + 1) * share_rows, :]
            if m == 0:
                total = jnp.sum(fg[...], axis=0, keepdims=True) / fw_ref[...]
                size = D // comm.parts
                core = lax.axis_index("stream")
                for n in range(width // size):
                    pair, inside = divmod(n * size, PAIR)
                    row = total[:, pair * PAIR : (pair + 1) * PAIR]
                    row = jnp.broadcast_to(row, (8, PAIR))
                    if inside:
                        row = pltpu.roll(row, PAIR - inside, 1)
                    share = core * (D // comm.streams // size) + call * (width // size) + n
                    feature_own[comm.place(feature_kind, share)] = row


def backward(comm, normed, g, w_proj, kept, cosine, sine, backs, sums, fw, flows, plan):
    q, k, v, mixed, den, states = kept
    rows = g.shape[0]
    streams, parts = comm.streams, comm.parts
    calls = HEADS // streams // 2 // GROUPS
    blocks = rows // BLK
    per = blocks + BACK_STEPS
    width = GROUPS * PAIR

    def at(i):
        return jnp.maximum(blocks - 1 - irem(i, per), 0)

    def call(i):
        return idiv(i, per)

    row_spec = pl.BlockSpec((BLK, width), lambda i: (at(i), call(i)))
    table_spec = pl.BlockSpec((BLK, PAIR), lambda i: (at(i), 0))
    low = jax.ShapeDtypeStruct((rows, calls * width), bf16)
    inner = []
    for c in range(calls):
        start, when = plan.get(f"q{c}", (None, ()))
        shape = (parts, D // parts, 3 * width)
        inner.append((Flow(f"q{c}", KIND[f"q{c}"], 0, shape, None, start, when, (c + 1) * per), 4, c))
    inner.append((Flow("feature", KIND["feature"], 0, (parts, 8, PAIR), None, None, (), calls * per), 5, None))
    return with_comm(
        comm,
        partial(backward_kernel, comm, blocks, [KIND[f"q{c}"] for c in range(calls)], KIND["feature"]),
        calls * per,
        [
            pl.BlockSpec((BLK, D), lambda i: (at(i), 0)),
            pl.BlockSpec((width, D), lambda i: (lax.axis_index("stream") * calls + call(i), 0)),
            row_spec,
            row_spec,
            row_spec,
            row_spec,
            row_spec,
            pl.BlockSpec((GROUPS, 1, PAIR, 2 * PAIR), lambda i: (call(i), at(i), 0, 0)),
            table_spec,
            table_spec,
            pl.BlockSpec((2 * PAIR, 2 * PAIR), lambda i: (0, 0)),
            pl.BlockSpec((PAIR, 2 * PAIR), lambda i: (0, 0)),
            pl.BlockSpec((2 * PAIR, PAIR), lambda i: (0, 0)),
            pl.BlockSpec((1, width), lambda i: (0, lax.axis_index("stream") * calls + call(i))),
            ANY,
        ],
        [row_spec, row_spec, row_spec],
        [low, low, low],
        flows,
        [g, w_proj, q, k, v, mixed, den, states, cosine, sine, *backs, sums, fw, normed],
        [
            pltpu.VMEM((GROUPS, PAIR, 2 * PAIR), f32),
            pltpu.VMEM((rows, 3 * width), bf16),
            pltpu.VMEM((rows, D), bf16),
            pltpu.VMEM((8, width), f32),
            pltpu.VMEM((calls, parts, D // parts, 3 * width), f32),
            pltpu.VMEM((parts, 8, PAIR), f32),
            pltpu.SemaphoreType.DMA,
        ],
        inner,
        name="attention_backward",
        cost_estimate=pl.CostEstimate(
            flops=2 * 65536 * GROUPS * calls * (blocks * 6500 + 16384),
            bytes_accessed=2 * (2 * rows * D + width * D + rows * width * 24),
            transcendentals=0,
        ),
    )


def tail_kernel(
    comm, tiles, gathered,
    act_ref, dh_ref, mix_ref, dq_ref, dk_ref, dv_ref, tok_ref, cot_ref, valid_ref, gain_ref,
    wproj_ref, wqkv_hbm, win_hbm, wout_hbm,
    out_ref, grad_ref,
    win, wout, wqkv, mine, arrived, in_sem, out_sem, qkv_sem, send_sem, recv_sem,
):
    step = pl.program_id(0)
    units = win.shape[1]
    strips = unit_strips(comm, win_hbm, wout_hbm, 0, units, gathered)
    loads = []
    for n, (a, b, at, size) in enumerate(strips):
        loads.append(pltpu.make_async_copy(a, win.at[:, pl.ds(at, size)], in_sem.at[n]))
        loads.append(pltpu.make_async_copy(b, wout.at[pl.ds(at, size), :], out_sem.at[n]))

    core = lax.axis_index("stream")
    width = mix_ref.shape[1]
    for n in range(3):
        start = pl.multiple_of((n * comm.streams + core) * width, width)
        loads.append(
            pltpu.make_async_copy(wqkv_hbm.at[:, pl.ds(start, width)], wqkv.at[:, pl.ds(n * width, width)], qkv_sem.at[n])
        )

    def send(i, part):
        return pltpu.make_async_remote_copy(
            src_ref=mine.at[irem(i, 3), part],
            dst_ref=arrived.at[i, part],
            send_sem=send_sem.at[i, part],
            recv_sem=recv_sem.at[i, part],
            device_id=comm.other_core(),
            device_id_type=MESH,
        )

    @pl.when(step == 0)
    def _():
        for load in loads:
            load.start()
        for load in loads:
            load.wait()

    @pl.when((step >= 3) & (step < tiles))
    def _():
        send(step - 3, 0).wait_send()
        send(step - 3, 1).wait_send()

    @pl.when(step >= 2)
    def _():
        send(step - 2, 0).wait_recv()
        send(step - 2, 1).wait_recv()

    def products():
        slot = irem(step, 3)
        mine[slot, 0] = dot(act_ref[...], wout[...])
        mine[slot, 0] += dot(mix_ref[...], wproj_ref[...])
        send(step, 0).start()
        d_qkv = jnp.concatenate([dq_ref[...], dk_ref[...], dv_ref[...]], 1)
        mine[slot, 1] = dot_nt(dh_ref[...], win[...])
        mine[slot, 1] += dot_nt(d_qkv, wqkv[...])
        send(step, 1).start()

    def finish_rows():
        slot = irem(step + 1, 3)
        x = tok_ref[...].astype(f32)
        centered = x - jnp.mean(x, axis=-1, keepdims=True)
        var = jnp.mean(centered * centered, axis=-1, keepdims=True)
        inv_std = lax.rsqrt(var + EPSILON)
        unit = centered * inv_std
        out_ref[...] = (x + (mine[slot, 0] + arrived[step - 2, 0]) * valid_ref[...]).astype(bf16)
        scaled = (mine[slot, 1] + arrived[step - 2, 1]) * gain_ref[...]
        mean = jnp.mean(scaled, axis=-1, keepdims=True)
        cross = jnp.mean(scaled * unit, axis=-1, keepdims=True)
        grad_ref[...] = (cot_ref[...].astype(f32) + inv_std * (scaled - mean - unit * cross)).astype(bf16)

    @pl.when(step < 2)
    def _():
        products()

    @pl.when((step >= 2) & (step < tiles))
    def _():
        finish_rows()
        products()

    @pl.when(step >= tiles)
    def _():
        finish_rows()

    @pl.when(step == tiles + 1)
    def _():
        for i in (tiles - 3, tiles - 2, tiles - 1):
            send(i, 0).wait_send()
            send(i, 1).wait_send()


def tail(comm, active, d_hidden, mixed, d_qkv, tokens, cotangent, valid, gain, weights, w_proj, w_qkv, flows):
    w_in, w_out, gathered = weights
    rows, units = active.shape
    width = mixed.shape[1]
    tiles = rows // TILE
    strips = 1 if gathered else comm.parts

    def now(i):
        return (jnp.minimum(i, tiles - 1), 0)

    def before(i):
        return (jnp.maximum(i - 2, 0), 0)

    shape = jax.ShapeDtypeStruct((rows, D), bf16)
    return with_comm(
        comm,
        partial(tail_kernel, comm, tiles, gathered),
        tiles + 2,
        [
            pl.BlockSpec((TILE, units), now),
            pl.BlockSpec((TILE, units), now),
            pl.BlockSpec((TILE, width), now),
            pl.BlockSpec((TILE, width), now),
            pl.BlockSpec((TILE, width), now),
            pl.BlockSpec((TILE, width), now),
            pl.BlockSpec((TILE, D), before),
            pl.BlockSpec((TILE, D), before),
            pl.BlockSpec((TILE, 1), before),
            pl.BlockSpec((1, D), lambda i: (0, 0)),
            pl.BlockSpec((width, D), lambda i: (lax.axis_index("stream"), 0)),
            ANY,
            ANY,
            ANY,
        ],
        [pl.BlockSpec((TILE, D), before), pl.BlockSpec((TILE, D), before)],
        [shape, shape],
        flows,
        [active, d_hidden, mixed, *d_qkv, tokens, cotangent, valid, gain, w_proj, w_qkv, w_in, w_out],
        [
            pltpu.VMEM((D, units), bf16),
            pltpu.VMEM((units, D), bf16),
            pltpu.VMEM((D, 3 * width), bf16),
            pltpu.VMEM((3, 2, TILE, D), f32),
            pltpu.VMEM((tiles, 2, TILE, D), f32),
            pltpu.SemaphoreType.DMA((strips,)),
            pltpu.SemaphoreType.DMA((strips,)),
            pltpu.SemaphoreType.DMA((3,)),
            pltpu.SemaphoreType.DMA((tiles, 2)),
            pltpu.SemaphoreType.DMA((tiles, 2)),
        ],
        exchange=True,
        name="tail",
        cost_estimate=pl.CostEstimate(
            flops=2 * rows * D * (2 * units + 4 * width),
            bytes_accessed=2 * (rows + D) * (2 * units + 4 * width) + 8 * rows * D,
            transcendentals=0,
        ),
    )


KIND = {
    "in0": "xx",
    "in1": "xz",
    "in2": "yz",
    "in3": "xy",
    "o0": "xz",
    "o1": "xp",
    "o2": "zx",
    "o3": "xy",
    "pr": "xx",
    "q0": "xy",
    "q1": "xp",
    "feature": "xy",
}
FRONT = {
    "in0": (3, (10, 15)),
    "in1": (6, (14, -1)),
    "in2": (11, (-1,)),
    "o1": (14, (-1,)),
    "o2": (15, (-1,)),
}
FORWARD = {
    "o2": (0, (8, -1)),
    "o0": (0, (8, -1)),
    "o1": (0, (8, -1)),
    "o3": (1, (-1,)),
    "in2": (3, (8, -1)),
}
BACKWARD = {
    "pr": (0, (12, -1)),
    "in3": (0, (12, 18)),
    "o3": (0, (14, 19, -1)),
    "o2": (0, (8,)),
    "o1": (0, (8,)),
    "in2": (0, (8,)),
    "in0": (1, (11,)),
    "in1": (3, (8, 12)),
    "q0": (11, (-1,)),
    "o0": (12, (17, -1)),
}
TAIL = {
    "feature": (0, (5, 9)),
    "q1": (0, (4, 8, -1)),
    "q0": (0, (7, 9, -1)),
    "in3": (0, (1, 4)),
    "pr": (1, (5,)),
    "in0": (2, (5,)),
}


def solution(mesh):
    comm = Comm(mesh.shape["dp"], mesh.shape["stream"])
    parts, streams = comm.parts, comm.streams
    cosine_np, sine_np, map_np, back_high_np, back_low_np = attention_tables()
    sums_np = np.zeros((2 * PAIR, PAIR), np.float32)
    for base in (0, PAIR):
        sums_np[base : base + HEAD, HEAD] = 1.0
        sums_np[base + HEAD : base + PAIR, 0] = 1.0

    def partner(value):
        pairs = []
        for d in range(parts):
            for s in range(streams):
                pairs.append((d * streams + s, d * streams + (s ^ 1)))
        return lax.ppermute(value, ("dp", "stream"), pairs)

    def body(tokens, norm_gain, w_qkv, w_proj, w_in, w_out, feature_weight, lengths, cotangent):
        comm.kernels = 0
        rows = tokens.shape[0]
        chip = lax.axis_index("dp")
        stream = lax.axis_index("stream")
        gain = norm_gain.reshape(1, D)
        fw = feature_weight.reshape(1, D)
        cosine, sine = jnp.asarray(cosine_np), jnp.asarray(sine_np)
        valid = (jnp.arange(rows) < lengths[0]).astype(f32).reshape(rows, 1)
        weights = gather_units(comm, w_in, w_out)
        units = FF // streams
        done = {}

        def flows_of(plan):
            flows = []
            for name, (start, sums) in plan.items():
                if name in done and done[name][0] < comm.steps:
                    taken, array = done[name]
                    sums = sums[: comm.steps - taken]
                    flows.append(Flow(name, KIND[name], taken, array.shape, array, start, sums))
            return flows

        def landed(shares, plan):
            for name, array in shares.items():
                taken = done[name][0] if name in done else 0
                done[name] = (taken + (len(plan[name][1][: comm.steps - taken]) if name in plan else 0), array)

        (normed, g, act, d_hidden), shares = front(comm, tokens, cotangent, valid, gain, weights, FRONT)
        landed(shares, FRONT)
        kept, shares = forward(
            comm, normed, g, w_qkv, cosine, sine, fw, jnp.asarray(map_np), valid, flows_of(FORWARD), FORWARD
        )
        landed(shares, FORWARD)
        backs = (jnp.asarray(back_high_np), jnp.asarray(back_low_np))
        d_qkv, shares = backward(
            comm, normed, g, w_proj, kept, cosine, sine, backs, jnp.asarray(sums_np, bf16), fw,
            flows_of(BACKWARD), BACKWARD,
        )
        landed(shares, BACKWARD)
        (output, input_grad), shares = tail(
            comm, act, d_hidden, kept[3], d_qkv, tokens, cotangent, valid, gain, weights, w_proj, w_qkv,
            flows_of(TAIL),
        )
        landed(shares, TAIL)
        left = {}
        for name, (taken, _) in done.items():
            if taken < comm.steps:
                left[name] = (0, tuple(range(1, comm.steps - taken + 1)))
        if left:
            length = 1 + max(len(sums) for _, sums in left.values())
            _, shares = with_comm(
                comm, lambda *refs: None, length, [], [], [], flows_of(left), [], name="rest"
            )
            landed(shares, left)
        final = {name: array[0] for name, (_, array) in done.items()}

        value = final["feature"]
        value = value + partner(value)
        share = D // (parts * streams)
        feature_grad = lax.dynamic_slice(value, (0, stream * share), (1, share)).reshape(share)

        half = D // parts // streams
        names = [f"in{c}" for c in range(units // UNITS)]
        names += [f"q{c}" for c in range(HEADS // streams // 2 // GROUPS)] + ["pr"]
        mine = jnp.concatenate([lax.dynamic_slice_in_dim(final[n], stream * half, half) for n in names], 1)
        other = partner(
            jnp.concatenate([lax.dynamic_slice_in_dim(final[n], (1 - stream) * half, half) for n in names], 1)
        )
        a = jnp.where(stream == 0, mine, other)
        b = jnp.where(stream == 0, other, mine)
        unit = units // parts
        in_grad = jnp.concatenate(
            [src[:, unit * i : unit * (i + 1)] for i in range(parts) for src in (a, b)], 1
        )
        qa, qb = a[:, units : units + 3 * D // streams], b[:, units : units + 3 * D // streams]
        wide = GROUPS * PAIR
        calls = HEADS // streams // 2 // GROUPS

        def third(src, which):
            return [src[:, (3 * n + which) * wide : (3 * n + which + 1) * wide] for n in range(calls)]

        qkv_grad = jnp.concatenate(sum([third(qa, w) + third(qb, w) for w in range(3)], []), 1)
        proj_grad = jnp.concatenate([a[:, units + 3 * D // streams :], b[:, units + 3 * D // streams :]], 1)
        out_grad = jnp.concatenate([final[f"o{n}"] for n in range(D // OUT_COLUMNS)], 1)
        first_row = (chip * streams + stream) * half
        w_in_rows = lax.dynamic_slice_in_dim(w_in, first_row, half).astype(f32)
        w_qkv_rows = lax.dynamic_slice_in_dim(w_qkv, first_row, half).astype(f32)
        gain_rows = lax.dynamic_slice_in_dim(norm_gain, first_row, half)
        gain_grad = (jnp.sum(w_in_rows * in_grad, 1) + jnp.sum(w_qkv_rows * qkv_grad, 1)) / gain_rows
        return output, input_grad, gain_grad, qkv_grad, proj_grad, in_grad, out_grad, feature_grad

    both = P(("dp", "stream"), None)
    return jax.shard_map(
        body,
        mesh=mesh,
        in_specs=(P("dp", None), P(), P(), P(), P(), P(), P(), P("dp"), P("dp", None)),
        out_specs=(
            P("dp", None), P("dp", None), P(("dp", "stream")), both, both, both, both, P(("dp", "stream")),
        ),
        check_vma=False,
    )
```

```python
import math
from functools import partial

import jax
import jax.numpy as jnp
import numpy as np
from jax import lax
from jax.experimental import pallas as pl
from jax.experimental.pallas import tpu as pltpu
from jax.sharding import PartitionSpec as P

D = 1024
HEADS = 16
HEAD = 64
FF = 4096
ROT = 16
SLOT = 2048
EPSILON = 1e-05

f32 = jnp.float32
bf16 = jnp.bfloat16
VMEM_LIMIT = 62 * 1024 * 1024
BLK = 256
PAIR = 2 * HEAD


def dot(a, b):
    return lax.dot_general(a, b, (((1,), (0,)), ((), ())), preferred_element_type=f32)


def dot_nt(a, b):
    return lax.dot_general(a, b, (((1,), (1,)), ((), ())), preferred_element_type=f32)


def dot_tn(a, b):
    return lax.dot_general(a, b, (((0,), (0,)), ((), ())), preferred_element_type=f32)


def erf_inverse(y):
    x = 0.0
    for _ in range(200):
        step = (math.erf(x) - y) / (2.0 / math.sqrt(math.pi) * math.exp(-x * x))
        x -= max(-0.5, min(0.5, step))
    return x


def feature_table():
    i = np.arange(HEAD, dtype=np.float64)
    cos_table = np.cos(np.pi * (2.0 * i[:, None] + 1.0) * i[None, :] / (2.0 * HEAD))
    weights = np.where(i == 0, math.sqrt(1.0 / HEAD), math.sqrt(2.0 / HEAD))
    quantiles = math.sqrt(2.0) * np.array([erf_inverse(2.0 * (m + 0.5) / HEAD - 1.0) for m in range(HEAD)])
    return cos_table * (weights * 0.5 * quantiles)[None, :]


def split_table(table):
    high = table.astype(np.float32).astype(bf16)
    low = (table - high.astype(np.float64)).astype(np.float32).astype(bf16)
    return high, low


def attention_tables():
    half = ROT // 2
    pos = np.arange(SLOT, dtype=np.float32)
    inverse = (np.float32(10000.0) ** (-2.0 * np.arange(half, dtype=np.float32) / np.float32(ROT))).astype(np.float32)
    angles = (pos[:, None] * inverse[None, :]).astype(np.float32).astype(np.float64)
    cos_one = np.ones((SLOT, HEAD))
    sin_one = np.zeros((SLOT, HEAD))
    cos_one[:, :half] = np.cos(angles)
    cos_one[:, half:ROT] = np.cos(angles)
    sin_one[:, :half] = np.sin(angles)
    sin_one[:, half:ROT] = -np.sin(angles)
    cosine = np.concatenate([cos_one, cos_one], 1).astype(np.float32)
    sine = np.concatenate([sin_one, sin_one], 1).astype(np.float32)
    one = feature_table()
    pair = np.zeros((PAIR, PAIR))
    pair[:HEAD, :HEAD] = one
    pair[HEAD:, HEAD:] = one
    swapped = pair.copy()
    for base in (0, HEAD):
        swapped[base : base + half] = pair[base + half : base + ROT]
        swapped[base + half : base + ROT] = pair[base : base + half]
    both = np.concatenate([pair, swapped], 0)
    high, low = split_table(both)
    forward = np.concatenate([high, low], 1)
    back_high, back_low = split_table(np.concatenate([pair.T, swapped.T], 1))
    back_high2 = np.concatenate([back_high, back_high], 0)
    return cosine, sine, forward, back_high2, back_low


def params(**extra):
    return pltpu.CompilerParams(vmem_limit_bytes=VMEM_LIMIT, **extra)


ANY = pl.BlockSpec(memory_space=pl.ANY)
MESH = pl.DeviceIdType.MESH


def idiv(a, b):
    return lax.div(a, jnp.int32(b))


def irem(a, b):
    return lax.rem(a, jnp.int32(b))


FIRST_BITS = {
    "xy": ("xzy", "yzx"), "zz": ("zxy", "zyx"), "xx": ("xyz", "yxz"), "xz": ("xzy", "zyx"),
    "yz": ("yzx", "zxy"), "xp": ("xyz", "yzx"), "zx": ("zyx", "xyz"), "zy": ("zxy", "yxz"),
}


class Comm:
    def __init__(self, parts, streams):
        self.parts, self.streams = parts, streams
        self.steps = parts.bit_length() - 1
        self.kernels = 0

    def orders(self, kind):
        result = []
        for s in range(2):
            order = [1 << b for b in range(self.steps)]
            if self.steps >= 3:
                order[:3] = [1 << "xyz".index(axis) for axis in FIRST_BITS[kind][s]]
            result.append(order)
        return result

    def place(self, kinds, share, which=None):
        chip, core = lax.axis_index("dp"), lax.axis_index("stream")
        kinds = [kinds] if isinstance(kinds, str) else list(kinds)
        total = jnp.int32(0)
        for b in range(self.steps):
            mask = 1 << b
            weight = jnp.int32(0)
            for n, kind in enumerate(kinds):
                values = [1 << (self.steps - 1 - order.index(mask)) for order in self.orders(kind)]
                value = values[0] + core * (values[1] - values[0])
                weight = value if n == 0 else jnp.where(which == n, value, weight)
            own = irem(idiv(chip, mask), 2)
            theirs = (share >> b) & 1 if isinstance(share, int) else irem(idiv(share, mask), 2)
            total = total + weight * irem(own + theirs, 2)
        return total

    def partner(self, kind, step):
        chip, core = lax.axis_index("dp"), lax.axis_index("stream")
        chips = []
        for order in self.orders(kind):
            mask = order[step]
            chips.append(chip + mask - 2 * mask * irem(idiv(chip, mask), 2))
        return (chips[0] + core * (chips[1] - chips[0]), core)

    def other_core(self):
        return (lax.axis_index("dp"), 1 - lax.axis_index("stream"))


class Flow:
    def __init__(self, name, kind, first, shape, array=None, start=None, sums=(), ready=0):
        self.name, self.kind, self.first, self.shape, self.array = name, kind, first, tuple(shape), array
        self.start, self.sums, self.ready = start, tuple(sums), ready
        self.half = shape[0] // 2
        self.slots = sum(self.half >> k for k in range(len(self.sums)))

    def out_shape(self):
        return (self.shape[0] >> len(self.sums),) + self.shape[1:]

    def scratch(self):
        half, (_, rows, columns) = self.half, self.shape
        kept = [pltpu.VMEM((2 * half, rows, columns), f32)] if self.array is not None else []
        count = max(len(self.sums), 1)
        return kept + [
            pltpu.VMEM((max(self.slots, 1), rows, columns), f32),
            pltpu.SemaphoreType.DMA((count,)),
            pltpu.SemaphoreType.DMA((count,)),
            pltpu.SemaphoreType.DMA((2,)),
        ]

    def bind(self, comm, own, source, out, scratch):
        self.comm, self.source, self.out = comm, source, out
        scratch = list(scratch)
        self.own = scratch.pop(0) if self.array is not None else own
        self.recv, self.send_sem, self.recv_sem, self.local_sem = scratch

    def offset(self, k):
        return sum(self.half >> j for j in range(k))

    def remote(self, k):
        count = self.half >> k
        return pltpu.make_async_remote_copy(
            src_ref=self.own.at[pl.ds(count, count)],
            dst_ref=self.recv.at[pl.ds(self.offset(k), count)],
            send_sem=self.send_sem.at[k],
            recv_sem=self.recv_sem.at[k],
            device_id=self.comm.partner(self.kind, self.first + k),
            device_id_type=MESH,
        )

    def load(self):
        return pltpu.make_async_copy(self.source, self.own, self.local_sem.at[0])

    def store(self):
        return pltpu.make_async_copy(
            self.own.at[pl.ds(0, self.shape[0] >> len(self.sums))], self.out, self.local_sem.at[1]
        )

    def moves(self):
        return self.start is not None

    def events(self, step, last):
        if not self.moves():
            when = self.ready

            @pl.when((step == when) if not last else (step < 0))
            def _():
                self.store().start()

            return

        if not last:

            if self.array is not None and self.start > 0:

                @pl.when(step == self.start - 1)
                def _():
                    self.load().start()

            @pl.when(step == self.start)
            def _():
                if self.array is not None:
                    self.load().wait()
                self.remote(0).start()

        for k, at in enumerate(self.sums):
            if (at < 0) != last:
                continue

            @pl.when(step >= 0 if last else step == at)
            def _(k=k):
                self.remote(k).wait_recv()
                count = self.half >> k
                base = self.offset(k)

                def add(p, carry):
                    self.own[p] = self.own[p] + self.recv[base + p]
                    return carry

                lax.fori_loop(0, count, add, 0)
                if k + 1 < len(self.sums):
                    self.remote(k + 1).start()
                else:
                    self.store().start()

    def finish(self):
        if self.moves():
            for k in range(len(self.sums)):
                self.remote(k).wait_send()
        self.store().wait()


def with_comm(
    comm, kernel, steps, in_specs, out_specs, out_shape, flows, operands, scratch_shapes=(), inner=(), exchange=False,
    share_flows=False, name=None, **call,
):
    base_in, base_out, base_scratch = len(in_specs), len(out_specs), len(scratch_shapes)
    every = list(flows) + [flow for flow, _, _ in inner]
    flow_scratch = [flow.scratch() if flow.moves() or flow.array is not None else [pltpu.SemaphoreType.DMA((2,))] for flow in every]
    remote = any(flow.moves() for flow in every)

    def run(*refs):
        refs = list(refs)

        def take(count):
            taken = refs[:count]
            del refs[:count]
            return taken

        own_in, flow_in = take(base_in), take(len(flows))
        own_out, flow_out = take(base_out), take(len(every))
        own_scratch = take(base_scratch)
        for n, flow in enumerate(every):
            got = take(len(flow_scratch[n]))
            if n < len(flows):
                flow.bind(comm, None, flow_in[n], flow_out[n], got)
            else:
                _, index, at = inner[n - len(flows)]
                if not flow.moves():
                    got = [None, None, None] + got
                own = own_scratch[index] if at is None else own_scratch[index].at[at]
                flow.bind(comm, own, None, flow_out[n], got)
        step = pl.program_id(0)
        if remote or exchange:

            @pl.when(step == 0)
            def _():
                for flow in every:
                    if flow.array is not None and flow.start == 0:
                        flow.load().start()
                barrier = pltpu.get_barrier_semaphore()
                chip, core = lax.axis_index("dp"), lax.axis_index("stream")
                others = []
                if remote:
                    for b in range(comm.steps):
                        mask = 1 << b
                        others.append((chip + mask - 2 * mask * irem(idiv(chip, mask), 2), core))
                if exchange:
                    others.append(comm.other_core())
                for other in others:
                    pl.semaphore_signal(barrier, inc=1, device_id=other, device_id_type=MESH)
                pl.semaphore_wait(barrier, len(others))

        for flow in every:
            flow.events(step, False)
        kernel(*own_in, *own_out, *own_scratch, **({"flows": every} if share_flows else {}))

        @pl.when(step == steps - 1)
        def _():
            for flow in every:
                if flow.moves():
                    flow.events(step, True)
                elif flow.ready >= steps:
                    flow.store().start()
            for flow in every:
                flow.finish()

    extra = {}
    if remote or exchange:
        extra = dict(collective_id=comm.kernels, has_side_effects=True)
        comm.kernels += 1
    results = pl.pallas_call(
        run,
        grid=(steps,),
        in_specs=list(in_specs) + [ANY] * len(flows),
        out_specs=list(out_specs) + [ANY] * len(every),
        out_shape=list(out_shape) + [jax.ShapeDtypeStruct(flow.out_shape(), f32) for flow in every],
        scratch_shapes=list(scratch_shapes) + sum(flow_scratch, []),
        compiler_params=params(**extra),
        name=name,
        **call,
    )(*operands, *[flow.array for flow in flows])
    results = list(results)
    return results[:base_out], dict(zip([flow.name for flow in every], results[base_out:]))


def unit_strips(comm, w_in_ref, w_out_ref, first, units, gathered):
    if gathered:
        first = first if isinstance(first, int) else pl.multiple_of(first, 128)
        return [(w_in_ref.at[:, pl.ds(first, units)], w_out_ref.at[pl.ds(first, units), :], 0, units)]
    unit = FF // (comm.parts * comm.streams)
    core = lax.axis_index("stream")
    strips = []
    for n in range(units // unit):
        start = (idiv(jnp.int32(first), unit) + n) * comm.streams + core
        start = pl.multiple_of(start * unit, unit)
        strips.append((w_in_ref.at[:, pl.ds(start, unit)], w_out_ref.at[pl.ds(start, unit), :], n * unit, unit))
    return strips


def gather_units(comm, w_in, w_out):
    parts, streams = comm.parts, comm.streams
    unit = FF // (parts * streams)
    if unit % 128 == 0:
        return w_in, w_out, False
    core = lax.axis_index("stream")
    a = lax.dynamic_index_in_dim(w_in.reshape(D, parts, streams, unit), core, 2, False)
    b = lax.dynamic_index_in_dim(w_out.reshape(parts, streams, unit, D), core, 1, False)
    return a.reshape(D, parts * unit), b.reshape(parts * unit, D), True


def gelu_parts(x):
    cdf = 0.5 + 0.5 * lax.erf(x * math.sqrt(0.5))
    return x * cdf, cdf + x * jnp.exp(x * x * -0.5) * (1.0 / math.sqrt(2.0 * math.pi))


TILE = 256
UNITS = 512
FRONT_TILE = 1024
CHUNK_STEPS = SLOT // FRONT_TILE + 1
OUT_COLUMNS = 256


def front_kernel(
    comm, kinds, out_kinds, gathered,
    tok_hbm, cot_hbm, valid_ref, gain_ref, win_hbm, wout_hbm,
    normed_hbm, g_hbm, act_hbm, dh_hbm,
    normed, g, win, wout, act, d_hidden, in_own, out_own,
    tok_sem, cot_sem, in_sem, out_sem, normed_sem, g_sem, act_sem, dh_sem,
):
    step = pl.program_id(0)
    rows = normed.shape[0]
    chunks = act.shape[0]
    tile = FRONT_TILE
    tiles = rows // tile
    chunk = idiv(step, CHUNK_STEPS)
    phase = irem(step, CHUNK_STEPS)
    working = chunk < chunks
    slot = irem(chunk, 2)

    def tile_rows(i):
        return pl.ds(pl.multiple_of(i * tile, tile), tile)

    def row_load(i, hbm, vmem, sem):
        return pltpu.make_async_copy(hbm.at[tile_rows(i), :], vmem.at[tile_rows(i), :], sem.at[i])

    def row_store(i, vmem, hbm, sem):
        return pltpu.make_async_copy(vmem.at[tile_rows(i), :], hbm.at[tile_rows(i), :], sem.at[i])

    def weight_loads(c):
        s = irem(jnp.int32(c), 2)
        loads = []
        for n, (a, b, at, size) in enumerate(unit_strips(comm, win_hbm, wout_hbm, c * UNITS, UNITS, gathered)):
            loads.append(pltpu.make_async_copy(a, win.at[s, :, pl.ds(at, size)], in_sem.at[s, n]))
            loads.append(pltpu.make_async_copy(b, wout.at[s, pl.ds(at, size), :], out_sem.at[s, n]))
        return loads

    def low_stores(c):
        columns = pl.ds(pl.multiple_of(c * UNITS, UNITS), UNITS)
        return (
            pltpu.make_async_copy(act.at[c], act_hbm.at[:, columns], act_sem.at[c]),
            pltpu.make_async_copy(d_hidden.at[irem(c, 2)], dh_hbm.at[:, columns], dh_sem.at[c]),
        )

    @pl.when(step == 0)
    def _():
        row_load(0, tok_hbm, normed, tok_sem).start()
        row_load(0, cot_hbm, g, cot_sem).start()
        for load in weight_loads(0):
            load.start()
        for i in range(1, tiles):
            row_load(i, tok_hbm, normed, tok_sem).start()
            row_load(i, cot_hbm, g, cot_sem).start()

    @pl.when(working & (chunk == 0) & (phase < tiles))
    def _():
        row_load(phase, tok_hbm, normed, tok_sem).wait()
        row_load(phase, cot_hbm, g, cot_sem).wait()
        here = tile_rows(phase)
        x = normed[here, :].astype(f32)
        centered = x - jnp.mean(x, axis=-1, keepdims=True)
        var = jnp.mean(centered * centered, axis=-1, keepdims=True)
        normed[here, :] = (centered * lax.rsqrt(var + EPSILON) * gain_ref[...]).astype(bf16)
        g[here, :] = (g[here, :].astype(f32) * valid_ref[here, :]).astype(bf16)
        row_store(phase, normed, normed_hbm, normed_sem).start()
        row_store(phase, g, g_hbm, g_sem).start()

    @pl.when(working & (phase == 0))
    def _():
        for load in weight_loads(chunk):
            load.wait()

    @pl.when((phase == 0) & (chunk + 1 < chunks))
    def _():
        for load in weight_loads(chunk + 1):
            load.start()

    @pl.when(working & (phase < tiles))
    def _():
        here = tile_rows(phase)
        hidden = dot(normed[here, :], win[slot])
        d_active = dot_nt(g[here, :], wout[slot])
        value, slope = gelu_parts(hidden)
        act[chunk, here, :] = value.astype(bf16)
        d_hidden[slot, here, :] = (d_active * slope).astype(bf16)

    share_rows = D // comm.parts

    @pl.when(working & (phase == tiles))
    def _():
        for copy in low_stores(chunk):
            copy.start()
        made = dot_tn(normed[...], d_hidden[slot])
        for share in range(comm.parts):
            in_own[chunk, comm.place(kinds, share, chunk)] = made[share * share_rows : (share + 1) * share_rows, :]
        low_stores(chunk)[1].wait()

    unit_rows = FF // comm.streams // comm.parts
    blocks = D // OUT_COLUMNS
    for block in range(blocks):

        @pl.when(step == chunks * CHUNK_STEPS + block)
        def _(block=block):
            right = g[:, block * OUT_COLUMNS : (block + 1) * OUT_COLUMNS]
            for c in range(chunks):
                made = dot_tn(act[c], right)
                for n in range(UNITS // unit_rows):
                    share = c * (UNITS // unit_rows) + n
                    out_own[block, comm.place(out_kinds[block], share)] = made[n * unit_rows : (n + 1) * unit_rows, :]

    @pl.when(step == pl.num_programs(0) - 1)
    def _():
        for i in range(tiles):
            row_store(i, normed, normed_hbm, normed_sem).wait()
            row_store(i, g, g_hbm, g_sem).wait()
        for c in range(chunks):
            low_stores(jnp.int32(c))[0].wait()


def front(comm, tokens, cotangent, valid, gain, weights, plan):
    w_in, w_out, gathered = weights
    rows = tokens.shape[0]
    units = FF // comm.streams
    chunks, blocks = units // UNITS, D // OUT_COLUMNS
    tiles = rows // FRONT_TILE
    parts = comm.parts
    strips = 1 if gathered else UNITS // (units // parts)
    share_rows, unit_rows = D // parts, units // parts
    kinds = [KIND[f"in{c}"] for c in range(chunks)]
    out_kinds = [KIND[f"o{b}"] for b in range(blocks)]
    steps = chunks * CHUNK_STEPS + blocks
    inner = []
    for c in range(chunks):
        start, sums = plan.get(f"in{c}", (None, ()))
        shape = (parts, share_rows, UNITS)
        flow = Flow(f"in{c}", kinds[c], 0, shape, None, start, sums, (c + 1) * CHUNK_STEPS)
        inner.append((flow, 6, c))
    for b in range(blocks):
        start, sums = plan.get(f"o{b}", (None, ()))
        shape = (parts, unit_rows, OUT_COLUMNS)
        flow = Flow(f"o{b}", out_kinds[b], 0, shape, None, start, sums, chunks * CHUNK_STEPS + b + 1)
        inner.append((flow, 7, b))
    low = jax.ShapeDtypeStruct((rows, D), bf16)
    wide = jax.ShapeDtypeStruct((rows, units), bf16)
    return with_comm(
        comm,
        partial(front_kernel, comm, kinds, out_kinds, gathered),
        steps,
        [ANY, ANY, pl.BlockSpec((rows, 1), lambda i: (0, 0)), pl.BlockSpec((1, D), lambda i: (0, 0)), ANY, ANY],
        [ANY] * 4,
        [low, low, wide, wide],
        [],
        [tokens, cotangent, valid, gain, w_in, w_out],
        [
            pltpu.VMEM((rows, D), bf16),
            pltpu.VMEM((rows, D), bf16),
            pltpu.VMEM((2, D, UNITS), bf16),
            pltpu.VMEM((2, UNITS, D), bf16),
            pltpu.VMEM((chunks, rows, UNITS), bf16),
            pltpu.VMEM((2, rows, UNITS), bf16),
            pltpu.VMEM((chunks, parts, share_rows, UNITS), f32),
            pltpu.VMEM((blocks, parts, unit_rows, OUT_COLUMNS), f32),
            pltpu.SemaphoreType.DMA((tiles,)),
            pltpu.SemaphoreType.DMA((tiles,)),
            pltpu.SemaphoreType.DMA((2, strips)),
            pltpu.SemaphoreType.DMA((2, strips)),
            pltpu.SemaphoreType.DMA((tiles,)),
            pltpu.SemaphoreType.DMA((tiles,)),
            pltpu.SemaphoreType.DMA((chunks,)),
            pltpu.SemaphoreType.DMA((chunks,)),
        ],
        inner,
        name="front",
        cost_estimate=pl.CostEstimate(
            flops=8 * rows * D * units, bytes_accessed=12 * rows * D + 8 * units * D, transcendentals=rows * units
        ),
    )


def causal_mask(transposed):
    row = lax.broadcasted_iota(jnp.int32, (BLK, BLK), 0)
    col = lax.broadcasted_iota(jnp.int32, (BLK, BLK), 1)
    return col >= row if transposed else row >= col


def head_masks():
    lane = lax.broadcasted_iota(jnp.int32, (1, PAIR), 1)
    first = lane < HEAD
    m0 = jnp.where(first, 1.0, 0.0)
    return m0.astype(bf16), (1.0 - m0).astype(bf16)


def state_mask():
    row = lax.broadcasted_iota(jnp.int32, (PAIR, 2 * PAIR), 0)
    col = lax.broadcasted_iota(jnp.int32, (PAIR, 2 * PAIR), 1)
    return (row < HEAD) == (col < PAIR)


def forward_kernel(
    comm, groups, kind,
    normed_ref, wq_ref, wk_ref, wv_ref, cos_ref, sin_ref, fw_ref, map_ref, valid_ref, right_ref,
    q_ref, k_ref, v_ref, mix_ref, den_ref, state_ref,
    state, mixed_all, sent, arrived, proj_own, send_sem, recv_sem,
):
    step = pl.program_id(0)
    blocks = sent.shape[0]

    def to_partner(i):
        return pltpu.make_async_remote_copy(
            src_ref=sent.at[i],
            dst_ref=arrived.at[i],
            send_sem=send_sem.at[i],
            recv_sem=recv_sem.at[i],
            device_id=comm.other_core(),
            device_id_type=MESH,
        )

    @pl.when(step == 0)
    def _():
        state[...] = jnp.zeros_like(state)

    @pl.when(step < blocks)
    def _():
        rows = normed_ref[...]
        queries_all, keys_all, values_all = dot(rows, wq_ref[...]), dot(rows, wk_ref[...]), dot(rows, wv_ref[...])
        cosine, sine = cos_ref[...], sin_ref[...]
        valid = valid_ref[...]
        m0, m1 = head_masks()
        causal = causal_mask(False)
        keep_state = state_mask()
        first = lax.broadcasted_iota(jnp.int32, (BLK, PAIR), 1) < HEAD
        place = pl.ds(pl.multiple_of(step * BLK, BLK), BLK)
        each = range(groups)
        lanes = [slice(group * PAIR, (group + 1) * PAIR) for group in each]
        turned = [
            jnp.concatenate(
                [
                    jnp.concatenate([queries_all[:, here] * cosine, queries_all[:, here] * sine], 1),
                    jnp.concatenate([keys_all[:, here] * cosine, keys_all[:, here] * sine], 1),
                ],
                0,
            )
            for here in lanes
        ]
        high = [t.astype(bf16) for t in turned]
        low = [(t - h.astype(f32)).astype(bf16) for t, h in zip(turned, high)]
        main = [dot(h, map_ref[...]) for h in high]
        rest = [dot(l, map_ref[:, :PAIR]) for l in low]
        phi = [
            jnp.exp(m[:, :PAIR] + m[:, PAIR:] + r) * fw_ref[:, here] for m, r, here in zip(main, rest, lanes)
        ]
        q = [f[:BLK].astype(bf16) for f in phi]
        k = [(f[BLK:] * valid).astype(bf16) for f in phi]
        v = [values_all[:, here].astype(bf16) for here in lanes]
        for n in each:
            q_ref[:, lanes[n]] = q[n]
            k_ref[:, lanes[n]] = k[n]
            v_ref[:, lanes[n]] = v[n]
        v0 = [x * m0 + m1 for x in v]
        v1 = [x * m1 + m0 for x in v]
        s0 = [jnp.where(causal, dot_nt(q[n] * m0, k[n]), 0.0).astype(bf16) for n in each]
        s1 = [jnp.where(causal, dot_nt(q[n] * m1, k[n]), 0.0).astype(bf16) for n in each]
        before = [jnp.where(keep_state, state[n], 0.0).astype(bf16) for n in each]
        far = [dot(q[n], before[n]) for n in each]
        o0 = [dot(s0[n], v0[n]) + far[n][:, :PAIR] for n in each]
        o1 = [dot(s1[n], v1[n]) + far[n][:, PAIR:] for n in each]
        for n in each:
            state_ref[n, 0] = before[n]
            state[n] += dot_tn(k[n], jnp.concatenate([v0[n], v1[n]], 1))
        for n in each:
            here = lanes[n]
            numerator = jnp.where(first, o0[n], o1[n])
            denominator = pltpu.roll(jnp.where(first, o1[n], o0[n]), HEAD, 1)
            mixed = (numerator / denominator).astype(bf16)
            mix_ref[:, here] = mixed
            mixed_all[place, here] = mixed
            sent[step, :, here] = mixed.astype(f32)
            den_ref[:, here] = denominator
        to_partner(step).start()

    share_rows = D // comm.parts
    width = groups * PAIR
    core = lax.axis_index("stream")
    for side in range(2):

        @pl.when(step == blocks + side)
        def _(side=side):
            if side == 0:
                left = mixed_all[...]
                base = core * (width // share_rows)
            else:
                for i in range(blocks):
                    to_partner(i).wait_recv()
                left = arrived[...].reshape(blocks * BLK, width).astype(bf16)
                base = (1 - core) * (width // share_rows)
            made = dot_tn(left, right_ref[...])
            for n in range(width // share_rows):
                proj_own[comm.place(kind, base + n)] = made[n * share_rows : (n + 1) * share_rows, :]
            if side == 1:
                for i in range(blocks):
                    to_partner(i).wait_send()


def forward(comm, normed, g, w_qkv, cosine, sine, fw, table, valid, flows, plan):
    rows = normed.shape[0]
    streams, parts = comm.streams, comm.parts
    groups = HEADS // streams // 2
    width = groups * PAIR
    blocks = rows // BLK

    def at(i):
        return jnp.minimum(i, blocks - 1)

    row_spec = pl.BlockSpec((BLK, width), lambda i: (at(i), 0))
    table_spec = pl.BlockSpec((BLK, PAIR), lambda i: (at(i), 0))
    low = jax.ShapeDtypeStruct((rows, width), bf16)

    def weight_spec(which):
        return pl.BlockSpec((D, width), lambda i: (0, which * streams + lax.axis_index("stream")))

    start, sums = plan.get("pr", (None, ()))
    kind = KIND["pr"]
    columns = D // streams
    inner = [(Flow("pr", kind, 0, (parts, D // parts, columns), None, start, sums, blocks + 2), 4, None)]
    return with_comm(
        comm,
        partial(forward_kernel, comm, groups, kind),
        blocks + 2,
        [
            pl.BlockSpec((BLK, D), lambda i: (at(i), 0)),
            weight_spec(0),
            weight_spec(1),
            weight_spec(2),
            table_spec,
            table_spec,
            pl.BlockSpec((1, width), lambda i: (0, lax.axis_index("stream"))),
            pl.BlockSpec((2 * PAIR, 2 * PAIR), lambda i: (0, 0)),
            pl.BlockSpec((BLK, 1), lambda i: (at(i), 0)),
            pl.BlockSpec((rows, columns), lambda i: (0, lax.axis_index("stream"))),
        ],
        [row_spec, row_spec, row_spec, row_spec, row_spec,
         pl.BlockSpec((groups, 1, PAIR, 2 * PAIR), lambda i: (0, at(i), 0, 0))],
        [low, low, low, low, jax.ShapeDtypeStruct((rows, width), f32),
         jax.ShapeDtypeStruct((groups, blocks, PAIR, 2 * PAIR), bf16)],
        flows,
        [normed, w_qkv, w_qkv, w_qkv, cosine, sine, fw, table, valid, g],
        [
            pltpu.VMEM((groups, PAIR, 2 * PAIR), f32),
            pltpu.VMEM((rows, width), bf16),
            pltpu.VMEM((blocks, BLK, width), f32),
            pltpu.VMEM((blocks, BLK, width), f32),
            pltpu.VMEM((parts, D // parts, columns), f32),
            pltpu.SemaphoreType.DMA((blocks,)),
            pltpu.SemaphoreType.DMA((blocks,)),
        ],
        inner,
        exchange=True,
        name="attention_forward",
        cost_estimate=pl.CostEstimate(
            flops=groups * blocks * 2 * 65536 * 5000,
            bytes_accessed=rows * D * 2 + 3 * D * width * 2 + rows * width * 16,
            transcendentals=2 * rows * width,
        ),
    )


GROUPS = 2
BACK_STEPS = 2


def backward_kernel(
    comm, blocks, kinds, feature_kind,
    g_ref, wp_ref, q_ref, k_ref, v_ref, mix_ref, den_ref, state_ref, cos_ref, sin_ref, back_ref, back_low_ref,
    sums_ref, fw_ref, normed_hbm,
    dq_ref, dk_ref, dv_ref,
    later, d_all, normed, fg, qkv_own, feature_own, load_sem,
):
    step = pl.program_id(0)
    per = blocks + BACK_STEPS
    call, phase = idiv(step, per), irem(step, per)
    width = GROUPS * PAIR
    load = pltpu.make_async_copy(normed_hbm, normed, load_sem)

    @pl.when(step == 0)
    def _():
        load.start()
        feature_own[...] = jnp.zeros_like(feature_own)

    @pl.when(phase == 0)
    def _():
        later[...] = jnp.zeros_like(later)
        fg[...] = jnp.zeros_like(fg)

    @pl.when(phase < blocks)
    def _():
        m0, m1 = head_masks()
        first = lax.broadcasted_iota(jnp.int32, (BLK, PAIR), 1) < HEAD
        left = lax.broadcasted_iota(jnp.int32, (PAIR, PAIR), 1) < HEAD
        own = (lax.broadcasted_iota(jnp.int32, (PAIR, PAIR), 0) < HEAD) == left
        causal, flipped = causal_mask(False), causal_mask(True)
        keep_state = state_mask()
        cosine, sine = cos_ref[...], sin_ref[...]
        d_mixed_all = dot_nt(g_ref[...], wp_ref[...])
        place = pl.ds(pl.multiple_of((blocks - 1 - phase) * BLK, BLK), BLK)
        each = range(GROUPS)
        lanes = [slice(group * PAIR, (group + 1) * PAIR) for group in each]
        q = [q_ref[:, here] for here in lanes]
        k = [k_ref[:, here] for here in lanes]
        v = [v_ref[:, here] for here in lanes]
        q0, q1 = [x * m0 for x in q], [x * m1 for x in q]
        k0, k1 = [x * m0 for x in k], [x * m1 for x in k]
        v0, v1 = [x * m0 + m1 for x in v], [x * m1 + m0 for x in v]
        st0 = [jnp.where(flipped, dot_nt(k[n], q0[n]), 0.0).astype(bf16) for n in each]
        st1 = [jnp.where(flipped, dot_nt(k[n], q1[n]), 0.0).astype(bf16) for n in each]
        numer = [d_mixed_all[:, here] / den_ref[:, here] for here in lanes]
        product = [numer[n] * mix_ref[:, lanes[n]].astype(f32) for n in each]
        p_high = [x.astype(bf16) for x in product]
        p_low = [(x - h.astype(f32)).astype(bf16) for x, h in zip(product, p_high)]
        sums = [dot(jnp.concatenate([p_high[n], p_low[n]], 1), sums_ref[...]) for n in each]
        behind = [later[n] for n in each]
        after = [jnp.where(keep_state, x, 0.0).astype(bf16) for x in behind]
        after_v = [
            jnp.where(own, jnp.where(left, x[:, :PAIR], x[:, PAIR:]), 0.0).astype(bf16) for x in behind
        ]
        d_v = [dot(k[n], after_v[n]) for n in each]
        d_k = [dot_nt(jnp.concatenate([v0[n], v1[n]], 1), after[n]) for n in each]
        d_o0 = [jnp.where(first, numer[n], -sums[n]).astype(bf16) for n in each]
        d_o1 = [jnp.where(first, -sums[n], numer[n]).astype(bf16) for n in each]
        d_o = [jnp.concatenate([d_o0[n], d_o1[n]], 1) for n in each]
        low = [x.astype(bf16) for x in numer]
        ds0 = [jnp.where(causal, dot_nt(d_o0[n], v0[n]), 0.0).astype(bf16) for n in each]
        ds1 = [jnp.where(causal, dot_nt(d_o1[n], v1[n]), 0.0).astype(bf16) for n in each]
        dst0 = [jnp.where(flipped, dot_nt(v0[n], d_o0[n]), 0.0).astype(bf16) for n in each]
        dst1 = [jnp.where(flipped, dot_nt(v1[n], d_o1[n]), 0.0).astype(bf16) for n in each]
        d_q = [dot_nt(d_o[n], state_ref[n, 0]) for n in each]
        d_v = [d_v[n] + dot(st0[n], low[n] * m0) + dot(st1[n], low[n] * m1) for n in each]
        d_q = [d_q[n] + dot(ds0[n], k0[n]) + dot(ds1[n], k1[n]) for n in each]
        d_k = [d_k[n] + dot(dst0[n], q0[n]) + dot(dst1[n], q1[n]) for n in each]
        for n in each:
            later[n] += dot_tn(q[n], d_o[n])
        e_q = [d_q[n] * q[n].astype(f32) for n in each]
        e_k = [d_k[n] * k[n].astype(f32) for n in each]
        both = [jnp.concatenate([e_q[n], e_k[n]], 0) for n in each]
        high = [x.astype(bf16) for x in both]
        lower = [(x - h.astype(f32)).astype(bf16) for x, h in zip(both, high)]
        turned = [
            dot(jnp.concatenate([high[n], lower[n]], 1), back_ref[...]) + dot(high[n], back_low_ref[...])
            for n in each
        ]
        for n in each:
            here = lanes[n]
            fg[:, here] += jnp.sum((e_q[n] + e_k[n]).reshape(BLK // 8, 8, PAIR), axis=0)
            dv = d_v[n].astype(bf16)
            dq = (turned[n][:BLK, :PAIR] * cosine + turned[n][:BLK, PAIR:] * sine).astype(bf16)
            dk = (turned[n][BLK:, :PAIR] * cosine + turned[n][BLK:, PAIR:] * sine).astype(bf16)
            dq_ref[:, here] = dq
            dk_ref[:, here] = dk
            dv_ref[:, here] = dv
            d_all[place, n * PAIR : (n + 1) * PAIR] = dq
            d_all[place, width + n * PAIR : width + (n + 1) * PAIR] = dk
            d_all[place, 2 * width + n * PAIR : 2 * width + (n + 1) * PAIR] = dv

    @pl.when(step == blocks)
    def _():
        load.wait()

    share_rows = D // comm.parts
    wide = D // BACK_STEPS
    for m in range(BACK_STEPS):

        @pl.when(phase == blocks + m)
        def _(m=m):
            made = dot_tn(normed[:, m * wide : (m + 1) * wide], d_all[...])
            for n in range(wide // share_rows):
                share = m * (wide // share_rows) + n
                qkv_own[call, comm.place(kinds, share, call)] = made[n * share_rows : (n + 1) * share_rows, :]
            if m == 0:
                total = jnp.sum(fg[...], axis=0, keepdims=True) / fw_ref[...]
                size = D // comm.parts
                core = lax.axis_index("stream")
                for n in range(width // size):
                    pair, inside = divmod(n * size, PAIR)
                    row = total[:, pair * PAIR : (pair + 1) * PAIR]
                    row = jnp.broadcast_to(row, (8, PAIR))
                    if inside:
                        row = pltpu.roll(row, PAIR - inside, 1)
                    share = core * (D // comm.streams // size) + call * (width // size) + n
                    feature_own[comm.place(feature_kind, share)] = row


def backward(comm, normed, g, w_proj, kept, cosine, sine, backs, sums, fw, flows, plan):
    q, k, v, mixed, den, states = kept
    rows = g.shape[0]
    streams, parts = comm.streams, comm.parts
    calls = HEADS // streams // 2 // GROUPS
    blocks = rows // BLK
    per = blocks + BACK_STEPS
    width = GROUPS * PAIR

    def at(i):
        return jnp.maximum(blocks - 1 - irem(i, per), 0)

    def call(i):
        return idiv(i, per)

    row_spec = pl.BlockSpec((BLK, width), lambda i: (at(i), call(i)))
    table_spec = pl.BlockSpec((BLK, PAIR), lambda i: (at(i), 0))
    low = jax.ShapeDtypeStruct((rows, calls * width), bf16)
    inner = []
    for c in range(calls):
        start, when = plan.get(f"q{c}", (None, ()))
        shape = (parts, D // parts, 3 * width)
        inner.append((Flow(f"q{c}", KIND[f"q{c}"], 0, shape, None, start, when, (c + 1) * per), 4, c))
    inner.append((Flow("feature", KIND["feature"], 0, (parts, 8, PAIR), None, None, (), calls * per), 5, None))
    return with_comm(
        comm,
        partial(backward_kernel, comm, blocks, [KIND[f"q{c}"] for c in range(calls)], KIND["feature"]),
        calls * per,
        [
            pl.BlockSpec((BLK, D), lambda i: (at(i), 0)),
            pl.BlockSpec((width, D), lambda i: (lax.axis_index("stream") * calls + call(i), 0)),
            row_spec,
            row_spec,
            row_spec,
            row_spec,
            row_spec,
            pl.BlockSpec((GROUPS, 1, PAIR, 2 * PAIR), lambda i: (call(i), at(i), 0, 0)),
            table_spec,
            table_spec,
            pl.BlockSpec((2 * PAIR, 2 * PAIR), lambda i: (0, 0)),
            pl.BlockSpec((PAIR, 2 * PAIR), lambda i: (0, 0)),
            pl.BlockSpec((2 * PAIR, PAIR), lambda i: (0, 0)),
            pl.BlockSpec((1, width), lambda i: (0, lax.axis_index("stream") * calls + call(i))),
            ANY,
        ],
        [row_spec, row_spec, row_spec],
        [low, low, low],
        flows,
        [g, w_proj, q, k, v, mixed, den, states, cosine, sine, *backs, sums, fw, normed],
        [
            pltpu.VMEM((GROUPS, PAIR, 2 * PAIR), f32),
            pltpu.VMEM((rows, 3 * width), bf16),
            pltpu.VMEM((rows, D), bf16),
            pltpu.VMEM((8, width), f32),
            pltpu.VMEM((calls, parts, D // parts, 3 * width), f32),
            pltpu.VMEM((parts, 8, PAIR), f32),
            pltpu.SemaphoreType.DMA,
        ],
        inner,
        name="attention_backward",
        cost_estimate=pl.CostEstimate(
            flops=2 * 65536 * GROUPS * calls * (blocks * 6500 + 16384),
            bytes_accessed=2 * (2 * rows * D + width * D + rows * width * 24),
            transcendentals=0,
        ),
    )


def tail_kernel(
    comm, tiles, gathered,
    act_ref, dh_ref, mix_ref, dq_ref, dk_ref, dv_ref, tok_ref, cot_ref, valid_ref, gain_ref,
    wproj_ref, wqkv_hbm, win_hbm, wout_hbm,
    out_ref, grad_ref,
    win, wout, wqkv, mine, arrived, in_sem, out_sem, qkv_sem, send_sem, recv_sem,
):
    step = pl.program_id(0)
    units = win.shape[1]
    strips = unit_strips(comm, win_hbm, wout_hbm, 0, units, gathered)
    loads = []
    for n, (a, b, at, size) in enumerate(strips):
        loads.append(pltpu.make_async_copy(a, win.at[:, pl.ds(at, size)], in_sem.at[n]))
        loads.append(pltpu.make_async_copy(b, wout.at[pl.ds(at, size), :], out_sem.at[n]))

    core = lax.axis_index("stream")
    width = mix_ref.shape[1]
    for n in range(3):
        start = pl.multiple_of((n * comm.streams + core) * width, width)
        loads.append(
            pltpu.make_async_copy(wqkv_hbm.at[:, pl.ds(start, width)], wqkv.at[:, pl.ds(n * width, width)], qkv_sem.at[n])
        )

    def send(i, part):
        return pltpu.make_async_remote_copy(
            src_ref=mine.at[irem(i, 3), part],
            dst_ref=arrived.at[i, part],
            send_sem=send_sem.at[i, part],
            recv_sem=recv_sem.at[i, part],
            device_id=comm.other_core(),
            device_id_type=MESH,
        )

    @pl.when(step == 0)
    def _():
        for load in loads:
            load.start()
        for load in loads:
            load.wait()

    @pl.when((step >= 3) & (step < tiles))
    def _():
        send(step - 3, 0).wait_send()
        send(step - 3, 1).wait_send()

    @pl.when(step >= 2)
    def _():
        send(step - 2, 0).wait_recv()
        send(step - 2, 1).wait_recv()

    def products():
        slot = irem(step, 3)
        mine[slot, 0] = dot(act_ref[...], wout[...])
        mine[slot, 0] += dot(mix_ref[...], wproj_ref[...])
        send(step, 0).start()
        d_qkv = jnp.concatenate([dq_ref[...], dk_ref[...], dv_ref[...]], 1)
        mine[slot, 1] = dot_nt(dh_ref[...], win[...])
        mine[slot, 1] += dot_nt(d_qkv, wqkv[...])
        send(step, 1).start()

    def finish_rows():
        slot = irem(step + 1, 3)
        x = tok_ref[...].astype(f32)
        centered = x - jnp.mean(x, axis=-1, keepdims=True)
        var = jnp.mean(centered * centered, axis=-1, keepdims=True)
        inv_std = lax.rsqrt(var + EPSILON)
        unit = centered * inv_std
        out_ref[...] = (x + (mine[slot, 0] + arrived[step - 2, 0]) * valid_ref[...]).astype(bf16)
        scaled = (mine[slot, 1] + arrived[step - 2, 1]) * gain_ref[...]
        mean = jnp.mean(scaled, axis=-1, keepdims=True)
        cross = jnp.mean(scaled * unit, axis=-1, keepdims=True)
        grad_ref[...] = (cot_ref[...].astype(f32) + inv_std * (scaled - mean - unit * cross)).astype(bf16)

    @pl.when(step < 2)
    def _():
        products()

    @pl.when((step >= 2) & (step < tiles))
    def _():
        finish_rows()
        products()

    @pl.when(step >= tiles)
    def _():
        finish_rows()

    @pl.when(step == tiles + 1)
    def _():
        for i in (tiles - 3, tiles - 2, tiles - 1):
            send(i, 0).wait_send()
            send(i, 1).wait_send()


def tail(comm, active, d_hidden, mixed, d_qkv, tokens, cotangent, valid, gain, weights, w_proj, w_qkv, flows):
    w_in, w_out, gathered = weights
    rows, units = active.shape
    width = mixed.shape[1]
    tiles = rows // TILE
    strips = 1 if gathered else comm.parts

    def now(i):
        return (jnp.minimum(i, tiles - 1), 0)

    def before(i):
        return (jnp.maximum(i - 2, 0), 0)

    shape = jax.ShapeDtypeStruct((rows, D), bf16)
    return with_comm(
        comm,
        partial(tail_kernel, comm, tiles, gathered),
        tiles + 2,
        [
            pl.BlockSpec((TILE, units), now),
            pl.BlockSpec((TILE, units), now),
            pl.BlockSpec((TILE, width), now),
            pl.BlockSpec((TILE, width), now),
            pl.BlockSpec((TILE, width), now),
            pl.BlockSpec((TILE, width), now),
            pl.BlockSpec((TILE, D), before),
            pl.BlockSpec((TILE, D), before),
            pl.BlockSpec((TILE, 1), before),
            pl.BlockSpec((1, D), lambda i: (0, 0)),
            pl.BlockSpec((width, D), lambda i: (lax.axis_index("stream"), 0), pipeline_mode=pl.Buffered(1)),
            ANY,
            ANY,
            ANY,
        ],
        [pl.BlockSpec((TILE, D), before), pl.BlockSpec((TILE, D), before)],
        [shape, shape],
        flows,
        [active, d_hidden, mixed, *d_qkv, tokens, cotangent, valid, gain, w_proj, w_qkv, w_in, w_out],
        [
            pltpu.VMEM((D, units), bf16),
            pltpu.VMEM((units, D), bf16),
            pltpu.VMEM((D, 3 * width), bf16),
            pltpu.VMEM((3, 2, TILE, D), f32),
            pltpu.VMEM((tiles, 2, TILE, D), f32),
            pltpu.SemaphoreType.DMA((strips,)),
            pltpu.SemaphoreType.DMA((strips,)),
            pltpu.SemaphoreType.DMA((3,)),
            pltpu.SemaphoreType.DMA((tiles, 2)),
            pltpu.SemaphoreType.DMA((tiles, 2)),
        ],
        exchange=True,
        name="tail",
        cost_estimate=pl.CostEstimate(
            flops=2 * rows * D * (2 * units + 4 * width),
            bytes_accessed=2 * (rows + D) * (2 * units + 4 * width) + 8 * rows * D,
            transcendentals=0,
        ),
    )


def rest_kernel(comm, names, widths, ready, length, *refs, flows=()):
    held = dict(zip(ready, refs))
    refs = refs[len(ready) :]
    other_ref, feature_ref, landing, feature_landing, send_sem, recv_sem = refs
    moving = {flow.name: flow for flow in flows}
    step = pl.program_id(0)
    core = lax.axis_index("stream")
    half = landing.shape[0]

    def copy(n, name):
        source = held[name] if name in held else moving[name].own
        if name == "feature":
            source, target = source.at[0], feature_landing
        else:
            source = source.at[0, pl.ds(pl.multiple_of((1 - core) * half, half), half), :]
            target = landing.at[:, pl.ds(sum(widths[:n]), widths[n])]
        return pltpu.make_async_remote_copy(
            src_ref=source,
            dst_ref=target,
            send_sem=send_sem.at[n],
            recv_sem=recv_sem.at[n],
            device_id=comm.other_core(),
            device_id_type=MESH,
        )

    @pl.when(step == 0)
    def _():
        for n, name in enumerate(names):
            if name in held:
                copy(n, name).start()

    @pl.when(step == length - 1)
    def _():
        for n, name in enumerate(names):
            if name not in held:
                copy(n, name).start()
        for n, name in enumerate(names):
            copy(n, name).wait()
        other_ref[...] = landing[...]
        feature_ref[...] = feature_landing[...]


def rest(comm, done, names, plan, flows):
    half = D // comm.parts // comm.streams
    ready = [name for name in names if name not in plan]
    widths = [done[name][1].shape[2] if name != "feature" else 0 for name in names]
    length = 2 + max([0] + [len(sums) for _, sums in plan.values()])
    shape = (half, sum(widths))
    return with_comm(
        comm,
        partial(rest_kernel, comm, names, widths, ready, length),
        length,
        [ANY] * len(ready),
        [pl.BlockSpec(shape, lambda i: (0, 0)), pl.BlockSpec((8, PAIR), lambda i: (0, 0))],
        [jax.ShapeDtypeStruct(shape, f32), jax.ShapeDtypeStruct((8, PAIR), f32)],
        flows,
        [done[name][1] for name in ready],
        [
            pltpu.VMEM(shape, f32),
            pltpu.VMEM((8, PAIR), f32),
            pltpu.SemaphoreType.DMA((len(names),)),
            pltpu.SemaphoreType.DMA((len(names),)),
        ],
        exchange=True,
        share_flows=True,
        name="rest",
    )


def assemble_kernel(comm, in_count, call_count, out_count, *refs):
    refs = list(refs)

    def take(count):
        taken = refs[:count]
        del refs[:count]
        return taken

    ins, calls, (proj_ref,), outs = take(in_count), take(call_count), take(1), take(out_count)
    other_ref, feature_ref, feature_other, win_ref, wqkv_ref, gain_ref, output_hbm, input_hbm = take(8)
    in_grad, qkv_grad, proj_grad, out_grad, gain_grad, feature_grad, output_out, input_out, stage, in_sem, out_sem = refs
    core = lax.axis_index("stream")
    half = in_grad.shape[0]
    chunks = stage.shape[1]
    rows = stage.shape[2]
    loads, stores = [], []
    for n, (source, target) in enumerate(((output_hbm, output_out), (input_hbm, input_out))):
        for c in range(chunks):
            part = pl.ds(c * rows, rows)
            loads.append(pltpu.make_async_copy(source.at[part, :], stage.at[n, c], in_sem.at[n, c]))
            stores.append(pltpu.make_async_copy(stage.at[n, c], target.at[part, :], out_sem.at[n, c]))
    for load in loads:
        load.start()
    for n, ref in enumerate(outs):
        out_grad[:, n * OUT_COLUMNS : (n + 1) * OUT_COLUMNS] = ref[0]
    here = pl.ds(pl.multiple_of(core * half, half), half)
    unit = FF // comm.parts // comm.streams
    units = FF // comm.streams
    wide = GROUPS * PAIR
    columns = D // comm.streams
    for load, store in zip(loads, stores):
        load.wait()
        store.start()
    for side in range(2):

        @pl.when(core == side)
        def _(side=side):
            for n in range(comm.parts):
                mine = ins[n * unit // UNITS][0, here, n * unit % UNITS : n * unit % UNITS + unit]
                other = other_ref[:, n * unit : (n + 1) * unit]
                pair = (mine, other) if side == 0 else (other, mine)
                for k in range(2):
                    at = (2 * n + k) * unit
                    in_grad[:, at : at + unit] = pair[k]
            for which in range(3):
                for n in range(call_count):
                    mine = calls[n][0, here, which * wide : (which + 1) * wide]
                    at = units + (3 * n + which) * wide
                    other = other_ref[:, at : at + wide]
                    pair = (mine, other) if side == 0 else (other, mine)
                    for k in range(2):
                        at = which * D + k * columns + n * wide
                        qkv_grad[:, at : at + wide] = pair[k]
            at = units + 3 * columns
            pair = (proj_ref[0, here, :], other_ref[:, at : at + columns])
            for k in range(2):
                proj_grad[:, k * columns : (k + 1) * columns] = pair[k if side == 0 else 1 - k]
            share = feature_grad.shape[1]
            total = feature_ref[0] + feature_other[...]
            feature_grad[...] = total[0:1, side * share : (side + 1) * share]

    total = jnp.sum(win_ref[...].astype(f32) * in_grad[...], axis=1, keepdims=True)
    total += jnp.sum(wqkv_ref[...].astype(f32) * qkv_grad[...], axis=1, keepdims=True)
    gain_grad[...] = total / gain_ref[...]
    for store in stores:
        store.wait()


def assemble(comm, final, other, feature_other, w_in, w_qkv, norm_gain, output, input_grad):
    parts, streams = comm.parts, comm.streams
    half, share = D // parts // streams, D // (parts * streams)
    in_names = [f"in{c}" for c in range(FF // streams // UNITS)]
    call_names = [f"q{c}" for c in range(HEADS // streams // 2 // GROUPS)]
    out_names = [f"o{b}" for b in range(D // OUT_COLUMNS)]

    def whole(array):
        return pl.BlockSpec(array.shape, lambda i, n=array.ndim: (0,) * n)

    def rows_of(columns):
        return pl.BlockSpec((half, columns), lambda i: (lax.axis_index("dp") * streams + lax.axis_index("stream"), 0))

    pieces = [final[n] for n in in_names + call_names + ["pr"] + out_names] + [other, final["feature"], feature_other]
    shapes = [(half, FF), (half, 3 * D), (half, D), (FF // parts // streams, D), (half, 1), (1, share)]
    low = jax.ShapeDtypeStruct(output.shape, bf16)
    return pl.pallas_call(
        partial(assemble_kernel, comm, len(in_names), len(call_names), len(out_names)),
        grid=(1,),
        in_specs=[whole(piece) for piece in pieces] + [rows_of(FF), rows_of(3 * D), rows_of(1), ANY, ANY],
        out_specs=[pl.BlockSpec(shape, lambda i: (0, 0)) for shape in shapes] + [ANY, ANY],
        out_shape=[jax.ShapeDtypeStruct(shape, f32) for shape in shapes] + [low, low],
        scratch_shapes=[
            pltpu.VMEM((2, 4, output.shape[0] // 4, D), bf16),
            pltpu.SemaphoreType.DMA((2, 4)),
            pltpu.SemaphoreType.DMA((2, 4)),
        ],
        compiler_params=params(),
        name="assemble",
    )(*pieces, w_in, w_qkv, norm_gain.reshape(D, 1), output, input_grad)


KIND = {
    "in0": "xz",
    "in1": "yz",
    "in2": "zx",
    "in3": "xy",
    "o0": "xx",
    "o1": "zx",
    "o2": "zz",
    "o3": "xx",
    "pr": "zx",
    "q0": "xx",
    "q1": "xx",
    "feature": "xy",
}
FRONT = {
    "in0": (3, (10, -1)),
    "in1": (6, (-1,)),
    "in2": (9, (-1,)),
    "o0": (13, (-1,)),
}
FORWARD = {
    "in2": (0, (6,)),
    "o1": (0, (8,)),
    "o3": (0, (-1,)),
    "o2": (4, (-1,)),
    "o0": (5, (-1,)),
    "in0": (7, (-1,)),
    "in3": (8, (-1,)),
}
BACKWARD = {
    "o1": (0, (7, 14, 17)),
    "pr": (0, (14, -1)),
    "o3": (1, (9, 16, 19)),
    "in1": (1, (9, 13)),
    "o0": (5, (11, 15)),
    "in0": (8, (13,)),
    "q0": (10, (-1,)),
    "in2": (15, (19, -1)),
}
TAIL = {
    "feature": (0, (5, 9)),
    "q1": (0, (8, -1)),
    "in1": (0, (2,)),
    "q0": (0, (6, 9, -1)),
    "in3": (0, (5, 7, 9)),
    "pr": (1, (5, 7)),
    "o2": (2, (7,)),
}


def solution(mesh):
    comm = Comm(mesh.shape["dp"], mesh.shape["stream"])
    parts, streams = comm.parts, comm.streams
    cosine_np, sine_np, map_np, back_high_np, back_low_np = attention_tables()
    sums_np = np.zeros((2 * PAIR, PAIR), np.float32)
    for base in (0, PAIR):
        sums_np[base : base + HEAD, HEAD] = 1.0
        sums_np[base + HEAD : base + PAIR, 0] = 1.0

    def body(tokens, norm_gain, w_qkv, w_proj, w_in, w_out, feature_weight, lengths, cotangent):
        comm.kernels = 0
        rows = tokens.shape[0]
        gain = norm_gain.reshape(1, D)
        fw = feature_weight.reshape(1, D)
        cosine, sine = jnp.asarray(cosine_np), jnp.asarray(sine_np)
        valid = (jnp.arange(rows) < lengths[0]).astype(f32).reshape(rows, 1)
        weights = gather_units(comm, w_in, w_out)
        units = FF // streams
        done = {}

        def flows_of(plan):
            flows = []
            for name, (start, sums) in plan.items():
                if name in done and done[name][0] < comm.steps:
                    taken, array = done[name]
                    sums = sums[: comm.steps - taken]
                    flows.append(Flow(name, KIND[name], taken, array.shape, array, start, sums))
            return flows

        def landed(shares, plan):
            for name, array in shares.items():
                taken = done[name][0] if name in done else 0
                done[name] = (taken + (len(plan[name][1][: comm.steps - taken]) if name in plan else 0), array)

        (normed, g, act, d_hidden), shares = front(comm, tokens, cotangent, valid, gain, weights, FRONT)
        landed(shares, FRONT)
        kept, shares = forward(
            comm, normed, g, w_qkv, cosine, sine, fw, jnp.asarray(map_np), valid, flows_of(FORWARD), FORWARD
        )
        landed(shares, FORWARD)
        backs = (jnp.asarray(back_high_np), jnp.asarray(back_low_np))
        d_qkv, shares = backward(
            comm, normed, g, w_proj, kept, cosine, sine, backs, jnp.asarray(sums_np, bf16), fw,
            flows_of(BACKWARD), BACKWARD,
        )
        landed(shares, BACKWARD)
        (output, input_grad), shares = tail(
            comm, act, d_hidden, kept[3], d_qkv, tokens, cotangent, valid, gain, weights, w_proj, w_qkv,
            flows_of(TAIL),
        )
        landed(shares, TAIL)
        left = {}
        for name, (taken, _) in done.items():
            if taken < comm.steps:
                left[name] = (0, tuple(range(1, comm.steps - taken + 1)))
        names = [f"in{c}" for c in range(units // UNITS)]
        names += [f"q{c}" for c in range(HEADS // streams // 2 // GROUPS)] + ["pr", "feature"]
        (other, feature_other), shares = rest(comm, done, names, left, flows_of(left))
        landed(shares, left)
        final = {name: array for name, (_, array) in done.items()}
        in_grad, qkv_grad, proj_grad, out_grad, gain_grad, feature_grad, output, input_grad = assemble(
            comm, final, other, feature_other, w_in, w_qkv, norm_gain, output, input_grad
        )
        return (
            output, input_grad, gain_grad.reshape(-1), qkv_grad, proj_grad, in_grad, out_grad, feature_grad.reshape(-1)
        )

    both = P(("dp", "stream"), None)
    return jax.shard_map(
        body,
        mesh=mesh,
        in_specs=(P("dp", None), P(), P(), P(), P(), P(), P(), P("dp"), P("dp", None)),
        out_specs=(
            P("dp", None), P("dp", None), P(("dp", "stream")), both, both, both, both, P(("dp", "stream")),
        ),
        check_vma=False,
    )
```
